128 devices in a mesh: cons: 4 (over y_lo, core), prod: 32 (over y_hi, z, x).
Axes of the slice: x: 4, y: 4 (y_hi: 2, y_lo: 2; y = y_hi * 2 + y_lo), z: 4, core: 2. Of those that a mesh axis runs over, the one named last changes fastest.
Arguments:
- tastes: bfloat16 [16384, 128], P('cons'), may hold values from -128 to 128
- price_coef: float32 [16384], P('cons'), may hold values from 0.5 to 5
- characteristics: bfloat16 [65536, 128], P('prod'), may hold values from -6 to 6
- mean_utility: float32 [65536], P('prod'), may hold values from -4 to 4
- panel_cols: int32 [256], replicated, may hold values from 0 to 65535
- firm_map: int32 [65536], P('prod'), may hold values from 0 to 65535, as said below
- inverses: float32 [512, 128, 128], P('prod'), may hold values from -0.5 to 0.5
Outputs:
- shares: float32 [65536], P('prod')
- markup: float32 [65536], P('prod')
- response: float32 [65536, 256], P('prod')
The draws below stay inside these ranges and needn't reach their ends.
Inputs may be any that keep to these rules, and one draw needn't show every extreme that they name: `firm_map`: a permutation of the products; the rows of firm order held by each index of prod name exactly 64 products held by each index of prod.
All inputs are finite; a program needn't handle non-finite values.
Results may differ from the reference program's by a relative error of at most 0.002.
The reference program's roundings to bfloat16 on the way count: a program that leaves them out, or rounds other values in their place, can miss the bound.
Values may be sent and summed in bfloat16 or wider, within the bound.
No kernel may reach another device: no remote copies, remote signals or barrier semaphores. Data moves between devices by JAX's collectives and lax.ppermute only.
A program may use at most 64 MiB of HBM per device.

```python
import math
import jax
import jax.numpy as jnp
from jax import lax

K = 128
COLS = 256
B = 128
JD = 2048
J = 65536
I = 16384
F = 512


def drawn_draws(key):
    key_chars, key_tastes = jax.random.split(jax.random.fold_in(key, 7), 2)
    chars_all = jnp.clip(jax.random.normal(key_chars, (J, K), jnp.float32), -6.0, 6.0)
    tastes_all = jnp.clip(jax.random.normal(key_tastes, (I, K), jnp.float32), -6.0, 6.0) * (3.0 / math.sqrt(K))
    return (chars_all, tastes_all)


def draw_characteristics(key, part):
    return drawn_draws(key)[0].astype(jnp.bfloat16)


def draw_tastes(key, part):
    return drawn_draws(key)[1].astype(jnp.bfloat16)


def shuffle_one(subkey):
    return jax.random.permutation(subkey, JD).astype(jnp.int32)


def draw_firm_map(key, part):
    sources = J // JD
    per_pair = JD // sources
    key_first, key_second = jax.random.split(jax.random.fold_in(key, 11))
    shuffled = jax.vmap(shuffle_one)(jax.random.split(key_first, sources))
    owned = shuffled + (jnp.arange(sources, dtype=jnp.int32) * JD)[:, None]
    routed = owned.reshape(sources, sources, per_pair).transpose(1, 0, 2).reshape(sources, JD)
    mixing = jax.vmap(shuffle_one)(jax.random.split(key_second, sources))
    mixed = jnp.take_along_axis(routed, mixing, axis=1)
    return mixed.reshape(J).astype(jnp.int32)


def with_ends(result, rng, smallest, top_value):
    longest = result.shape.index(max(result.shape))
    spots = []
    for shift in (0, 1):
        where = [jax.random.randint(jax.random.fold_in(rng, axis), (), 0, length) for axis, length in enumerate(result.shape)]
        where[longest] = (where[longest] + shift) % result.shape[longest]
        spots.append(tuple(where))
    return result.at[spots[0]].set(smallest).at[spots[1]].set(top_value)


def block_scale(own_key, extent, shards, least, largest):
    gain = 1.0
    for position, shards_of in shards:
        steps = jax.random.uniform(jax.random.fold_in(jax.random.fold_in(own_key, 6), position), (shards_of,), jnp.float32, least / len(shards), largest / len(shards))
        gain = gain * jnp.repeat(jnp.exp(steps), extent[position] // shards_of).reshape((-1,) + (1,) * (len(extent) - 1 - position))
    return gain


def gaussian(stream_key, shape, scale, most, cuts=(), held_as=jnp.bfloat16):
    drawn = scale * jax.random.normal(stream_key, shape, jnp.float32)
    if cuts:
        drawn = drawn * block_scale(stream_key, shape, cuts, -0.22, 0.18)
    return jnp.clip(drawn, -most, most).astype(held_as)


def setup_inputs(seed: int = 0) -> dict:
    streams_of = jax.random.split(jax.random.key(seed), 8)
    return {
        "tastes": draw_tastes(jax.random.fold_in(streams_of[7], 71), 0),
        "price_coef": jnp.clip(jnp.exp(math.log(5.0) - 2.3025851 * jax.random.uniform(streams_of[1], (I,), jnp.float32) ** block_scale(streams_of[1], (I,), ((0, 4),), -0.2, 0.2)), 0.5, 5.0),
        "characteristics": draw_characteristics(jax.random.fold_in(streams_of[7], 71), 0),
        "mean_utility": gaussian(streams_of[3], (J,), 1.0, 4.0, ((0, 32),), jnp.float32),
        "panel_cols": with_ends(jax.random.randint(streams_of[4], (COLS,), 0, J), jax.random.fold_in(streams_of[4], 1), 0, J - 1).astype(jnp.int32),
        "firm_map": draw_firm_map(jax.random.fold_in(streams_of[7], 71), 0),
        "inverses": gaussian(streams_of[6], (F, B, B), B ** -0.5, 0.5, ((0, 32),), jnp.float32),
    }


def reference(tastes, price_coef, characteristics, mean_utility, panel_cols, firm_map, inverses):
    count_products = characteristics.shape[0]
    count_consumers = tastes.shape[0]
    block_rows = min(512, count_consumers)
    block_count = count_consumers // block_rows
    col_chars = characteristics[panel_cols]
    col_means = mean_utility[panel_cols]
    taste_blocks = tastes.reshape(block_count, block_rows, tastes.shape[1])
    coef_blocks = price_coef.reshape(block_count, block_rows)

    def consume(state_now, inputs):
        panel_sum, share_sum, diag_sum = state_now
        taste_block, coef_block = inputs
        utility = jnp.dot(taste_block, characteristics.T, preferred_element_type=jnp.float32) + mean_utility[None, :]
        highest = jnp.maximum(jnp.max(utility, axis=1), 0.0)
        exponent = jnp.exp(utility - highest[:, None])
        denominator = jnp.exp(-highest) + jnp.sum(exponent, axis=1)
        scaled = count_products * exponent / denominator[:, None]
        share_sum = share_sum + jnp.sum(scaled, axis=0)
        diag_sum = diag_sum + jnp.dot(coef_block, scaled, precision=lax.Precision.HIGHEST)
        col_util = jnp.dot(taste_block, col_chars.T, preferred_element_type=jnp.float32) + col_means[None, :]
        col_scaled = count_products * jnp.exp(col_util - highest[:, None]) / denominator[:, None]
        weighted = (coef_block[:, None] * col_scaled).astype(jnp.bfloat16)
        panel_sum = panel_sum + lax.dot_general(scaled.astype(jnp.bfloat16), weighted, (((0,), (0,)), ((), ())), preferred_element_type=jnp.float32)
        return (panel_sum, share_sum, diag_sum), None

    start_state = (jnp.zeros((count_products, panel_cols.shape[0]), jnp.float32), jnp.zeros((count_products,), jnp.float32), jnp.zeros((count_products,), jnp.float32))
    (panel_sum, share_sum, diag_sum), _ = lax.scan(consume, start_state, (taste_blocks, coef_blocks))
    cross = panel_sum / count_consumers
    shares = share_sum / count_consumers
    diagonal = diag_sum / count_consumers
    product_ids = jnp.arange(count_products, dtype=jnp.int32)
    marks = (product_ids[:, None] == panel_cols[None, :]).astype(jnp.float32)
    jacobian = cross - diagonal[:, None] * marks
    block_size = inverses.shape[1]
    firm_count = inverses.shape[0]
    ordered = jacobian[firm_map].reshape(firm_count, block_size, panel_cols.shape[0])
    response = jnp.einsum("fab,fbc->fac", inverses, ordered, precision=lax.Precision.HIGHEST).reshape(count_products, panel_cols.shape[0])
    ordered_shares = shares[firm_map].reshape(firm_count, block_size)
    markup = jnp.einsum("fab,fb->fa", inverses, ordered_shares, precision=lax.Precision.HIGHEST).reshape(count_products)
    return shares, markup, response
```

```python
import jax
import jax.numpy as jnp
from jax import lax
from jax.experimental import pallas as pl
from jax.experimental.pallas import tpu as pltpu
from jax.sharding import PartitionSpec as P

NT = (((1,), (1,)), ((), ()))
VMEM_BYTES = 56 * 1024 * 1024


def dot_nt(left, right):
    return lax.dot_general(left, right, NT, preferred_element_type=jnp.float32)


def split3(values):
    high = lax.reduce_precision(values, 8, 7)
    middle = lax.reduce_precision(values - high, 8, 7)
    low = lax.reduce_precision(values - high - middle, 8, 7)
    high, middle, low = (piece.astype(jnp.bfloat16) for piece in (high, middle, low))
    return high, middle, low


def stats_kernel(block, chunk, chars_ref, tastes_ref, stat_ref, expo_ref, util_ref):
    rows = chars_ref.shape[0]
    tastes = tastes_ref[...]
    peak = jnp.full((8, block), -jnp.inf, jnp.float32)
    for start in range(0, rows, chunk):
        util = dot_nt(chars_ref[start : start + chunk, :], tastes)
        util_ref[start : start + chunk, :] = util
        peak = jnp.maximum(peak, jnp.max(util.reshape(chunk // 8, 8, block), axis=0))
    peak = jnp.max(peak, axis=0, keepdims=True)
    total = jnp.zeros((8, block), jnp.float32)
    for start in range(0, rows, chunk):
        expo = jnp.exp(util_ref[start : start + chunk, :] - peak)
        total = total + jnp.sum(expo.reshape(chunk // 8, 8, block), axis=0)
        expo_ref[start : start + chunk, :] = expo.astype(jnp.bfloat16)
    stat_ref[0:1, :] = peak
    stat_ref[1:2, :] = jnp.sum(total, axis=0, keepdims=True)


def stats(chars, tastes):
    rows, depth = chars.shape
    consumers = tastes.shape[0]
    block, chunk = 256, 256

    def kernel(*refs):
        stats_kernel(block, chunk, *refs)

    return pl.pallas_call(
        kernel,
        grid=(consumers // block,),
        in_specs=[
            pl.BlockSpec((rows, depth), lambda i: (0, 0)),
            pl.BlockSpec((block, depth), lambda i: (i, 0)),
        ],
        out_specs=[
            pl.BlockSpec((2, block), lambda i: (0, i)),
            pl.BlockSpec((rows, block), lambda i: (0, i)),
        ],
        out_shape=[
            jax.ShapeDtypeStruct((2, consumers), jnp.float32),
            jax.ShapeDtypeStruct((rows, consumers), jnp.bfloat16),
        ],
        scratch_shapes=[pltpu.VMEM((rows, block), jnp.float32)],
        compiler_params=pltpu.CompilerParams(vmem_limit_bytes=VMEM_BYTES),
        cost_estimate=pl.CostEstimate(
            flops=2 * rows * consumers * depth, bytes_accessed=rows * consumers * 2, transcendentals=rows * consumers
        ),
        name="stats",
    )(chars, tastes)


def pick_rows(ids_t, chars):
    per_pair, holders = ids_t.shape
    rows, depth = chars.shape
    group = max(1, 256 // per_pair)

    def kernel(ids_ref, chars_ref, out_ref):
        lanes = lax.broadcasted_iota(jnp.int32, (per_pair, rows), 1)
        table = chars_ref[...]
        for start in range(0, holders, group):
            marks = [
                jnp.where(ids_ref[:, q : q + 1] == lanes, 1.0, 0.0).astype(jnp.bfloat16)
                for q in range(start, min(start + group, holders))
            ]
            hot = jnp.concatenate(marks, axis=0)
            picked = jnp.dot(hot, table, preferred_element_type=jnp.float32)
            out_ref[start * per_pair : start * per_pair + hot.shape[0], :] = picked.astype(jnp.bfloat16)

    return pl.pallas_call(
        kernel,
        out_shape=jax.ShapeDtypeStruct((per_pair * holders, depth), jnp.bfloat16),
        compiler_params=pltpu.CompilerParams(vmem_limit_bytes=VMEM_BYTES),
        cost_estimate=pl.CostEstimate(flops=2 * rows * rows * depth, bytes_accessed=rows * depth * 4, transcendentals=0),
        name="pick_rows",
    )(ids_t, chars)


def place_rows(order, received):
    rows, depth = received.shape
    chunk = 256

    def kernel(order_ref, received_ref, out_ref):
        order_row = order_ref[...]
        table = received_ref[...]
        for start in range(0, rows, chunk):
            ids = start + lax.broadcasted_iota(jnp.int32, (chunk, rows), 0)
            hot = jnp.where(ids == order_row, 1.0, 0.0).astype(jnp.bfloat16)
            placed = jnp.dot(hot, table, preferred_element_type=jnp.float32)
            out_ref[start : start + chunk, :] = placed.astype(jnp.bfloat16)

    return pl.pallas_call(
        kernel,
        out_shape=jax.ShapeDtypeStruct((rows, depth), jnp.bfloat16),
        compiler_params=pltpu.CompilerParams(vmem_limit_bytes=VMEM_BYTES),
        cost_estimate=pl.CostEstimate(flops=2 * rows * rows * depth, bytes_accessed=rows * depth * 4, transcendentals=0),
        name="place_rows",
    )(order, received)


def lane_groups(values):
    total = values[:, 0:128]
    for start in range(128, values.shape[1], 128):
        total = total + values[:, start : start + 128]
    return total


def weights(tastes, row_values, col_chars):
    consumers, depth = tastes.shape
    cols = col_chars.shape[0]
    block = 1024

    def kernel(tastes_ref, rows_ref, cols_ref, weight_ref, diag_ref):
        @pl.when(pl.program_id(0) == 0)
        def _():
            diag_ref[...] = jnp.zeros_like(diag_ref)

        expo = jnp.exp(dot_nt(cols_ref[...], tastes_ref[...]) - rows_ref[0:1, :])
        weighted = rows_ref[2:3, :] * (expo * rows_ref[1:2, :])
        diag_ref[...] += lane_groups(weighted)
        weight_ref[...] = weighted.astype(jnp.bfloat16)

    return pl.pallas_call(
        kernel,
        grid=(consumers // block,),
        in_specs=[
            pl.BlockSpec((block, depth), lambda i: (i, 0)),
            pl.BlockSpec((3, block), lambda i: (0, i)),
            pl.BlockSpec((cols, depth), lambda i: (0, 0)),
        ],
        out_specs=[
            pl.BlockSpec((cols, block), lambda i: (0, i)),
            pl.BlockSpec((cols, 128), lambda i: (0, 0)),
        ],
        out_shape=[
            jax.ShapeDtypeStruct((cols, consumers), jnp.bfloat16),
            jax.ShapeDtypeStruct((cols, 128), jnp.float32),
        ],
        compiler_params=pltpu.CompilerParams(vmem_limit_bytes=VMEM_BYTES),
        cost_estimate=pl.CostEstimate(
            flops=2 * cols * consumers * depth, bytes_accessed=cols * consumers * 2, transcendentals=cols * consumers
        ),
        name="weights",
    )(tastes, row_values, col_chars)


def panel(chars, tastes, row_values, weighted):
    rows, depth = chars.shape
    consumers = tastes.shape[0]
    cols = weighted.shape[0]
    block, chunk = 1024, 256

    def kernel(chars_ref, tastes_ref, rows_ref, weight_ref, panel_ref, share_ref):
        @pl.when(pl.program_id(0) == 0)
        def _():
            panel_ref[...] = jnp.zeros_like(panel_ref)
            share_ref[...] = jnp.zeros_like(share_ref)

        people, weight = tastes_ref[...], weight_ref[...]
        peak, ratio = rows_ref[0:1, :], rows_ref[1:2, :]
        for start in range(0, rows, chunk):
            scaled = jnp.exp(dot_nt(chars_ref[start : start + chunk, :], people) - peak) * ratio
            share_ref[start : start + chunk, :] += lane_groups(scaled)
            panel_ref[start : start + chunk, :] += dot_nt(scaled.astype(jnp.bfloat16), weight)

    return pl.pallas_call(
        kernel,
        grid=(consumers // block,),
        in_specs=[
            pl.BlockSpec((rows, depth), lambda i: (0, 0)),
            pl.BlockSpec((block, depth), lambda i: (i, 0)),
            pl.BlockSpec((3, block), lambda i: (0, i)),
            pl.BlockSpec((cols, block), lambda i: (0, i)),
        ],
        out_specs=[
            pl.BlockSpec((rows, cols), lambda i: (0, 0)),
            pl.BlockSpec((rows, 128), lambda i: (0, 0)),
        ],
        out_shape=[
            jax.ShapeDtypeStruct((rows, cols), jnp.float32),
            jax.ShapeDtypeStruct((rows, 128), jnp.float32),
        ],
        compiler_params=pltpu.CompilerParams(vmem_limit_bytes=VMEM_BYTES),
        cost_estimate=pl.CostEstimate(
            flops=2 * rows * consumers * (depth + cols), bytes_accessed=rows * cols * 8, transcendentals=rows * consumers
        ),
        name="panel",
    )(chars, tastes, row_values, weighted)


def share_sums(expo, factors):
    rows, consumers = expo.shape
    block = 1024

    def kernel(expo_ref, factor_ref, out_ref):
        @pl.when(pl.program_id(0) == 0)
        def _():
            out_ref[...] = jnp.zeros_like(out_ref)

        out_ref[...] += dot_nt(factor_ref[...], expo_ref[...])

    return pl.pallas_call(
        kernel,
        grid=(consumers // block,),
        in_specs=[
            pl.BlockSpec((rows, block), lambda i: (0, i)),
            pl.BlockSpec((16, block), lambda i: (0, i)),
        ],
        out_specs=pl.BlockSpec((16, rows), lambda i: (0, 0)),
        out_shape=jax.ShapeDtypeStruct((16, rows), jnp.float32),
        compiler_params=pltpu.CompilerParams(vmem_limit_bytes=VMEM_BYTES),
        cost_estimate=pl.CostEstimate(flops=2 * rows * consumers * 128, bytes_accessed=rows * consumers * 2, transcendentals=0),
        name="share_sums",
    )(expo, factors)


def swap(value, axis, mask):
    size = lax.axis_size(axis)
    return lax.ppermute(value, axis, [(i, i ^ mask) for i in range(size)])


def butterfly_masks(size):
    masks, step = [], 1
    while step < size:
        masks.append(step)
        if step * 2 < size:
            masks.append(step * 3)
        step *= 4
    return masks


def body(tastes, price_coef, characteristics, mean_utility, panel_cols, firm_map, inverses):
    products, depth = characteristics.shape
    consumers = tastes.shape[0]
    cols = panel_cols.shape[0]
    holders = lax.axis_size("prod")
    per_pair = products // holders
    count_products = products * holders
    count_consumers = consumers * lax.axis_size("cons")
    base = lax.axis_index("prod") * products
    core = lax.axis_index("cons") % 2

    wanted, order = lax.sort((firm_map, lax.iota(jnp.int32, products)), num_keys=1)
    ids = lax.all_to_all(wanted.reshape(holders, per_pair), "prod", split_axis=0, concat_axis=0, tiled=True) - base

    pieces = jnp.stack(split3(mean_utility), axis=1)
    chars = jnp.concatenate([characteristics, jnp.pad(pieces, ((0, 0), (0, depth - 3)))], axis=1)
    beside = jnp.broadcast_to(lax.iota(jnp.int32, depth)[None, :] < 3, (consumers, depth)).astype(jnp.bfloat16)
    people = jnp.concatenate([tastes, beside], axis=1)

    product_ids = base + lax.iota(jnp.int32, products)
    hits = (panel_cols[:, None] == product_ids[None, :]).astype(jnp.bfloat16)
    col_chars = jnp.dot(hits, chars, preferred_element_type=jnp.float32).astype(jnp.bfloat16)

    stat, expo = stats(chars, people)

    sent = pick_rows(ids.T, chars).reshape(holders, per_pair, 2 * depth)
    received = lax.all_to_all(sent, "prod", split_axis=0, concat_axis=0, tiled=True).reshape(products, 2 * depth)
    firm_chars = place_rows(order.reshape(1, products), received)

    masks = butterfly_masks(holders)
    for mask in masks:
        col_chars = col_chars + swap(col_chars, "prod", mask)

    local_peak = stat[0]
    for mask in masks:
        other = swap(stat, "prod", mask)
        joint = jnp.maximum(stat[0], other[0])
        total = stat[1] * jnp.exp(stat[0] - joint) + other[1] * jnp.exp(other[0] - joint)
        stat = jnp.stack([joint, total])
    peak = jnp.maximum(stat[0], 0.0)
    denom = jnp.exp(-peak) + stat[1] * jnp.exp(stat[0] - peak)
    ratio = count_products / denom

    row_values = jnp.stack([peak, ratio, price_coef])
    weighted, diag_part = weights(people, row_values, col_chars)
    diagonal = jnp.sum(diag_part, axis=1)
    for mask in (1, 2):
        diagonal = diagonal + swap(diagonal, "cons", mask)
    room = 32768.0 / (count_products * jnp.maximum(diagonal, 1e-25))
    panel_part, share_part = panel(firm_chars, people, row_values, weighted)

    half = products // 2
    kept = lax.dynamic_slice_in_dim(panel_part, core * half, half, 0)
    given = lax.dynamic_slice_in_dim(panel_part, (1 - core) * half, half, 0)
    chip_sum = lax.optimization_barrier(((kept + swap(given, "cons", 1)) * room[None, :]).astype(jnp.float16))
    other_sum = swap(chip_sum, "cons", 2)

    factors = jnp.stack(split3(jnp.exp(local_peak - peak) * ratio), axis=0)
    own_shares = jnp.sum(share_sums(expo, jnp.pad(factors, ((0, 13), (0, 0)))), axis=0)
    sums = lax.psum(jnp.concatenate([own_shares, jnp.sum(share_part, axis=1)]), "cons") / count_consumers
    shares, firm_shares = sums[:products], sums[products:]

    firm_count, block_size = inverses.shape[0], inverses.shape[1]
    firm_ids = lax.dynamic_slice_in_dim(firm_map, core * half, half, 0)
    marks = firm_ids[:, None] == panel_cols[None, :]
    cross = (chip_sum.astype(jnp.float32) + other_sum.astype(jnp.float32)) / (room[None, :] * count_consumers)
    jacobian = cross - jnp.where(marks, diagonal[None, :] / count_consumers, 0.0)
    own_inverses = lax.dynamic_slice_in_dim(inverses, core * (firm_count // 2), firm_count // 2, 0)
    response = jnp.einsum(
        "fab,fbc->fac",
        own_inverses,
        jacobian.reshape(firm_count // 2, block_size, cols),
        precision=lax.Precision.HIGHEST,
    ).reshape(half, cols)
    other_response = swap(response, "cons", 1)
    response = jnp.where(
        core == 0,
        jnp.concatenate([response, other_response], axis=0),
        jnp.concatenate([other_response, response], axis=0),
    )
    markup = jnp.sum(inverses * firm_shares.reshape(firm_count, 1, block_size), axis=2).reshape(products)
    return (shares, markup, response)


def solution(mesh):
    return jax.shard_map(
        body,
        mesh=mesh,
        in_specs=(
            P("cons", None),
            P("cons"),
            P("prod", None),
            P("prod"),
            P(),
            P("prod"),
            P("prod", None, None),
        ),
        out_specs=(P("prod"), P("prod"), P("prod", None)),
        check_vma=False,
    )
```

```python
import jax
import jax.numpy as jnp
from jax import lax
from jax.experimental import pallas as pl
from jax.experimental.pallas import tpu as pltpu
from jax.sharding import PartitionSpec as P

NT = (((1,), (1,)), ((), ()))
VMEM_BYTES = 56 * 1024 * 1024


def dot_nt(left, right):
    return lax.dot_general(left, right, NT, preferred_element_type=jnp.float32)


def split3(values):
    high = lax.reduce_precision(values, 8, 7)
    middle = lax.reduce_precision(values - high, 8, 7)
    low = lax.reduce_precision(values - high - middle, 8, 7)
    high, middle, low = (piece.astype(jnp.bfloat16) for piece in (high, middle, low))
    return high, middle, low


def beside_ones(tastes):
    ones = lax.broadcasted_iota(jnp.int32, tastes.shape, 1) < 3
    return jnp.concatenate([tastes, jnp.where(ones, 1.0, 0.0).astype(tastes.dtype)], axis=1)


def stats_kernel(block, chunk, chars_ref, tastes_ref, stat_ref, expo_ref, util_ref):
    rows = chars_ref.shape[0]
    tastes = beside_ones(tastes_ref[...])
    peak = jnp.full((8, block), -jnp.inf, jnp.float32)
    for start in range(0, rows, chunk):
        util = dot_nt(chars_ref[start : start + chunk, :], tastes)
        util_ref[start : start + chunk, :] = util
        peak = jnp.maximum(peak, jnp.max(util.reshape(chunk // 8, 8, block), axis=0))
    peak = jnp.max(peak, axis=0, keepdims=True)
    total = jnp.zeros((8, block), jnp.float32)
    for start in range(0, rows, chunk):
        expo = jnp.exp(util_ref[start : start + chunk, :] - peak)
        total = total + jnp.sum(expo.reshape(chunk // 8, 8, block), axis=0)
        expo_ref[start : start + chunk, :] = expo.astype(jnp.bfloat16)
    stat_ref[0:1, :] = peak
    stat_ref[1:2, :] = jnp.sum(total, axis=0, keepdims=True)


def stats(chars, tastes):
    rows, depth = chars.shape
    consumers = tastes.shape[0]
    block, chunk = 256, 256

    def kernel(*refs):
        stats_kernel(block, chunk, *refs)

    return pl.pallas_call(
        kernel,
        grid=(consumers // block,),
        in_specs=[
            pl.BlockSpec((rows, depth), lambda i: (0, 0)),
            pl.BlockSpec((block, tastes.shape[1]), lambda i: (i, 0)),
        ],
        out_specs=[
            pl.BlockSpec((2, block), lambda i: (0, i)),
            pl.BlockSpec((rows, block), lambda i: (0, i)),
        ],
        out_shape=[
            jax.ShapeDtypeStruct((2, consumers), jnp.float32),
            jax.ShapeDtypeStruct((rows, consumers), jnp.bfloat16),
        ],
        scratch_shapes=[pltpu.VMEM((rows, block), jnp.float32)],
        compiler_params=pltpu.CompilerParams(vmem_limit_bytes=VMEM_BYTES),
        cost_estimate=pl.CostEstimate(
            flops=2 * rows * consumers * depth, bytes_accessed=rows * consumers * 2, transcendentals=rows * consumers
        ),
        name="stats",
    )(chars, tastes)


def pick_rows(ids_t, chars, tail):
    per_pair, holders = ids_t.shape
    rows, depth = chars.shape
    extra = tail.shape[0]
    each = per_pair + extra
    group = max(1, 256 // per_pair)

    def kernel(ids_ref, chars_ref, tail_ref, out_ref):
        lanes = lax.broadcasted_iota(jnp.int32, (per_pair, rows), 1)
        table = chars_ref[...]
        for start in range(0, holders, group):
            span = range(start, min(start + group, holders))
            marks = [jnp.where(ids_ref[:, q : q + 1] == lanes, 1.0, 0.0).astype(jnp.bfloat16) for q in span]
            picked = jnp.dot(jnp.concatenate(marks, axis=0), table, preferred_element_type=jnp.float32)
            for place, q in enumerate(span):
                mine = picked[place * per_pair : (place + 1) * per_pair, :]
                out_ref[q * each : q * each + per_pair, :] = mine.astype(jnp.bfloat16)
                out_ref[q * each + per_pair : (q + 1) * each, :] = tail_ref[...]

    return pl.pallas_call(
        kernel,
        out_shape=jax.ShapeDtypeStruct((each * holders, depth), jnp.bfloat16),
        compiler_params=pltpu.CompilerParams(vmem_limit_bytes=VMEM_BYTES),
        cost_estimate=pl.CostEstimate(flops=2 * rows * rows * depth, bytes_accessed=rows * depth * 4, transcendentals=0),
        name="pick_rows",
    )(ids_t, chars, tail)


def place_rows(order, received, holders):
    rows = order.shape[1]
    total, depth = received.shape
    per_pair, each = rows // holders, total // holders
    chunk = 256

    def kernel(order_ref, received_ref, out_ref):
        order_row = order_ref[...]
        table = jnp.concatenate([received_ref[q * each : q * each + per_pair, :] for q in range(holders)], axis=0)
        for start in range(0, rows, chunk):
            ids = start + lax.broadcasted_iota(jnp.int32, (chunk, rows), 0)
            hot = jnp.where(ids == order_row, 1.0, 0.0).astype(jnp.bfloat16)
            placed = jnp.dot(hot, table, preferred_element_type=jnp.float32)
            out_ref[start : start + chunk, :] = placed.astype(jnp.bfloat16)

    return pl.pallas_call(
        kernel,
        out_shape=jax.ShapeDtypeStruct((rows, depth), jnp.bfloat16),
        compiler_params=pltpu.CompilerParams(vmem_limit_bytes=VMEM_BYTES),
        cost_estimate=pl.CostEstimate(flops=2 * rows * rows * depth, bytes_accessed=rows * depth * 4, transcendentals=0),
        name="place_rows",
    )(order, received)


def lane_groups(values):
    total = values[:, 0:128]
    for start in range(128, values.shape[1], 128):
        total = total + values[:, start : start + 128]
    return total


def weights(tastes, row_values, col_chars):
    consumers = tastes.shape[0]
    cols, depth = col_chars.shape
    block = 1024

    def kernel(tastes_ref, rows_ref, cols_ref, weight_ref, diag_ref):
        @pl.when(pl.program_id(0) == 0)
        def _():
            diag_ref[...] = jnp.zeros_like(diag_ref)

        expo = jnp.exp(dot_nt(cols_ref[...], beside_ones(tastes_ref[...])) - rows_ref[0:1, :])
        weighted = rows_ref[2:3, :] * (expo * rows_ref[1:2, :])
        diag_ref[...] += lane_groups(weighted)
        weight_ref[...] = weighted.astype(jnp.bfloat16)

    return pl.pallas_call(
        kernel,
        grid=(consumers // block,),
        in_specs=[
            pl.BlockSpec((block, tastes.shape[1]), lambda i: (i, 0)),
            pl.BlockSpec((3, block), lambda i: (0, i)),
            pl.BlockSpec((cols, depth), lambda i: (0, 0)),
        ],
        out_specs=[
            pl.BlockSpec((cols, block), lambda i: (0, i)),
            pl.BlockSpec((cols, 128), lambda i: (0, 0)),
        ],
        out_shape=[
            jax.ShapeDtypeStruct((cols, consumers), jnp.bfloat16),
            jax.ShapeDtypeStruct((cols, 128), jnp.float32),
        ],
        compiler_params=pltpu.CompilerParams(vmem_limit_bytes=VMEM_BYTES),
        cost_estimate=pl.CostEstimate(
            flops=2 * cols * consumers * depth, bytes_accessed=cols * consumers * 2, transcendentals=cols * consumers
        ),
        name="weights",
    )(tastes, row_values, col_chars)


def panel(chars, part, parts, tastes, row_values, weighted):
    rows, depth = chars.shape[0] // parts, chars.shape[1]
    consumers = tastes.shape[0]
    cols = weighted.shape[0]
    block, chunk = 1024, 256

    def kernel(chars_ref, tastes_ref, rows_ref, weight_ref, panel_ref, share_ref):
        @pl.when(pl.program_id(0) == 0)
        def _():
            panel_ref[...] = jnp.zeros_like(panel_ref)
            share_ref[...] = jnp.zeros_like(share_ref)

        people, weight = beside_ones(tastes_ref[...]), weight_ref[...]
        peak, ratio = rows_ref[0:1, :], rows_ref[1:2, :]
        for start in range(0, rows, chunk):
            scaled = jnp.exp(dot_nt(chars_ref[start : start + chunk, :], people) - peak) * ratio
            share_ref[start : start + chunk, :] += lane_groups(scaled)
            panel_ref[start : start + chunk, :] += dot_nt(scaled.astype(jnp.bfloat16), weight)

    return pl.pallas_call(
        kernel,
        grid=(consumers // block,),
        in_specs=[
            pl.BlockSpec((rows, depth), lambda i: (part, 0)),
            pl.BlockSpec((block, tastes.shape[1]), lambda i: (i, 0)),
            pl.BlockSpec((3, block), lambda i: (0, i)),
            pl.BlockSpec((cols, block), lambda i: (0, i)),
        ],
        out_specs=[
            pl.BlockSpec((rows, cols), lambda i: (0, 0)),
            pl.BlockSpec((rows, 128), lambda i: (0, 0)),
        ],
        out_shape=[
            jax.ShapeDtypeStruct((rows, cols), jnp.float32),
            jax.ShapeDtypeStruct((rows, 128), jnp.float32),
        ],
        compiler_params=pltpu.CompilerParams(vmem_limit_bytes=VMEM_BYTES),
        cost_estimate=pl.CostEstimate(
            flops=2 * rows * consumers * (depth + cols), bytes_accessed=rows * cols * 8, transcendentals=rows * consumers
        ),
        name="panel",
    )(chars, tastes, row_values, weighted)


def share_sums(expo, factors):
    rows, consumers = expo.shape
    block = 1024

    def kernel(expo_ref, factor_ref, out_ref):
        @pl.when(pl.program_id(0) == 0)
        def _():
            out_ref[...] = jnp.zeros_like(out_ref)

        out_ref[...] += dot_nt(expo_ref[...], factor_ref[...])

    return pl.pallas_call(
        kernel,
        grid=(consumers // block,),
        in_specs=[
            pl.BlockSpec((rows, block), lambda i: (0, i)),
            pl.BlockSpec((128, block), lambda i: (0, i)),
        ],
        out_specs=pl.BlockSpec((rows, 128), lambda i: (0, 0)),
        out_shape=jax.ShapeDtypeStruct((rows, 128), jnp.float32),
        compiler_params=pltpu.CompilerParams(vmem_limit_bytes=VMEM_BYTES),
        cost_estimate=pl.CostEstimate(flops=2 * rows * consumers * 128, bytes_accessed=rows * consumers * 2, transcendentals=0),
        name="share_sums",
    )(expo, factors)


def swap(value, axis, mask):
    size = lax.axis_size(axis)
    return lax.ppermute(value, axis, [(i, i ^ mask) for i in range(size)])


def butterfly_masks(size):
    masks, step = [], 1
    while step < size:
        masks.append(step)
        if step * 2 < size:
            masks.append(step * 3)
        step *= 4
    return masks


def body(tastes, price_coef, characteristics, mean_utility, panel_cols, firm_map, inverses):
    products, depth = characteristics.shape
    consumers = tastes.shape[0]
    cols = panel_cols.shape[0]
    holders = lax.axis_size("prod")
    per_pair = products // holders
    count_products = products * holders
    count_consumers = consumers * lax.axis_size("cons")
    base = lax.axis_index("prod") * products
    core = lax.axis_index("cons") % 2

    pieces = jnp.stack(split3(mean_utility), axis=1)
    chars = jnp.concatenate([characteristics, jnp.pad(pieces, ((0, 0), (0, depth - 3)))], axis=1)
    width = 2 * depth

    wanted, order = lax.sort((firm_map, lax.iota(jnp.int32, products)), num_keys=1)
    wanted = (wanted % products).reshape(holders, per_pair)
    digits = jnp.concatenate([wanted // 256, wanted % 256], axis=1).astype(jnp.bfloat16)
    digits = jnp.pad(digits, ((0, 0), (0, width - 2 * per_pair)))[:, None, :]
    product_ids = base + lax.iota(jnp.int32, products)
    hits = (panel_cols[:, None] == product_ids[None, :]).astype(jnp.bfloat16)
    col_part = jnp.dot(hits, chars, preferred_element_type=jnp.float32).astype(jnp.bfloat16)
    share_cols = cols // holders
    message = jnp.concatenate([col_part.reshape(holders, share_cols, width), digits], axis=1)
    message = jnp.pad(message, ((0, 0), (0, -(share_cols + 1) % 16), (0, 0)))
    first = lax.all_to_all(message, "prod", split_axis=0, concat_axis=0, tiled=True)

    stat, expo = stats(chars, tastes)
    local_peak = stat[0]

    asked = first[:, share_cols, : 2 * per_pair].astype(jnp.int32)
    ids = asked[:, :per_pair] * 256 + asked[:, per_pair:]
    collected = jnp.sum(first[:, :share_cols, :].astype(jnp.float32), axis=0).astype(jnp.bfloat16)
    collected = jnp.pad(collected, ((0, -share_cols % 16), (0, 0)))
    each = per_pair + collected.shape[0]
    sent = pick_rows(ids.T, chars, collected).reshape(holders, each, width)
    second = lax.all_to_all(sent, "prod", split_axis=0, concat_axis=0, tiled=True)
    col_chars = second[:, per_pair : per_pair + share_cols, :].reshape(cols, width)
    half, quarter = products // 2, products // 4
    kept_row = (order // half == core).astype(jnp.int32)
    place = (order // quarter % 2) * half + kept_row * quarter + order % quarter
    firm_chars = place_rows(place.reshape(1, products), second.reshape(holders * each, width), holders)

    for mask in butterfly_masks(holders):
        other = swap(stat, "prod", mask)
        joint = jnp.maximum(stat[0], other[0])
        total = stat[1] * jnp.exp(stat[0] - joint) + other[1] * jnp.exp(other[0] - joint)
        stat = jnp.stack([joint, total])
    peak = jnp.maximum(stat[0], 0.0)
    denom = jnp.exp(-peak) + stat[1] * jnp.exp(stat[0] - peak)
    ratio = count_products / denom

    row_values = jnp.stack([peak, ratio, price_coef])
    weighted, diag_part = weights(tastes, row_values, col_chars)
    diagonal = jnp.sum(diag_part, axis=1)
    for mask in (1, 2):
        diagonal = diagonal + swap(diagonal, "cons", mask)
    room = 32768.0 / (count_products * jnp.maximum(diagonal, 1e-25))

    firm_count, block_size = inverses.shape[0], inverses.shape[1]
    own_inverses = lax.dynamic_slice_in_dim(inverses, core * (firm_count // 2), firm_count // 2, 0)
    firm_ids = lax.dynamic_slice_in_dim(firm_map, core * half, half, 0)
    chip_sums, other_sums, share_parts = [], [], []
    for part in (0, 1):
        given, given_share = panel(firm_chars, 2 * part, 4, tastes, row_values, weighted)
        got = swap(given, "cons", 1)
        kept, kept_share = panel(firm_chars, 2 * part + 1, 4, tastes, row_values, weighted)
        chip_sum = lax.optimization_barrier(((kept + got) * room[None, :]).astype(jnp.float16))
        chip_sums.append(chip_sum)
        other_sums.append(swap(chip_sum, "cons", 2))
        share_parts.append((given_share, kept_share))

    given_share = jnp.sum(jnp.concatenate([share_parts[0][0], share_parts[1][0]]), axis=1)
    kept_share = jnp.sum(jnp.concatenate([share_parts[0][1], share_parts[1][1]]), axis=1)
    first_half = jnp.where(core == 0, kept_share, given_share)
    second_half = jnp.where(core == 0, given_share, kept_share)
    factors = jnp.stack(split3(jnp.exp(local_peak - peak) * ratio), axis=0)
    own_shares = jnp.sum(share_sums(expo, jnp.pad(factors, ((0, 125), (0, 0)))), axis=1)
    sums = jnp.concatenate([own_shares, first_half, second_half])
    for mask in (1, 2):
        sums = sums + swap(sums, "cons", mask)
    sums = sums / count_consumers
    other_sums[1], sums = lax.optimization_barrier((other_sums[1], sums))
    shares, firm_shares = sums[:products], sums[products:]

    responses = []
    for part in (0, 1):
        both = chip_sums[part].astype(jnp.float32) + other_sums[part].astype(jnp.float32)
        part_ids = firm_ids[part * quarter : (part + 1) * quarter]
        marks = part_ids[:, None] == panel_cols[None, :]
        jacobian = both / (room[None, :] * count_consumers) - jnp.where(marks, diagonal[None, :] / count_consumers, 0.0)
        blocks = firm_count // 4
        response = jnp.einsum(
            "fab,fbc->fac",
            own_inverses[part * blocks : (part + 1) * blocks],
            jacobian.reshape(blocks, block_size, cols),
            precision=lax.Precision.HIGHEST,
        ).reshape(quarter, cols)
        responses.append((response, swap(response, "cons", 1)))
    mine = [pair[0] for pair in responses]
    theirs = [pair[1] for pair in responses]
    response = jnp.where(core == 0, jnp.concatenate(mine + theirs, axis=0), jnp.concatenate(theirs + mine, axis=0))
    markup = jnp.sum(inverses * firm_shares.reshape(firm_count, 1, block_size), axis=2).reshape(products)
    return (shares, markup, response)


def solution(mesh):
    return jax.shard_map(
        body,
        mesh=mesh,
        in_specs=(
            P("cons", None),
            P("cons"),
            P("prod", None),
            P("prod"),
            P(),
            P("prod"),
            P("prod", None, None),
        ),
        out_specs=(P("prod"), P("prod"), P("prod", None)),
        check_vma=False,
    )
```

```python
import jax
import jax.numpy as jnp
from jax import lax
from jax.experimental import pallas as pl
from jax.experimental.pallas import tpu as pltpu
from jax.sharding import PartitionSpec as P

NT = (((1,), (1,)), ((), ()))
VMEM_BYTES = 24 * 1024 * 1024


def dot_nt(left, right):
    return lax.dot_general(left, right, NT, preferred_element_type=jnp.float32)


def split3(values):
    high = lax.reduce_precision(values, 8, 7)
    middle = lax.reduce_precision(values - high, 8, 7)
    low = lax.reduce_precision(values - high - middle, 8, 7)
    high, middle, low = (piece.astype(jnp.bfloat16) for piece in (high, middle, low))
    return high, middle, low


def beside_ones(tastes):
    ones = lax.broadcasted_iota(jnp.int32, tastes.shape, 1) < 3
    return jnp.concatenate([tastes, jnp.where(ones, 1.0, 0.0).astype(tastes.dtype)], axis=1)


def stats(chars, tastes, gate):
    rows, depth = chars.shape
    consumers = tastes.shape[0]
    block, sub, chunk = 2048, 256, 256
    count = block // sub

    def kernel(chars_ref, tastes_ref, gate_ref, stat_ref, util_ref):
        people = [beside_ones(tastes_ref[k * sub : (k + 1) * sub, :]) for k in range(count)]
        before = None
        for k in range(count + 1):
            peak = jnp.full((8, sub), -jnp.inf, jnp.float32)
            total = jnp.zeros((8, sub), jnp.float32)
            for start in range(0, rows, chunk):
                if k < count:
                    util = dot_nt(chars_ref[start : start + chunk, :], people[k])
                    util_ref[k % 2, start : start + chunk, :] = util
                    peak = jnp.maximum(peak, jnp.max(util.reshape(chunk // 8, 8, sub), axis=0))
                if k > 0:
                    expo = jnp.exp(util_ref[(k - 1) % 2, start : start + chunk, :] - before)
                    total = total + jnp.sum(expo.reshape(chunk // 8, 8, sub), axis=0)
            if k > 0:
                stat_ref[0:1, (k - 1) * sub : k * sub] = before
                stat_ref[1:2, (k - 1) * sub : k * sub] = jnp.sum(total, axis=0, keepdims=True)
            before = jnp.max(peak, axis=0, keepdims=True)

    return pl.pallas_call(
        kernel,
        grid=(consumers // block,),
        in_specs=[
            pl.BlockSpec((rows, depth), lambda i: (0, 0)),
            pl.BlockSpec((block, tastes.shape[1]), lambda i: (i, 0)),
            pl.BlockSpec(memory_space=pl.ANY),
        ],
        out_specs=pl.BlockSpec((2, block), lambda i: (0, i)),
        out_shape=jax.ShapeDtypeStruct((2, consumers), jnp.float32),
        scratch_shapes=[pltpu.VMEM((2, rows, sub), jnp.float32)],
        compiler_params=pltpu.CompilerParams(vmem_limit_bytes=VMEM_BYTES),
        name="stats",
    )(chars, tastes, gate)


def pick_rows(ids_t, chars, tail, stat):
    per_pair, holders = ids_t.shape
    rows, depth = chars.shape
    extra = tail.shape[0]
    each = per_pair + extra
    group = max(1, 256 // per_pair)

    def kernel(ids_ref, chars_ref, tail_ref, stat_ref, out_ref, stat_out_ref):
        stat_out_ref[...] = stat_ref[...]
        lanes = lax.broadcasted_iota(jnp.int32, (per_pair, rows), 1)
        table = chars_ref[...]
        for start in range(0, holders, group):
            span = range(start, min(start + group, holders))
            marks = [jnp.where(ids_ref[:, q : q + 1] == lanes, 1.0, 0.0).astype(jnp.bfloat16) for q in span]
            picked = jnp.dot(jnp.concatenate(marks, axis=0), table, preferred_element_type=jnp.float32)
            for place, q in enumerate(span):
                mine = picked[place * per_pair : (place + 1) * per_pair, :]
                out_ref[q * each : q * each + per_pair, :] = mine.astype(jnp.bfloat16)
                out_ref[q * each + per_pair : (q + 1) * each, :] = tail_ref[...]

    return pl.pallas_call(
        kernel,
        out_shape=[jax.ShapeDtypeStruct((each * holders, depth), jnp.bfloat16), jax.ShapeDtypeStruct(stat.shape, stat.dtype)],
        compiler_params=pltpu.CompilerParams(vmem_limit_bytes=VMEM_BYTES),
        name="pick_rows",
    )(ids_t, chars, tail, stat)


def place_rows(order, received, holders, stat):
    rows = order.shape[1]
    total, depth = received.shape
    per_pair, each = rows // holders, total // holders
    chunk = 256

    def kernel(order_ref, received_ref, stat_ref, out_ref, stat_out_ref):
        stat_out_ref[...] = stat_ref[...]
        order_row = order_ref[...]
        table = jnp.concatenate([received_ref[q * each : q * each + per_pair, :] for q in range(holders)], axis=0)
        for start in range(0, rows, chunk):
            ids = start + lax.broadcasted_iota(jnp.int32, (chunk, rows), 0)
            hot = jnp.where(ids == order_row, 1.0, 0.0).astype(jnp.bfloat16)
            placed = jnp.dot(hot, table, preferred_element_type=jnp.float32)
            out_ref[start : start + chunk, :] = placed.astype(jnp.bfloat16)

    return pl.pallas_call(
        kernel,
        out_shape=[jax.ShapeDtypeStruct((rows, depth), jnp.bfloat16), jax.ShapeDtypeStruct(stat.shape, stat.dtype)],
        compiler_params=pltpu.CompilerParams(vmem_limit_bytes=VMEM_BYTES),
        name="place_rows",
    )(order, received, stat)


def lane_groups(values):
    total = values[:, 0:128]
    for start in range(128, values.shape[1], 128):
        total = total + values[:, start : start + 128]
    return total


def first_panel(chars, parts, tastes, row_values, col_chars):
    rows, depth = chars.shape[0] // parts, chars.shape[1]
    consumers = tastes.shape[0]
    cols = col_chars.shape[0]
    block, chunk = 1024, 256

    def kernel(chars_ref, tastes_ref, rows_ref, cols_ref, panel_ref, share_ref, weight_ref, diag_ref):
        @pl.when(pl.program_id(0) == 0)
        def _():
            panel_ref[...] = jnp.zeros_like(panel_ref)
            share_ref[...] = jnp.zeros_like(share_ref)
            diag_ref[...] = jnp.zeros_like(diag_ref)

        people = beside_ones(tastes_ref[...])
        peak, ratio = rows_ref[0:1, :], rows_ref[1:2, :]
        weighted = rows_ref[2:3, :] * (jnp.exp(dot_nt(cols_ref[...], people) - peak) * ratio)
        diag_ref[...] += lane_groups(weighted)
        weight = weighted.astype(jnp.bfloat16)
        weight_ref[...] = weight
        for start in range(0, rows, chunk):
            scaled = jnp.exp(dot_nt(chars_ref[start : start + chunk, :], people) - peak) * ratio
            share_ref[start : start + chunk, :] += lane_groups(scaled)
            panel_ref[start : start + chunk, :] += dot_nt(scaled.astype(jnp.bfloat16), weight)

    return pl.pallas_call(
        kernel,
        grid=(consumers // block,),
        in_specs=[
            pl.BlockSpec((rows, depth), lambda i: (0, 0)),
            pl.BlockSpec((block, tastes.shape[1]), lambda i: (i, 0)),
            pl.BlockSpec((3, block), lambda i: (0, i)),
            pl.BlockSpec((cols, depth), lambda i: (0, 0)),
        ],
        out_specs=[
            pl.BlockSpec((rows, cols), lambda i: (0, 0)),
            pl.BlockSpec((rows, 128), lambda i: (0, 0)),
            pl.BlockSpec((cols, block), lambda i: (0, i)),
            pl.BlockSpec((cols, 128), lambda i: (0, 0)),
        ],
        out_shape=[
            jax.ShapeDtypeStruct((rows, cols), jnp.float32),
            jax.ShapeDtypeStruct((rows, 128), jnp.float32),
            jax.ShapeDtypeStruct((cols, consumers), jnp.bfloat16),
            jax.ShapeDtypeStruct((cols, 128), jnp.float32),
        ],
        compiler_params=pltpu.CompilerParams(vmem_limit_bytes=VMEM_BYTES),
        cost_estimate=pl.CostEstimate(
            flops=2 * rows * consumers * (depth + cols), bytes_accessed=rows * cols * 8, transcendentals=rows * consumers
        ),
        name="first_panel",
    )(chars, tastes, row_values, col_chars)


def panel(chars, part, parts, tastes, row_values, weighted, gate):
    rows, depth = chars.shape[0] // parts, chars.shape[1]
    consumers = tastes.shape[0]
    cols = weighted.shape[0]
    chunk = 256

    def kernel(chars_ref, tastes_ref, rows_ref, weight_ref, gate_ref, panel_ref, share_ref):
        people, weight = beside_ones(tastes_ref[...]), weight_ref[...]
        peak, ratio = rows_ref[0:1, :], rows_ref[1:2, :]
        for start in range(0, rows, chunk):
            scaled = jnp.exp(dot_nt(chars_ref[start : start + chunk, :], people) - peak) * ratio
            share_ref[start : start + chunk, :] = lane_groups(scaled)
            panel_ref[start : start + chunk, :] = dot_nt(scaled.astype(jnp.bfloat16), weight)

    return pl.pallas_call(
        kernel,
        grid=(1,),
        in_specs=[
            pl.BlockSpec((rows, depth), lambda i: (part, 0)),
            pl.BlockSpec(tastes.shape, lambda i: (0, 0)),
            pl.BlockSpec((3, consumers), lambda i: (0, 0)),
            pl.BlockSpec((cols, consumers), lambda i: (0, 0)),
            pl.BlockSpec(memory_space=pl.ANY),
        ],
        out_specs=[
            pl.BlockSpec((rows, cols), lambda i: (0, 0)),
            pl.BlockSpec((rows, 128), lambda i: (0, 0)),
        ],
        out_shape=[
            jax.ShapeDtypeStruct((rows, cols), jnp.float32),
            jax.ShapeDtypeStruct((rows, 128), jnp.float32),
        ],
        compiler_params=pltpu.CompilerParams(vmem_limit_bytes=VMEM_BYTES),
        cost_estimate=pl.CostEstimate(
            flops=2 * rows * consumers * (depth + cols), bytes_accessed=rows * cols * 8, transcendentals=rows * consumers
        ),
        name="panel",
    )(chars, tastes, row_values, weighted, gate)


def share_sums(chars, tastes, row_values, gate):
    rows, depth = chars.shape
    consumers = tastes.shape[0]
    block, chunk = 1024, 256

    def kernel(chars_ref, tastes_ref, rows_ref, gate_ref, share_ref):
        @pl.when(pl.program_id(0) == 0)
        def _():
            share_ref[...] = jnp.zeros_like(share_ref)

        people = beside_ones(tastes_ref[...])
        peak, ratio = rows_ref[0:1, :], rows_ref[1:2, :]
        for start in range(0, rows, chunk):
            scaled = jnp.exp(dot_nt(chars_ref[start : start + chunk, :], people) - peak) * ratio
            share_ref[start : start + chunk, :] += lane_groups(scaled)

    return pl.pallas_call(
        kernel,
        grid=(consumers // block,),
        in_specs=[
            pl.BlockSpec((rows, depth), lambda i: (0, 0)),
            pl.BlockSpec((block, tastes.shape[1]), lambda i: (i, 0)),
            pl.BlockSpec((3, block), lambda i: (0, i)),
            pl.BlockSpec(memory_space=pl.ANY),
        ],
        out_specs=pl.BlockSpec((rows, 128), lambda i: (0, 0)),
        out_shape=jax.ShapeDtypeStruct((rows, 128), jnp.float32),
        compiler_params=pltpu.CompilerParams(vmem_limit_bytes=VMEM_BYTES),
        name="share_sums",
    )(chars, tastes, row_values, gate)


def swap(value, axis, mask):
    size = lax.axis_size(axis)
    return lax.ppermute(value, axis, [(i, i ^ mask) for i in range(size)])


def butterfly_masks(size):
    masks, step = [], 1
    while step < size:
        masks.append(step)
        if step * 2 < size:
            masks.append(step * 3)
        step *= 4
    return masks


def body(tastes, price_coef, characteristics, mean_utility, panel_cols, firm_map, inverses):
    products, depth = characteristics.shape
    consumers = tastes.shape[0]
    cols = panel_cols.shape[0]
    holders = lax.axis_size("prod")
    per_pair = products // holders
    count_products = products * holders
    count_consumers = consumers * lax.axis_size("cons")
    base = lax.axis_index("prod") * products
    core = lax.axis_index("cons") % 2

    pieces = jnp.stack(split3(mean_utility), axis=1)
    chars = jnp.concatenate([characteristics, jnp.pad(pieces, ((0, 0), (0, depth - 3)))], axis=1)
    width = 2 * depth

    wanted, order = lax.sort((firm_map, lax.iota(jnp.int32, products)), num_keys=1)
    wanted = (wanted % products).reshape(holders, per_pair)
    digits = jnp.concatenate([wanted // 256, wanted % 256], axis=1).astype(jnp.bfloat16)
    digits = jnp.pad(digits, ((0, 0), (0, width - 2 * per_pair)))[:, None, :]
    product_ids = base + lax.iota(jnp.int32, products)
    hits = (panel_cols[:, None] == product_ids[None, :]).astype(jnp.bfloat16)
    col_part = jnp.dot(hits, chars, preferred_element_type=jnp.float32).astype(jnp.bfloat16)
    share_cols = cols // holders
    message = jnp.concatenate([col_part.reshape(holders, share_cols, width), digits], axis=1)
    message = jnp.pad(message, ((0, 0), (0, -(share_cols + 1) % 16), (0, 0)))
    first = lax.all_to_all(message, "prod", split_axis=0, concat_axis=0, tiled=True)

    stat = stats(chars, tastes, message)

    asked = first[:, share_cols, : 2 * per_pair].astype(jnp.int32)
    ids = asked[:, :per_pair] * 256 + asked[:, per_pair:]
    collected = jnp.sum(first[:, :share_cols, :].astype(jnp.float32), axis=0).astype(jnp.bfloat16)
    collected = jnp.pad(collected, ((0, -share_cols % 16), (0, 0)))
    each = per_pair + collected.shape[0]
    sent, stat = pick_rows(ids.T, chars, collected, stat)
    second = lax.all_to_all(sent.reshape(holders, each, width), "prod", split_axis=0, concat_axis=0, tiled=True)
    col_chars = second[:, per_pair : per_pair + share_cols, :].reshape(cols, width)
    half, quarter = products // 2, products // 4
    kept_row = (order // half == core).astype(jnp.int32)
    place = (order // quarter % 2) * half + kept_row * quarter + order % quarter
    for hop, mask in enumerate(butterfly_masks(holders)):
        if hop == 1:
            firm_chars, stat = place_rows(place.reshape(1, products), second.reshape(holders * each, width), holders, stat)
        other = swap(stat, "prod", mask)
        joint = jnp.maximum(stat[0], other[0])
        total = stat[1] * jnp.exp(stat[0] - joint) + other[1] * jnp.exp(other[0] - joint)
        stat = jnp.stack([joint, total])
    peak = jnp.maximum(stat[0], 0.0)
    denom = jnp.exp(-peak) + stat[1] * jnp.exp(stat[0] - peak)
    ratio = count_products / denom

    row_values = jnp.stack([peak, ratio, price_coef])
    given, given_share, weighted, diag_part = first_panel(firm_chars, 4, tastes, row_values, col_chars)
    diagonal = jnp.sum(diag_part, axis=1)
    for mask in (1, 2):
        diagonal = diagonal + swap(diagonal, "cons", mask)
    room = 32768.0 / (count_products * jnp.maximum(diagonal, 1e-25))

    firm_count, block_size = inverses.shape[0], inverses.shape[1]
    own_inverses = lax.dynamic_slice_in_dim(inverses, core * (firm_count // 2), firm_count // 2, 0)
    firm_ids = lax.dynamic_slice_in_dim(firm_map, core * half, half, 0)
    blocks = firm_count // 4
    chip_sums, share_parts, responses = [], [], []

    def respond(part, chip_sum, other_sum):
        both = chip_sum.astype(jnp.float32) + other_sum.astype(jnp.float32)
        part_ids = firm_ids[part * quarter : (part + 1) * quarter]
        marks = part_ids[:, None] == panel_cols[None, :]
        jacobian = both / (room[None, :] * count_consumers) - jnp.where(marks, diagonal[None, :] / count_consumers, 0.0)
        response = jnp.einsum(
            "fab,fbc->fac",
            own_inverses[part * blocks : (part + 1) * blocks],
            jacobian.reshape(blocks, block_size, cols),
            precision=lax.Precision.HIGHEST,
        ).reshape(quarter, cols)
        responses.append((response, swap(response, "cons", 1)))

    for part in (0, 1):
        if part:
            given, given_share = panel(firm_chars, 2 * part, 4, tastes, row_values, weighted, gate)
        got = swap(given, "cons", 1)
        kept, kept_share = panel(firm_chars, 2 * part + 1, 4, tastes, row_values, weighted, given)
        fitted = (kept + got) * room[None, :]
        chip_sum, gate = lax.optimization_barrier((fitted.astype(jnp.float16), jnp.max(fitted, axis=0, keepdims=True)))
        chip_sums.append((chip_sum, swap(chip_sum, "cons", 2)))
        share_parts.append((given_share, kept_share))
    respond(0, *chip_sums[0])
    gate = gate + responses[0][0][:8]

    given_share = jnp.sum(jnp.concatenate([share_parts[0][0], share_parts[1][0]]), axis=1)
    kept_share = jnp.sum(jnp.concatenate([share_parts[0][1], share_parts[1][1]]), axis=1)
    first_half = jnp.where(core == 0, kept_share, given_share)
    second_half = jnp.where(core == 0, given_share, kept_share)
    own_shares = jnp.sum(share_sums(chars, tastes, row_values, gate), axis=1)
    sums = jnp.concatenate([own_shares, first_half, second_half])
    for mask in (1, 2):
        sums = sums + swap(sums, "cons", mask)
    sums = sums / count_consumers
    shares, firm_shares = sums[:products], sums[products:]

    respond(1, *chip_sums[1])
    mine = [pair[0] for pair in responses]
    theirs = [pair[1] for pair in responses]
    response = jnp.where(core == 0, jnp.concatenate(mine + theirs, axis=0), jnp.concatenate(theirs + mine, axis=0))
    markup = jnp.sum(inverses * firm_shares.reshape(firm_count, 1, block_size), axis=2).reshape(products)
    return (shares, markup, response)


def solution(mesh):
    return jax.shard_map(
        body,
        mesh=mesh,
        in_specs=(
            P("cons", None),
            P("cons"),
            P("prod", None),
            P("prod"),
            P(),
            P("prod"),
            P("prod", None, None),
        ),
        out_specs=(P("prod"), P("prod"), P("prod", None)),
        check_vma=False,
    )
```

```python
import jax
import jax.numpy as jnp
from jax import lax
from jax.experimental import pallas as pl
from jax.experimental.pallas import tpu as pltpu
from jax.sharding import PartitionSpec as P

NT = (((1,), (1,)), ((), ()))
VMEM_BYTES = 24 * 1024 * 1024


def dot_nt(left, right):
    return lax.dot_general(left, right, NT, preferred_element_type=jnp.float32)


def split3(values):
    high = lax.reduce_precision(values, 8, 7)
    middle = lax.reduce_precision(values - high, 8, 7)
    low = lax.reduce_precision(values - high - middle, 8, 7)
    high, middle, low = (piece.astype(jnp.bfloat16) for piece in (high, middle, low))
    return high, middle, low


def beside_ones(tastes):
    ones = lax.broadcasted_iota(jnp.int32, tastes.shape, 1) < 3
    return jnp.concatenate([tastes, jnp.where(ones, 1.0, 0.0).astype(tastes.dtype)], axis=1)


def stats(chars, tastes, gate):
    rows, depth = chars.shape
    consumers = tastes.shape[0]
    block, sub, chunk = 2048, 256, 256
    count = block // sub

    def kernel(chars_ref, tastes_ref, gate_ref, stat_ref, util_ref):
        people = [beside_ones(tastes_ref[k * sub : (k + 1) * sub, :]) for k in range(count)]
        before = None
        for k in range(count + 1):
            peak = jnp.full((8, sub), -jnp.inf, jnp.float32)
            total = jnp.zeros((8, sub), jnp.float32)
            for start in range(0, rows, chunk):
                if k < count:
                    util = dot_nt(chars_ref[start : start + chunk, :], people[k])
                    util_ref[k % 2, start : start + chunk, :] = util
                    peak = jnp.maximum(peak, jnp.max(util.reshape(chunk // 8, 8, sub), axis=0))
                if k > 0:
                    expo = jnp.exp(util_ref[(k - 1) % 2, start : start + chunk, :] - before)
                    total = total + jnp.sum(expo.reshape(chunk // 8, 8, sub), axis=0)
            if k > 0:
                stat_ref[0:1, (k - 1) * sub : k * sub] = before
                stat_ref[1:2, (k - 1) * sub : k * sub] = jnp.sum(total, axis=0, keepdims=True)
            before = jnp.max(peak, axis=0, keepdims=True)

    return pl.pallas_call(
        kernel,
        grid=(consumers // block,),
        in_specs=[
            pl.BlockSpec((rows, depth), lambda i: (0, 0)),
            pl.BlockSpec((block, tastes.shape[1]), lambda i: (i, 0)),
            pl.BlockSpec(memory_space=pl.ANY),
        ],
        out_specs=pl.BlockSpec((2, block), lambda i: (0, i)),
        out_shape=jax.ShapeDtypeStruct((2, consumers), jnp.float32),
        scratch_shapes=[pltpu.VMEM((2, rows, sub), jnp.float32)],
        compiler_params=pltpu.CompilerParams(vmem_limit_bytes=VMEM_BYTES),
        name="stats",
    )(chars, tastes, gate)


def pick_rows(ids_t, chars, tail, stat):
    per_pair, holders = ids_t.shape
    rows, depth = chars.shape
    extra = tail.shape[0]
    each = per_pair + extra
    group = max(1, 256 // per_pair)

    def kernel(ids_ref, chars_ref, tail_ref, stat_ref, out_ref, stat_out_ref):
        stat_out_ref[...] = stat_ref[...]
        lanes = lax.broadcasted_iota(jnp.int32, (per_pair, rows), 1)
        table = chars_ref[...]
        for start in range(0, holders, group):
            span = range(start, min(start + group, holders))
            marks = [jnp.where(ids_ref[:, q : q + 1] == lanes, 1.0, 0.0).astype(jnp.bfloat16) for q in span]
            picked = jnp.dot(jnp.concatenate(marks, axis=0), table, preferred_element_type=jnp.float32)
            for place, q in enumerate(span):
                mine = picked[place * per_pair : (place + 1) * per_pair, :]
                out_ref[q * each : q * each + per_pair, :] = mine.astype(jnp.bfloat16)
                out_ref[q * each + per_pair : (q + 1) * each, :] = tail_ref[...]

    return pl.pallas_call(
        kernel,
        out_shape=[jax.ShapeDtypeStruct((each * holders, depth), jnp.bfloat16), jax.ShapeDtypeStruct(stat.shape, stat.dtype)],
        compiler_params=pltpu.CompilerParams(vmem_limit_bytes=VMEM_BYTES),
        name="pick_rows",
    )(ids_t, chars, tail, stat)


def place_rows(order, received, holders, stat):
    rows = order.shape[1]
    total, depth = received.shape
    per_pair, each = rows // holders, total // holders
    chunk = 256

    def kernel(order_ref, received_ref, stat_ref, out_ref, stat_out_ref):
        stat_out_ref[...] = stat_ref[...]
        order_row = order_ref[...]
        table = jnp.concatenate([received_ref[q * each : q * each + per_pair, :] for q in range(holders)], axis=0)
        for start in range(0, rows, chunk):
            ids = start + lax.broadcasted_iota(jnp.int32, (chunk, rows), 0)
            hot = jnp.where(ids == order_row, 1.0, 0.0).astype(jnp.bfloat16)
            placed = jnp.dot(hot, table, preferred_element_type=jnp.float32)
            out_ref[start : start + chunk, :] = placed.astype(jnp.bfloat16)

    return pl.pallas_call(
        kernel,
        out_shape=[jax.ShapeDtypeStruct((rows, depth), jnp.bfloat16), jax.ShapeDtypeStruct(stat.shape, stat.dtype)],
        compiler_params=pltpu.CompilerParams(vmem_limit_bytes=VMEM_BYTES),
        name="place_rows",
    )(order, received, stat)


def lane_groups(values):
    total = values[:, 0:128]
    for start in range(128, values.shape[1], 128):
        total = total + values[:, start : start + 128]
    return total


def first_panel(chars, parts, tastes, row_values, col_chars):
    rows, depth = chars.shape[0] // parts, chars.shape[1]
    consumers = tastes.shape[0]
    cols = col_chars.shape[0]
    block, chunk = 1024, 256

    def kernel(chars_ref, tastes_ref, rows_ref, cols_ref, panel_ref, share_ref, weight_ref, diag_ref):
        @pl.when(pl.program_id(0) == 0)
        def _():
            panel_ref[...] = jnp.zeros_like(panel_ref)
            share_ref[...] = jnp.zeros_like(share_ref)
            diag_ref[...] = jnp.zeros_like(diag_ref)

        people = beside_ones(tastes_ref[...])
        peak, ratio = rows_ref[0:1, :], rows_ref[1:2, :]
        weighted = rows_ref[2:3, :] * (jnp.exp(dot_nt(cols_ref[...], people) - peak) * ratio)
        diag_ref[...] += lane_groups(weighted)
        weight = weighted.astype(jnp.bfloat16)
        weight_ref[...] = weight
        for start in range(0, rows, chunk):
            scaled = jnp.exp(dot_nt(chars_ref[start : start + chunk, :], people) - peak) * ratio
            share_ref[start : start + chunk, :] += lane_groups(scaled)
            panel_ref[start : start + chunk, :] += dot_nt(scaled.astype(jnp.bfloat16), weight)

    return pl.pallas_call(
        kernel,
        grid=(consumers // block,),
        in_specs=[
            pl.BlockSpec((rows, depth), lambda i: (0, 0)),
            pl.BlockSpec((block, tastes.shape[1]), lambda i: (i, 0)),
            pl.BlockSpec((3, block), lambda i: (0, i)),
            pl.BlockSpec((cols, depth), lambda i: (0, 0)),
        ],
        out_specs=[
            pl.BlockSpec((rows, cols), lambda i: (0, 0)),
            pl.BlockSpec((rows, 128), lambda i: (0, 0)),
            pl.BlockSpec((cols, block), lambda i: (0, i)),
            pl.BlockSpec((cols, 128), lambda i: (0, 0)),
        ],
        out_shape=[
            jax.ShapeDtypeStruct((rows, cols), jnp.float32),
            jax.ShapeDtypeStruct((rows, 128), jnp.float32),
            jax.ShapeDtypeStruct((cols, consumers), jnp.bfloat16),
            jax.ShapeDtypeStruct((cols, 128), jnp.float32),
        ],
        compiler_params=pltpu.CompilerParams(vmem_limit_bytes=VMEM_BYTES),
        cost_estimate=pl.CostEstimate(
            flops=2 * rows * consumers * (depth + cols), bytes_accessed=rows * cols * 8, transcendentals=rows * consumers
        ),
        name="first_panel",
    )(chars, tastes, row_values, col_chars)


def panel(chars, part, parts, tastes, row_values, weighted, gate):
    rows, depth = chars.shape[0] // parts, chars.shape[1]
    consumers = tastes.shape[0]
    cols = weighted.shape[0]
    chunk = 256

    def kernel(chars_ref, tastes_ref, rows_ref, weight_ref, gate_ref, panel_ref, share_ref):
        people, weight = beside_ones(tastes_ref[...]), weight_ref[...]
        peak, ratio = rows_ref[0:1, :], rows_ref[1:2, :]
        for start in range(0, rows, chunk):
            scaled = jnp.exp(dot_nt(chars_ref[start : start + chunk, :], people) - peak) * ratio
            share_ref[start : start + chunk, :] = lane_groups(scaled)
            panel_ref[start : start + chunk, :] = dot_nt(scaled.astype(jnp.bfloat16), weight)

    return pl.pallas_call(
        kernel,
        grid=(1,),
        in_specs=[
            pl.BlockSpec((rows, depth), lambda i: (part, 0)),
            pl.BlockSpec(tastes.shape, lambda i: (0, 0)),
            pl.BlockSpec((3, consumers), lambda i: (0, 0)),
            pl.BlockSpec((cols, consumers), lambda i: (0, 0)),
            pl.BlockSpec(memory_space=pl.ANY),
        ],
        out_specs=[
            pl.BlockSpec((rows, cols), lambda i: (0, 0)),
            pl.BlockSpec((rows, 128), lambda i: (0, 0)),
        ],
        out_shape=[
            jax.ShapeDtypeStruct((rows, cols), jnp.float32),
            jax.ShapeDtypeStruct((rows, 128), jnp.float32),
        ],
        compiler_params=pltpu.CompilerParams(vmem_limit_bytes=VMEM_BYTES),
        cost_estimate=pl.CostEstimate(
            flops=2 * rows * consumers * (depth + cols), bytes_accessed=rows * cols * 8, transcendentals=rows * consumers
        ),
        name="panel",
    )(chars, tastes, row_values, weighted, gate)


def share_sums(chars, tastes, row_values, gate):
    rows, depth = chars.shape
    consumers = tastes.shape[0]
    block, chunk = 1024, 256

    def kernel(chars_ref, tastes_ref, rows_ref, gate_ref, share_ref):
        @pl.when(pl.program_id(0) == 0)
        def _():
            share_ref[...] = jnp.zeros_like(share_ref)

        people = beside_ones(tastes_ref[...])
        peak, ratio = rows_ref[0:1, :], rows_ref[1:2, :]
        for start in range(0, rows, chunk):
            scaled = jnp.exp(dot_nt(chars_ref[start : start + chunk, :], people) - peak) * ratio
            share_ref[start : start + chunk, :] += lane_groups(scaled)

    return pl.pallas_call(
        kernel,
        grid=(consumers // block,),
        in_specs=[
            pl.BlockSpec((rows, depth), lambda i: (0, 0)),
            pl.BlockSpec((block, tastes.shape[1]), lambda i: (i, 0)),
            pl.BlockSpec((3, block), lambda i: (0, i)),
            pl.BlockSpec(memory_space=pl.ANY),
        ],
        out_specs=pl.BlockSpec((rows, 128), lambda i: (0, 0)),
        out_shape=jax.ShapeDtypeStruct((rows, 128), jnp.float32),
        compiler_params=pltpu.CompilerParams(vmem_limit_bytes=VMEM_BYTES),
        name="share_sums",
    )(chars, tastes, row_values, gate)


def swap(value, axis, mask):
    size = lax.axis_size(axis)
    return lax.ppermute(value, axis, [(i, i ^ mask) for i in range(size)])


def butterfly_masks(size):
    masks, step = [], 1
    while step < size:
        masks.append(step)
        if step * 2 < size:
            masks.append(step * 3)
        step *= 4
    return masks


def body(tastes, price_coef, characteristics, mean_utility, panel_cols, firm_map, inverses):
    products, depth = characteristics.shape
    consumers = tastes.shape[0]
    cols = panel_cols.shape[0]
    holders = lax.axis_size("prod")
    per_pair = products // holders
    count_products = products * holders
    count_consumers = consumers * lax.axis_size("cons")
    base = lax.axis_index("prod") * products
    core = lax.axis_index("cons") % 2

    pieces = jnp.stack(split3(mean_utility), axis=1)
    chars = jnp.concatenate([characteristics, jnp.pad(pieces, ((0, 0), (0, depth - 3)))], axis=1)
    width = 2 * depth

    wanted, order = lax.sort((firm_map, lax.iota(jnp.int32, products)), num_keys=1)
    wanted = (wanted % products).reshape(holders, per_pair)
    digits = jnp.concatenate([wanted // 256, wanted % 256], axis=1).astype(jnp.bfloat16)
    digits = jnp.pad(digits, ((0, 0), (0, width - 2 * per_pair)))[:, None, :]
    product_ids = base + lax.iota(jnp.int32, products)
    hits = (panel_cols[:, None] == product_ids[None, :]).astype(jnp.bfloat16)
    col_part = jnp.dot(hits, chars, preferred_element_type=jnp.float32).astype(jnp.bfloat16)
    share_cols = cols // holders
    message = jnp.concatenate([col_part.reshape(holders, share_cols, width), digits], axis=1)
    message = jnp.pad(message, ((0, 0), (0, -(share_cols + 1) % 16), (0, 0)))
    first = lax.all_to_all(message, "prod", split_axis=0, concat_axis=0, tiled=True)

    stat = stats(chars, tastes, message)

    asked = first[:, share_cols, : 2 * per_pair].astype(jnp.int32)
    ids = asked[:, :per_pair] * 256 + asked[:, per_pair:]
    collected = jnp.sum(first[:, :share_cols, :].astype(jnp.float32), axis=0).astype(jnp.bfloat16)
    collected = jnp.pad(collected, ((0, -share_cols % 16), (0, 0)))
    each = per_pair + collected.shape[0]
    sent, stat = pick_rows(ids.T, chars, collected, stat)
    second = lax.all_to_all(sent.reshape(holders, each, width), "prod", split_axis=0, concat_axis=0, tiled=True)
    col_chars = second[:, per_pair : per_pair + share_cols, :].reshape(cols, width)
    half, quarter = products // 2, products // 4
    kept_row = (order // half == core).astype(jnp.int32)
    place = (order // quarter % 2) * half + kept_row * quarter + order % quarter
    def join(stat, masks):
        for mask in masks:
            other = swap(stat, "prod", mask)
            joint = jnp.maximum(stat[0], other[0])
            total = stat[1] * jnp.exp(stat[0] - joint) + other[1] * jnp.exp(other[0] - joint)
            stat = jnp.stack([joint, total])
        return stat

    masks = butterfly_masks(holders)
    stat = lax.cond(panel_cols[0] >= 0, lambda value: join(value, masks[:3]), lambda value: value, stat)
    firm_chars, stat = place_rows(place.reshape(1, products), second.reshape(holders * each, width), holders, stat)
    stat = join(stat, masks[3:])
    peak = jnp.maximum(stat[0], 0.0)
    denom = jnp.exp(-peak) + stat[1] * jnp.exp(stat[0] - peak)
    ratio = count_products / denom

    row_values = jnp.stack([peak, ratio, price_coef])
    given, given_share, weighted, diag_part = first_panel(firm_chars, 4, tastes, row_values, col_chars)
    diagonal = jnp.sum(diag_part, axis=1)
    for mask in (1, 2):
        diagonal = diagonal + swap(diagonal, "cons", mask)
    room = 32768.0 / (count_products * jnp.maximum(diagonal, 1e-25))

    firm_count, block_size = inverses.shape[0], inverses.shape[1]
    own_inverses = lax.dynamic_slice_in_dim(inverses, core * (firm_count // 2), firm_count // 2, 0)
    firm_ids = lax.dynamic_slice_in_dim(firm_map, core * half, half, 0)
    blocks = firm_count // 4
    chip_sums, share_parts, responses = [], [], []

    def respond(part, chip_sum, other_sum):
        both = chip_sum.astype(jnp.float32) + other_sum.astype(jnp.float32)
        part_ids = firm_ids[part * quarter : (part + 1) * quarter]
        marks = part_ids[:, None] == panel_cols[None, :]
        jacobian = both / (room[None, :] * count_consumers) - jnp.where(marks, diagonal[None, :] / count_consumers, 0.0)
        response = jnp.einsum(
            "fab,fbc->fac",
            own_inverses[part * blocks : (part + 1) * blocks],
            jacobian.reshape(blocks, block_size, cols),
            precision=lax.Precision.HIGHEST,
        ).reshape(quarter, cols)
        responses.append((response, swap(response, "cons", 1)))

    for part in (0, 1):
        if part:
            given, given_share = panel(firm_chars, 2 * part, 4, tastes, row_values, weighted, gate)
        got = swap(given, "cons", 1)
        kept, kept_share = panel(firm_chars, 2 * part + 1, 4, tastes, row_values, weighted, given)
        fitted = (kept + got) * room[None, :]
        chip_sum, gate = lax.optimization_barrier((fitted.astype(jnp.float16), jnp.max(fitted, axis=0, keepdims=True)))
        chip_sums.append((chip_sum, swap(chip_sum, "cons", 2)))
        share_parts.append((given_share, kept_share))

    given_share = jnp.sum(jnp.concatenate([share_parts[0][0], share_parts[1][0]]), axis=1)
    kept_share = jnp.sum(jnp.concatenate([share_parts[0][1], share_parts[1][1]]), axis=1)
    first_half = jnp.where(core == 0, kept_share, given_share)
    second_half = jnp.where(core == 0, given_share, kept_share)
    own_shares = jnp.sum(share_sums(chars, tastes, row_values, gate), axis=1)
    sums = jnp.concatenate([own_shares, first_half, second_half])
    for mask in (1, 2):
        sums = sums + swap(sums, "cons", mask)
    sums = sums / count_consumers
    shares, firm_shares = sums[:products], sums[products:]

    respond(0, *chip_sums[0])
    respond(1, *chip_sums[1])
    mine = [pair[0] for pair in responses]
    theirs = [pair[1] for pair in responses]
    response = jnp.where(core == 0, jnp.concatenate(mine + theirs, axis=0), jnp.concatenate(theirs + mine, axis=0))
    markup = jnp.sum(inverses * firm_shares.reshape(firm_count, 1, block_size), axis=2).reshape(products)
    return (shares, markup, response)


def solution(mesh):
    return jax.shard_map(
        body,
        mesh=mesh,
        in_specs=(
            P("cons", None),
            P("cons"),
            P("prod", None),
            P("prod"),
            P(),
            P("prod"),
            P("prod", None, None),
        ),
        out_specs=(P("prod"), P("prod"), P("prod", None)),
        check_vma=False,
    )
```

```python
import jax
import jax.numpy as jnp
from jax import lax
from jax.experimental import pallas as pl
from jax.experimental.pallas import tpu as pltpu
from jax.sharding import PartitionSpec as P

NT = (((1,), (1,)), ((), ()))
VMEM_BYTES = 24 * 1024 * 1024


def dot_nt(left, right):
    return lax.dot_general(left, right, NT, preferred_element_type=jnp.float32)


def split3(values):
    high = lax.reduce_precision(values, 8, 7)
    middle = lax.reduce_precision(values - high, 8, 7)
    low = lax.reduce_precision(values - high - middle, 8, 7)
    high, middle, low = (piece.astype(jnp.bfloat16) for piece in (high, middle, low))
    return high, middle, low


def beside_ones(tastes):
    ones = lax.broadcasted_iota(jnp.int32, tastes.shape, 1) < 3
    return jnp.concatenate([tastes, jnp.where(ones, 1.0, 0.0).astype(tastes.dtype)], axis=1)


def stats(chars, tastes, gate):
    rows, depth = chars.shape
    consumers = tastes.shape[0]
    block, sub, chunk = 2048, 256, 256
    count = block // sub

    def kernel(chars_ref, tastes_ref, gate_ref, stat_ref, util_ref):
        people = [beside_ones(tastes_ref[k * sub : (k + 1) * sub, :]) for k in range(count)]
        before = None
        for k in range(count + 1):
            peak = jnp.full((8, sub), -jnp.inf, jnp.float32)
            total = jnp.zeros((8, sub), jnp.float32)
            for start in range(0, rows, chunk):
                if k < count:
                    util = dot_nt(chars_ref[start : start + chunk, :], people[k])
                    util_ref[k % 2, start : start + chunk, :] = util
                    peak = jnp.maximum(peak, jnp.max(util.reshape(chunk // 8, 8, sub), axis=0))
                if k > 0:
                    expo = jnp.exp(util_ref[(k - 1) % 2, start : start + chunk, :] - before)
                    total = total + jnp.sum(expo.reshape(chunk // 8, 8, sub), axis=0)
            if k > 0:
                stat_ref[0:1, (k - 1) * sub : k * sub] = before
                stat_ref[1:2, (k - 1) * sub : k * sub] = jnp.sum(total, axis=0, keepdims=True)
            before = jnp.max(peak, axis=0, keepdims=True)

    return pl.pallas_call(
        kernel,
        grid=(consumers // block,),
        in_specs=[
            pl.BlockSpec((rows, depth), lambda i: (0, 0)),
            pl.BlockSpec((block, tastes.shape[1]), lambda i: (i, 0)),
            pl.BlockSpec(memory_space=pl.ANY),
        ],
        out_specs=pl.BlockSpec((2, block), lambda i: (0, i)),
        out_shape=jax.ShapeDtypeStruct((2, consumers), jnp.float32),
        scratch_shapes=[pltpu.VMEM((2, rows, sub), jnp.float32)],
        compiler_params=pltpu.CompilerParams(vmem_limit_bytes=VMEM_BYTES),
        name="stats",
    )(chars, tastes, gate)


def pick_rows(ids_t, chars, tail, stat):
    per_pair, holders = ids_t.shape
    rows, depth = chars.shape
    each = per_pair + 16
    group, pair = 256 // per_pair, 128 // per_pair

    def kernel(ids_ref, chars_ref, tail_ref, stat_ref, out_ref, stat_out_ref):
        stat_out_ref[...] = stat_ref[...]
        lanes = lax.broadcasted_iota(jnp.int32, (per_pair, rows), 1)
        table = chars_ref[...]
        for start in range(0, holders, group):
            span = range(start, start + group)
            marks = [jnp.where(ids_ref[:, q : q + 1] == lanes, 1.0, 0.0).astype(jnp.bfloat16) for q in span]
            picked = jnp.dot(jnp.concatenate(marks, axis=0), table, preferred_element_type=jnp.float32)
            for place, q in enumerate(span):
                if place % pair == 0:
                    beside = picked[place * per_pair : (place + pair) * per_pair, 128:].T[:8, :]
                    block = jnp.concatenate([beside + tail_ref[0:8, :], tail_ref[8:16, :]], axis=0).astype(jnp.bfloat16)
                mine = picked[place * per_pair : (place + 1) * per_pair, :128]
                out_ref[q * each : q * each + per_pair, :] = mine.astype(jnp.bfloat16)
                out_ref[q * each + per_pair : (q + 1) * each, :] = block

    return pl.pallas_call(
        kernel,
        out_shape=[
            jax.ShapeDtypeStruct((each * holders, depth // 2), jnp.bfloat16),
            jax.ShapeDtypeStruct(stat.shape, stat.dtype),
        ],
        compiler_params=pltpu.CompilerParams(vmem_limit_bytes=VMEM_BYTES),
        name="pick_rows",
    )(ids_t, chars, tail, stat)


def place_rows(order, received, beside, holders, stat):
    rows = order.shape[1]
    total, depth = received.shape
    per_pair, each = rows // holders, total // holders
    chunk = 256

    def kernel(order_ref, received_ref, beside_ref, stat_ref, out_ref, stat_out_ref):
        stat_out_ref[...] = stat_ref[...]
        order_row = order_ref[...]
        table = jnp.concatenate([received_ref[q * each : q * each + per_pair, :] for q in range(holders)], axis=0)
        blank = jnp.zeros((120, 128), jnp.float32)
        columns = [
            jnp.concatenate([beside_ref[:, start : start + 128], blank], axis=0).T.astype(jnp.bfloat16)
            for start in range(0, rows, 128)
        ]
        table = jnp.concatenate([table, jnp.concatenate(columns, axis=0)], axis=1)
        for start in range(0, rows, chunk):
            ids = start + lax.broadcasted_iota(jnp.int32, (chunk, rows), 0)
            hot = jnp.where(ids == order_row, 1.0, 0.0).astype(jnp.bfloat16)
            placed = jnp.dot(hot, table, preferred_element_type=jnp.float32)
            out_ref[start : start + chunk, :] = placed.astype(jnp.bfloat16)

    return pl.pallas_call(
        kernel,
        out_shape=[jax.ShapeDtypeStruct((rows, 2 * depth), jnp.bfloat16), jax.ShapeDtypeStruct(stat.shape, stat.dtype)],
        compiler_params=pltpu.CompilerParams(vmem_limit_bytes=VMEM_BYTES),
        name="place_rows",
    )(order, received, beside, stat)


def lane_groups(values):
    total = values[:, 0:128]
    for start in range(128, values.shape[1], 128):
        total = total + values[:, start : start + 128]
    return total


def first_panel(chars, parts, tastes, row_values, col_chars):
    rows, depth = chars.shape[0] // parts, chars.shape[1]
    consumers = tastes.shape[0]
    cols = col_chars.shape[0]
    block, chunk = 1024, 256

    def kernel(chars_ref, tastes_ref, rows_ref, cols_ref, panel_ref, share_ref, weight_ref, diag_ref):
        step = pl.program_id(0)

        @pl.when(step == 0)
        def _():
            panel_ref[...] = jnp.zeros_like(panel_ref)
            share_ref[...] = jnp.zeros_like(share_ref)
            diag_ref[...] = jnp.zeros_like(diag_ref)

        people = beside_ones(tastes_ref[...])
        peak, ratio = rows_ref[0:1, :], rows_ref[1:2, :]
        weighted = rows_ref[2:3, :] * (jnp.exp(dot_nt(cols_ref[...], people) - peak) * ratio)
        diag_ref[...] += lane_groups(weighted)
        weight = weighted.astype(jnp.bfloat16)
        weight_ref[...] = weight
        for start in range(0, rows, chunk):
            scaled = jnp.exp(dot_nt(chars_ref[start : start + chunk, :], people) - peak) * ratio
            share_ref[start : start + chunk, :] += lane_groups(scaled)
            panel_ref[start : start + chunk, :] += dot_nt(scaled.astype(jnp.bfloat16), weight)

        @pl.when(step == pl.num_programs(0) - 1)
        def _():
            total = jnp.sum(diag_ref[...].T, axis=0, keepdims=True)
            panel_ref[rows:, :] = jnp.broadcast_to(total, (8, cols))

    return pl.pallas_call(
        kernel,
        grid=(consumers // block,),
        in_specs=[
            pl.BlockSpec((rows, depth), lambda i: (0, 0)),
            pl.BlockSpec((block, tastes.shape[1]), lambda i: (i, 0)),
            pl.BlockSpec((3, block), lambda i: (0, i)),
            pl.BlockSpec((cols, depth), lambda i: (0, 0)),
        ],
        out_specs=[
            pl.BlockSpec((rows + 8, cols), lambda i: (0, 0)),
            pl.BlockSpec((rows, 128), lambda i: (0, 0)),
            pl.BlockSpec((cols, block), lambda i: (0, i)),
        ],
        scratch_shapes=[pltpu.VMEM((cols, 128), jnp.float32)],
        out_shape=[
            jax.ShapeDtypeStruct((rows + 8, cols), jnp.float32),
            jax.ShapeDtypeStruct((rows, 128), jnp.float32),
            jax.ShapeDtypeStruct((cols, consumers), jnp.bfloat16),
        ],
        compiler_params=pltpu.CompilerParams(vmem_limit_bytes=VMEM_BYTES),
        cost_estimate=pl.CostEstimate(
            flops=2 * rows * consumers * (depth + cols), bytes_accessed=rows * cols * 8, transcendentals=rows * consumers
        ),
        name="first_panel",
    )(chars, tastes, row_values, col_chars)


def panel(chars, part, parts, tastes, row_values, weighted, gate):
    rows, depth = chars.shape[0] // parts, chars.shape[1]
    consumers = tastes.shape[0]
    cols = weighted.shape[0]
    chunk = 256

    def kernel(chars_ref, tastes_ref, rows_ref, weight_ref, gate_ref, panel_ref, share_ref):
        people, weight = beside_ones(tastes_ref[...]), weight_ref[...]
        peak, ratio = rows_ref[0:1, :], rows_ref[1:2, :]
        for start in range(0, rows, chunk):
            scaled = jnp.exp(dot_nt(chars_ref[start : start + chunk, :], people) - peak) * ratio
            share_ref[start : start + chunk, :] = lane_groups(scaled)
            panel_ref[start : start + chunk, :] = dot_nt(scaled.astype(jnp.bfloat16), weight)

    return pl.pallas_call(
        kernel,
        grid=(1,),
        in_specs=[
            pl.BlockSpec((rows, depth), lambda i: (part, 0)),
            pl.BlockSpec(tastes.shape, lambda i: (0, 0)),
            pl.BlockSpec((3, consumers), lambda i: (0, 0)),
            pl.BlockSpec((cols, consumers), lambda i: (0, 0)),
            pl.BlockSpec(memory_space=pl.ANY),
        ],
        out_specs=[
            pl.BlockSpec((rows, cols), lambda i: (0, 0)),
            pl.BlockSpec((rows, 128), lambda i: (0, 0)),
        ],
        out_shape=[
            jax.ShapeDtypeStruct((rows, cols), jnp.float32),
            jax.ShapeDtypeStruct((rows, 128), jnp.float32),
        ],
        compiler_params=pltpu.CompilerParams(vmem_limit_bytes=VMEM_BYTES),
        cost_estimate=pl.CostEstimate(
            flops=2 * rows * consumers * (depth + cols), bytes_accessed=rows * cols * 8, transcendentals=rows * consumers
        ),
        name="panel",
    )(chars, tastes, row_values, weighted, gate)


def share_sums(chars, tastes, row_values, gate):
    rows, depth = chars.shape
    consumers = tastes.shape[0]
    block, chunk = 1024, 256

    def kernel(chars_ref, tastes_ref, rows_ref, gate_ref, share_ref):
        @pl.when(pl.program_id(0) == 0)
        def _():
            share_ref[...] = jnp.zeros_like(share_ref)

        people = beside_ones(tastes_ref[...])
        peak, ratio = rows_ref[0:1, :], rows_ref[1:2, :]
        for start in range(0, rows, chunk):
            scaled = jnp.exp(dot_nt(chars_ref[start : start + chunk, :], people) - peak) * ratio
            share_ref[start : start + chunk, :] += lane_groups(scaled)

    return pl.pallas_call(
        kernel,
        grid=(consumers // block,),
        in_specs=[
            pl.BlockSpec((rows, depth), lambda i: (0, 0)),
            pl.BlockSpec((block, tastes.shape[1]), lambda i: (i, 0)),
            pl.BlockSpec((3, block), lambda i: (0, i)),
            pl.BlockSpec(memory_space=pl.ANY),
        ],
        out_specs=pl.BlockSpec((rows, 128), lambda i: (0, 0)),
        out_shape=jax.ShapeDtypeStruct((rows, 128), jnp.float32),
        compiler_params=pltpu.CompilerParams(vmem_limit_bytes=VMEM_BYTES),
        name="share_sums",
    )(chars, tastes, row_values, gate)


def swap(value, axis, mask):
    size = lax.axis_size(axis)
    return lax.ppermute(value, axis, [(i, i ^ mask) for i in range(size)])


def butterfly_masks(size):
    masks, step = [], 1
    while step < size:
        masks.append(step)
        if step * 2 < size:
            masks.append(step * 3)
        step *= 4
    return masks


def body(tastes, price_coef, characteristics, mean_utility, panel_cols, firm_map, inverses):
    products, depth = characteristics.shape
    consumers = tastes.shape[0]
    cols = panel_cols.shape[0]
    holders = lax.axis_size("prod")
    per_pair = products // holders
    count_products = products * holders
    count_consumers = consumers * lax.axis_size("cons")
    base = lax.axis_index("prod") * products
    core = lax.axis_index("cons") % 2

    pieces = jnp.stack(split3(mean_utility), axis=1)
    chars = jnp.concatenate([characteristics, jnp.pad(pieces, ((0, 0), (0, depth - 3)))], axis=1)

    wanted, order = lax.sort((firm_map, lax.iota(jnp.int32, products)), num_keys=1)
    wanted = (wanted % products).reshape(holders, per_pair)
    digits = jnp.concatenate([wanted // 256, wanted % 256], axis=1).astype(jnp.bfloat16)[:, None, :]
    product_ids = base + lax.iota(jnp.int32, products)
    hits = (panel_cols[:, None] == product_ids[None, :]).astype(jnp.bfloat16)
    col_part = jnp.dot(hits, chars, preferred_element_type=jnp.float32).astype(jnp.bfloat16)
    share_cols = cols // holders
    col_pieces = col_part[:, depth : depth + 3].reshape(holders, share_cols, 3).transpose(0, 2, 1)
    col_pieces = jnp.pad(col_pieces, ((0, 0), (0, 4), (0, depth - share_cols)))
    message = jnp.concatenate([col_part[:, :depth].reshape(holders, share_cols, depth), digits, col_pieces], axis=1)
    first = lax.all_to_all(message, "prod", split_axis=0, concat_axis=0, tiled=True)

    stat = stats(chars, tastes, message)

    asked = first[:, share_cols, :].astype(jnp.int32)
    ids = asked[:, :per_pair] * 256 + asked[:, per_pair:]
    summed = jnp.sum(first.astype(jnp.float32), axis=0)
    zeros = jnp.zeros((3, depth), jnp.float32)
    tail = jnp.concatenate([zeros, summed[share_cols + 1 : share_cols + 4], zeros[:2], summed[:share_cols]], axis=0)
    each = per_pair + 16
    sent, stat = pick_rows(ids.T, chars, tail, stat)
    second = lax.all_to_all(sent.reshape(holders, each, depth), "prod", split_axis=0, concat_axis=0, tiled=True)
    col_pieces = second[:, per_pair + 3 : per_pair + 6, :share_cols].transpose(0, 2, 1).reshape(cols, 3)
    col_chars = second[:, per_pair + 8 :, :].reshape(cols, depth)
    col_chars = jnp.concatenate([col_chars, jnp.pad(col_pieces, ((0, 0), (0, depth - 3)))], axis=1)
    mean_rows = second[:, per_pair : per_pair + 8, :].astype(jnp.float32)
    odd = lax.axis_index("prod") % 2 == 1
    mean_rows = jnp.where(odd, mean_rows[:, :, per_pair:], mean_rows[:, :, :per_pair])
    mean_rows = jnp.pad(mean_rows[:, :3], ((0, 0), (0, 5), (0, 0))).transpose(1, 0, 2).reshape(8, products)
    half = products // 2
    place = (order // half == core).astype(jnp.int32) * half + order % half

    def join(stat, masks):
        for mask in masks:
            other = swap(stat, "prod", mask)
            joint = jnp.maximum(stat[0], other[0])
            total = stat[1] * jnp.exp(stat[0] - joint) + other[1] * jnp.exp(other[0] - joint)
            stat = jnp.stack([joint, total])
        return stat

    masks = butterfly_masks(holders)
    stat = lax.cond(panel_cols[0] >= 0, lambda value: join(value, masks[:3]), lambda value: value, stat)
    firm_chars, stat = place_rows(
        place.reshape(1, products), second.reshape(holders * each, depth), mean_rows, holders, stat
    )
    stat = join(stat, masks[3:])
    peak = jnp.maximum(stat[0], 0.0)
    denom = jnp.exp(-peak) + stat[1] * jnp.exp(stat[0] - peak)
    ratio = count_products / denom

    row_values = jnp.stack([peak, ratio, price_coef])
    given, given_share, weighted = first_panel(firm_chars, 2, tastes, row_values, col_chars)
    got = swap(given, "cons", 1)
    kept, kept_share = panel(firm_chars, 1, 2, tastes, row_values, weighted, given)
    diagonal = given[half] + got[half]
    room = 32768.0 / (count_products * jnp.maximum(diagonal, 1e-25))
    fitted = (kept + got[:half]) * room[None, :]
    chip_sum, gate = lax.optimization_barrier((fitted.astype(jnp.float16), jnp.max(fitted, axis=0, keepdims=True)))
    other_sum = swap(chip_sum, "cons", 2)
    other_diagonal = swap(diagonal, "cons", 2)

    own_shares = jnp.sum(share_sums(chars, tastes, row_values, gate), axis=1)
    given_share, kept_share = jnp.sum(given_share, axis=1), jnp.sum(kept_share, axis=1)
    first_half = jnp.where(core == 0, kept_share, given_share)
    second_half = jnp.where(core == 0, given_share, kept_share)
    sums = jnp.concatenate([own_shares, first_half, second_half])
    for mask in (1, 2):
        sums = sums + swap(sums, "cons", mask)
    sums = sums / count_consumers
    shares, firm_shares = sums[:products], sums[products:]

    firm_count, block_size = inverses.shape[0], inverses.shape[1]
    own_inverses = lax.dynamic_slice_in_dim(inverses, core * (firm_count // 2), firm_count // 2, 0)
    firm_ids = lax.dynamic_slice_in_dim(firm_map, core * half, half, 0)
    other_room = 32768.0 / (count_products * jnp.maximum(other_diagonal, 1e-25))
    unfit, other_unfit = 1.0 / (room * count_consumers), 1.0 / (other_room * count_consumers)
    unfit = jnp.where(own_shares[0] >= 0.0, unfit, 0.0)
    cross = chip_sum.astype(jnp.float32) * unfit[None, :] + other_sum.astype(jnp.float32) * other_unfit[None, :]
    diagonal = (diagonal + other_diagonal) / count_consumers
    jacobian = cross - jnp.where(firm_ids[:, None] == panel_cols[None, :], diagonal[None, :], 0.0)
    mine = jnp.einsum(
        "fab,fbc->fac",
        own_inverses,
        jacobian.reshape(firm_count // 2, block_size, cols),
        precision=lax.Precision.HIGHEST,
    ).reshape(half, cols)
    theirs = swap(mine, "cons", 1)
    response = jnp.where(core == 0, jnp.concatenate([mine, theirs]), jnp.concatenate([theirs, mine]))
    markup = jnp.sum(inverses * firm_shares.reshape(firm_count, 1, block_size), axis=2).reshape(products)
    return (shares, markup, response)


def solution(mesh):
    return jax.shard_map(
        body,
        mesh=mesh,
        in_specs=(
            P("cons", None),
            P("cons"),
            P("prod", None),
            P("prod"),
            P(),
            P("prod"),
            P("prod", None, None),
        ),
        out_specs=(P("prod"), P("prod"), P("prod", None)),
        check_vma=False,
    )
```

```python
import jax
import jax.numpy as jnp
from jax import lax
from jax.experimental import pallas as pl
from jax.experimental.pallas import tpu as pltpu
from jax.sharding import PartitionSpec as P

NT = (((1,), (1,)), ((), ()))
VMEM_BYTES = 24 * 1024 * 1024


def dot_nt(left, right):
    return lax.dot_general(left, right, NT, preferred_element_type=jnp.float32)


def split3(values):
    high = lax.reduce_precision(values, 8, 7)
    middle = lax.reduce_precision(values - high, 8, 7)
    low = lax.reduce_precision(values - high - middle, 8, 7)
    high, middle, low = (piece.astype(jnp.bfloat16) for piece in (high, middle, low))
    return high, middle, low


def beside_ones(tastes):
    ones = lax.broadcasted_iota(jnp.int32, tastes.shape, 1) < 3
    return jnp.concatenate([tastes, jnp.where(ones, 1.0, 0.0).astype(tastes.dtype)], axis=1)


def stats(chars, tastes, gate):
    rows, depth = chars.shape
    consumers = tastes.shape[0]
    block, sub, chunk = 2048, 256, 256
    count = block // sub

    def kernel(chars_ref, tastes_ref, gate_ref, stat_ref, util_ref):
        people = [beside_ones(tastes_ref[k * sub : (k + 1) * sub, :]) for k in range(count)]
        before = None
        for k in range(count + 1):
            peak = jnp.full((8, sub), -jnp.inf, jnp.float32)
            total = jnp.zeros((8, sub), jnp.float32)
            for start in range(0, rows, chunk):
                if k < count:
                    util = dot_nt(chars_ref[start : start + chunk, :], people[k])
                    util_ref[k % 2, start : start + chunk, :] = util
                    peak = jnp.maximum(peak, jnp.max(util.reshape(chunk // 8, 8, sub), axis=0))
                if k > 0:
                    expo = jnp.exp(util_ref[(k - 1) % 2, start : start + chunk, :] - before)
                    total = total + jnp.sum(expo.reshape(chunk // 8, 8, sub), axis=0)
            if k > 0:
                stat_ref[0:1, (k - 1) * sub : k * sub] = before
                stat_ref[1:2, (k - 1) * sub : k * sub] = jnp.sum(total, axis=0, keepdims=True)
            before = jnp.max(peak, axis=0, keepdims=True)

    return pl.pallas_call(
        kernel,
        grid=(consumers // block,),
        in_specs=[
            pl.BlockSpec((rows, depth), lambda i: (0, 0)),
            pl.BlockSpec((block, tastes.shape[1]), lambda i: (i, 0)),
            pl.BlockSpec(memory_space=pl.ANY),
        ],
        out_specs=pl.BlockSpec((2, block), lambda i: (0, i)),
        out_shape=jax.ShapeDtypeStruct((2, consumers), jnp.float32),
        scratch_shapes=[pltpu.VMEM((2, rows, sub), jnp.float32)],
        compiler_params=pltpu.CompilerParams(vmem_limit_bytes=VMEM_BYTES),
        name="stats",
    )(chars, tastes, gate)


def pick_rows(ids_t, chars, tail, stat):
    per_pair, holders = ids_t.shape
    rows, depth = chars.shape
    each = per_pair + 16
    group, pair = 256 // per_pair, 128 // per_pair

    def kernel(ids_ref, chars_ref, tail_ref, stat_ref, out_ref, stat_out_ref):
        stat_out_ref[...] = stat_ref[...]
        lanes = lax.broadcasted_iota(jnp.int32, (per_pair, rows), 1)
        table = chars_ref[...]
        for start in range(0, holders, group):
            span = range(start, start + group)
            marks = [jnp.where(ids_ref[:, q : q + 1] == lanes, 1.0, 0.0).astype(jnp.bfloat16) for q in span]
            picked = jnp.dot(jnp.concatenate(marks, axis=0), table, preferred_element_type=jnp.float32)
            for place, q in enumerate(span):
                if place % pair == 0:
                    beside = picked[place * per_pair : (place + pair) * per_pair, 128:].T[:8, :]
                    block = jnp.concatenate([beside + tail_ref[0:8, :], tail_ref[8:16, :]], axis=0).astype(jnp.bfloat16)
                mine = picked[place * per_pair : (place + 1) * per_pair, :128]
                out_ref[q * each : q * each + per_pair, :] = mine.astype(jnp.bfloat16)
                out_ref[q * each + per_pair : (q + 1) * each, :] = block

    return pl.pallas_call(
        kernel,
        out_shape=[
            jax.ShapeDtypeStruct((each * holders, depth // 2), jnp.bfloat16),
            jax.ShapeDtypeStruct(stat.shape, stat.dtype),
        ],
        compiler_params=pltpu.CompilerParams(vmem_limit_bytes=VMEM_BYTES),
        name="pick_rows",
    )(ids_t, chars, tail, stat)


def place_rows(order, received, beside, holders, gate):
    rows = order.shape[1]
    total, depth = received.shape
    per_pair, each = rows // holders, total // holders
    chunk = 256

    def kernel(order_ref, received_ref, beside_ref, gate_ref, out_ref):
        order_row = order_ref[...]
        table = jnp.concatenate([received_ref[q * each : q * each + per_pair, :] for q in range(holders)], axis=0)
        blank = jnp.zeros((120, 128), jnp.float32)
        columns = [
            jnp.concatenate([beside_ref[:, start : start + 128], blank], axis=0).T.astype(jnp.bfloat16)
            for start in range(0, rows, 128)
        ]
        table = jnp.concatenate([table, jnp.concatenate(columns, axis=0)], axis=1)
        for start in range(0, rows, chunk):
            ids = start + lax.broadcasted_iota(jnp.int32, (chunk, rows), 0)
            hot = jnp.where(ids == order_row, 1.0, 0.0).astype(jnp.bfloat16)
            placed = jnp.dot(hot, table, preferred_element_type=jnp.float32)
            out_ref[start : start + chunk, :] = placed.astype(jnp.bfloat16)

    return pl.pallas_call(
        kernel,
        in_specs=[pl.BlockSpec(memory_space=pltpu.VMEM)] * 3 + [pl.BlockSpec(memory_space=pl.ANY)],
        out_shape=jax.ShapeDtypeStruct((rows, 2 * depth), jnp.bfloat16),
        compiler_params=pltpu.CompilerParams(vmem_limit_bytes=VMEM_BYTES),
        name="place_rows",
    )(order, received, beside, gate)


def lane_groups(values):
    total = values[:, 0:128]
    for start in range(128, values.shape[1], 128):
        total = total + values[:, start : start + 128]
    return total


def first_panel(chars, parts, tastes, row_values, col_chars):
    rows, depth = chars.shape[0] // parts, chars.shape[1]
    consumers = tastes.shape[0]
    cols = col_chars.shape[0]
    block, chunk = 1024, 256

    def kernel(chars_ref, tastes_ref, rows_ref, cols_ref, panel_ref, share_ref, weight_ref, diag_ref):
        step = pl.program_id(0)

        @pl.when(step == 0)
        def _():
            panel_ref[...] = jnp.zeros_like(panel_ref)
            share_ref[...] = jnp.zeros_like(share_ref)
            diag_ref[...] = jnp.zeros_like(diag_ref)

        people = beside_ones(tastes_ref[...])
        peak, ratio = rows_ref[0:1, :], rows_ref[1:2, :]
        weighted = rows_ref[2:3, :] * (jnp.exp(dot_nt(cols_ref[...], people) - peak) * ratio)
        diag_ref[...] += lane_groups(weighted)
        weight = weighted.astype(jnp.bfloat16)
        weight_ref[...] = weight
        for start in range(0, rows, chunk):
            scaled = jnp.exp(dot_nt(chars_ref[start : start + chunk, :], people) - peak) * ratio
            share_ref[start : start + chunk, :] += lane_groups(scaled)
            panel_ref[start : start + chunk, :] += dot_nt(scaled.astype(jnp.bfloat16), weight)

        @pl.when(step == pl.num_programs(0) - 1)
        def _():
            total = jnp.sum(diag_ref[...].T, axis=0, keepdims=True)
            panel_ref[rows:, :] = jnp.broadcast_to(total, (8, cols))

    return pl.pallas_call(
        kernel,
        grid=(consumers // block,),
        in_specs=[
            pl.BlockSpec((rows, depth), lambda i: (0, 0)),
            pl.BlockSpec((block, tastes.shape[1]), lambda i: (i, 0)),
            pl.BlockSpec((3, block), lambda i: (0, i)),
            pl.BlockSpec((cols, depth), lambda i: (0, 0)),
        ],
        out_specs=[
            pl.BlockSpec((rows + 8, cols), lambda i: (0, 0)),
            pl.BlockSpec((rows, 128), lambda i: (0, 0)),
            pl.BlockSpec((cols, block), lambda i: (0, i)),
        ],
        scratch_shapes=[pltpu.VMEM((cols, 128), jnp.float32)],
        out_shape=[
            jax.ShapeDtypeStruct((rows + 8, cols), jnp.float32),
            jax.ShapeDtypeStruct((rows, 128), jnp.float32),
            jax.ShapeDtypeStruct((cols, consumers), jnp.bfloat16),
        ],
        compiler_params=pltpu.CompilerParams(vmem_limit_bytes=VMEM_BYTES),
        cost_estimate=pl.CostEstimate(
            flops=2 * rows * consumers * (depth + cols), bytes_accessed=rows * cols * 8, transcendentals=rows * consumers
        ),
        name="first_panel",
    )(chars, tastes, row_values, col_chars)


def panel(chars, part, parts, tastes, row_values, weighted, gate):
    rows, depth = chars.shape[0] // parts, chars.shape[1]
    consumers = tastes.shape[0]
    cols = weighted.shape[0]
    chunk = 256

    def kernel(chars_ref, tastes_ref, rows_ref, weight_ref, gate_ref, panel_ref, share_ref):
        people, weight = beside_ones(tastes_ref[...]), weight_ref[...]
        peak, ratio = rows_ref[0:1, :], rows_ref[1:2, :]
        for start in range(0, rows, chunk):
            scaled = jnp.exp(dot_nt(chars_ref[start : start + chunk, :], people) - peak) * ratio
            share_ref[start : start + chunk, :] = lane_groups(scaled)
            panel_ref[start : start + chunk, :] = dot_nt(scaled.astype(jnp.bfloat16), weight)

    return pl.pallas_call(
        kernel,
        grid=(1,),
        in_specs=[
            pl.BlockSpec((rows, depth), lambda i: (part, 0)),
            pl.BlockSpec(tastes.shape, lambda i: (0, 0)),
            pl.BlockSpec((3, consumers), lambda i: (0, 0)),
            pl.BlockSpec((cols, consumers), lambda i: (0, 0)),
            pl.BlockSpec(memory_space=pl.ANY),
        ],
        out_specs=[
            pl.BlockSpec((rows, cols), lambda i: (0, 0)),
            pl.BlockSpec((rows, 128), lambda i: (0, 0)),
        ],
        out_shape=[
            jax.ShapeDtypeStruct((rows, cols), jnp.float32),
            jax.ShapeDtypeStruct((rows, 128), jnp.float32),
        ],
        compiler_params=pltpu.CompilerParams(vmem_limit_bytes=VMEM_BYTES),
        cost_estimate=pl.CostEstimate(
            flops=2 * rows * consumers * (depth + cols), bytes_accessed=rows * cols * 8, transcendentals=rows * consumers
        ),
        name="panel",
    )(chars, tastes, row_values, weighted, gate)


def share_sums(chars, tastes, row_values, gate):
    rows, depth = chars.shape
    consumers = tastes.shape[0]
    block, chunk = 1024, 256

    def kernel(chars_ref, tastes_ref, rows_ref, gate_ref, share_ref):
        @pl.when(pl.program_id(0) == 0)
        def _():
            share_ref[...] = jnp.zeros_like(share_ref)

        people = beside_ones(tastes_ref[...])
        peak, ratio = rows_ref[0:1, :], rows_ref[1:2, :]
        for start in range(0, rows, chunk):
            scaled = jnp.exp(dot_nt(chars_ref[start : start + chunk, :], people) - peak) * ratio
            share_ref[start : start + chunk, :] += lane_groups(scaled)

    return pl.pallas_call(
        kernel,
        grid=(consumers // block,),
        in_specs=[
            pl.BlockSpec((rows, depth), lambda i: (0, 0)),
            pl.BlockSpec((block, tastes.shape[1]), lambda i: (i, 0)),
            pl.BlockSpec((3, block), lambda i: (0, i)),
            pl.BlockSpec(memory_space=pl.ANY),
        ],
        out_specs=pl.BlockSpec((rows, 128), lambda i: (0, 0)),
        out_shape=jax.ShapeDtypeStruct((rows, 128), jnp.float32),
        compiler_params=pltpu.CompilerParams(vmem_limit_bytes=VMEM_BYTES),
        name="share_sums",
    )(chars, tastes, row_values, gate)


def swap(value, axis, mask):
    size = lax.axis_size(axis)
    return lax.ppermute(value, axis, [(i, i ^ mask) for i in range(size)])


def butterfly_masks(size):
    masks, step = [], 1
    while step < size:
        masks.append(step)
        if step * 2 < size:
            masks.append(step * 3)
        step *= 4
    return masks


def body(tastes, price_coef, characteristics, mean_utility, panel_cols, firm_map, inverses):
    products, depth = characteristics.shape
    consumers = tastes.shape[0]
    cols = panel_cols.shape[0]
    holders = lax.axis_size("prod")
    per_pair = products // holders
    count_products = products * holders
    count_consumers = consumers * lax.axis_size("cons")
    base = lax.axis_index("prod") * products
    core = lax.axis_index("cons") % 2

    pieces = jnp.stack(split3(mean_utility), axis=1)
    chars = jnp.concatenate([characteristics, jnp.pad(pieces, ((0, 0), (0, depth - 3)))], axis=1)

    wanted, order = lax.sort((firm_map, lax.iota(jnp.int32, products)), num_keys=1)
    wanted = (wanted % products).reshape(holders, per_pair)
    digits = jnp.concatenate([wanted // 256, wanted % 256], axis=1).astype(jnp.bfloat16)[:, None, :]
    product_ids = base + lax.iota(jnp.int32, products)
    hits = (panel_cols[:, None] == product_ids[None, :]).astype(jnp.bfloat16)
    col_part = jnp.dot(hits, chars, preferred_element_type=jnp.float32).astype(jnp.bfloat16)
    share_cols = cols // holders
    col_pieces = col_part[:, depth : depth + 3].reshape(holders, share_cols, 3).transpose(0, 2, 1)
    col_pieces = jnp.pad(col_pieces, ((0, 0), (0, 4), (0, depth - share_cols)))
    message = jnp.concatenate([col_part[:, :depth].reshape(holders, share_cols, depth), digits, col_pieces], axis=1)
    first = lax.all_to_all(message, "prod", split_axis=0, concat_axis=0, tiled=True)

    stat = stats(chars, tastes, message)

    asked = first[:, share_cols, :].astype(jnp.int32)
    ids = asked[:, :per_pair] * 256 + asked[:, per_pair:]
    summed = jnp.sum(first.astype(jnp.float32), axis=0)
    zeros = jnp.zeros((3, depth), jnp.float32)
    tail = jnp.concatenate([zeros, summed[share_cols + 1 : share_cols + 4], zeros[:2], summed[:share_cols]], axis=0)
    each = per_pair + 16
    sent, stat = pick_rows(ids.T, chars, tail, stat)
    second = lax.all_to_all(sent.reshape(holders, each, depth), "prod", split_axis=0, concat_axis=0, tiled=True)
    col_pieces = second[:, per_pair + 3 : per_pair + 6, :share_cols].transpose(0, 2, 1).reshape(cols, 3)
    col_chars = second[:, per_pair + 8 :, :].reshape(cols, depth)
    col_chars = jnp.concatenate([col_chars, jnp.pad(col_pieces, ((0, 0), (0, depth - 3)))], axis=1)
    mean_rows = second[:, per_pair : per_pair + 8, :].astype(jnp.float32)
    odd = lax.axis_index("prod") % 2 == 1
    mean_rows = jnp.where(odd, mean_rows[:, :, per_pair:], mean_rows[:, :, :per_pair])
    mean_rows = jnp.pad(mean_rows[:, :3], ((0, 0), (0, 5), (0, 0))).transpose(1, 0, 2).reshape(8, products)
    half = products // 2
    place = (order // half == core).astype(jnp.int32) * half + order % half

    def join(stat, masks):
        for mask in masks:
            other = swap(stat, "prod", mask)
            joint = jnp.maximum(stat[0], other[0])
            total = stat[1] * jnp.exp(stat[0] - joint) + other[1] * jnp.exp(other[0] - joint)
            stat = jnp.stack([joint, total])
        return stat

    masks = butterfly_masks(holders)
    stat = lax.cond(panel_cols[0] >= 0, lambda value: join(value, masks), lambda value: value, stat)
    firm_chars = place_rows(
        place.reshape(1, products), second.reshape(holders * each, depth), mean_rows, holders, stat
    )
    peak = jnp.maximum(stat[0], 0.0)
    denom = jnp.exp(-peak) + stat[1] * jnp.exp(stat[0] - peak)
    ratio = count_products / denom

    row_values = jnp.stack([peak, ratio, price_coef])
    given, given_share, weighted = first_panel(firm_chars, 2, tastes, row_values, col_chars)
    got = swap(given, "cons", 1)
    kept, kept_share = panel(firm_chars, 1, 2, tastes, row_values, weighted, given)
    diagonal = given[half] + got[half]
    room = 32768.0 / (count_products * jnp.maximum(diagonal, 1e-25))
    fitted = (kept + got[:half]) * room[None, :]
    chip_sum, gate = lax.optimization_barrier((fitted.astype(jnp.float16), jnp.max(fitted, axis=0, keepdims=True)))
    other_sum = swap(chip_sum, "cons", 2)

    given_share, kept_share = jnp.sum(given_share, axis=1), jnp.sum(kept_share, axis=1)
    first_half = jnp.where(core == 0, kept_share, given_share)
    second_half = jnp.where(core == 0, given_share, kept_share)

    def own_and_exchange(gate, others):
        own_shares = jnp.sum(share_sums(chars, tastes, row_values, gate), axis=1)
        sums = jnp.concatenate([own_shares, others])
        sums = sums + swap(sums, "cons", 1)
        return sums, swap(sums, "cons", 2)

    sums, other_sums = lax.cond(
        panel_cols[1] >= 0,
        own_and_exchange,
        lambda gate, others: (jnp.zeros(products + others.shape[0], jnp.float32),) * 2,
        gate,
        jnp.concatenate([first_half, second_half, given[half]]),
    )
    other_diagonal = other_sums[2 * products :]
    sums = (sums + other_sums) / count_consumers
    shares, firm_shares = sums[:products], sums[products : 2 * products]

    firm_count, block_size = inverses.shape[0], inverses.shape[1]
    own_inverses = lax.dynamic_slice_in_dim(inverses, core * (firm_count // 2), firm_count // 2, 0)
    firm_ids = lax.dynamic_slice_in_dim(firm_map, core * half, half, 0)
    other_room = 32768.0 / (count_products * jnp.maximum(other_diagonal, 1e-25))
    unfit, other_unfit = 1.0 / (room * count_consumers), 1.0 / (other_room * count_consumers)
    cross = chip_sum.astype(jnp.float32) * unfit[None, :] + other_sum.astype(jnp.float32) * other_unfit[None, :]
    diagonal = (diagonal + other_diagonal) / count_consumers
    jacobian = cross - jnp.where(firm_ids[:, None] == panel_cols[None, :], diagonal[None, :], 0.0)
    mine = jnp.einsum(
        "fab,fbc->fac",
        own_inverses,
        jacobian.reshape(firm_count // 2, block_size, cols),
        precision=lax.Precision.HIGHEST,
    ).reshape(half, cols)
    theirs = swap(mine, "cons", 1)
    response = jnp.where(core == 0, jnp.concatenate([mine, theirs]), jnp.concatenate([theirs, mine]))
    markup = jnp.sum(inverses * firm_shares.reshape(firm_count, 1, block_size), axis=2).reshape(products)
    return (shares, markup, response)


def solution(mesh):
    return jax.shard_map(
        body,
        mesh=mesh,
        in_specs=(
            P("cons", None),
            P("cons"),
            P("prod", None),
            P("prod"),
            P(),
            P("prod"),
            P("prod", None, None),
        ),
        out_specs=(P("prod"), P("prod"), P("prod", None)),
        check_vma=False,
    )
```

```python
import jax
import jax.numpy as jnp
from jax import lax
from jax.experimental import pallas as pl
from jax.experimental.pallas import tpu as pltpu
from jax.sharding import PartitionSpec as P

NT = (((1,), (1,)), ((), ()))
VMEM_BYTES = 24 * 1024 * 1024


def dot_nt(left, right):
    return lax.dot_general(left, right, NT, preferred_element_type=jnp.float32)


def split3(values):
    high = lax.reduce_precision(values, 8, 7)
    middle = lax.reduce_precision(values - high, 8, 7)
    low = lax.reduce_precision(values - high - middle, 8, 7)
    high, middle, low = (piece.astype(jnp.bfloat16) for piece in (high, middle, low))
    return high, middle, low


def beside_ones(tastes):
    ones = lax.broadcasted_iota(jnp.int32, tastes.shape, 1) < 3
    return jnp.concatenate([tastes, jnp.where(ones, 1.0, 0.0).astype(tastes.dtype)], axis=1)


def stats(chars, tastes, gate):
    rows, depth = chars.shape
    consumers = tastes.shape[0]
    block, sub, chunk = 2048, 256, 256
    count = block // sub

    def kernel(chars_ref, tastes_ref, gate_ref, stat_ref, util_ref):
        people = [beside_ones(tastes_ref[k * sub : (k + 1) * sub, :]) for k in range(count)]
        before = None
        for k in range(count + 1):
            peak = jnp.full((8, sub), -jnp.inf, jnp.float32)
            total = jnp.zeros((8, sub), jnp.float32)
            for start in range(0, rows, chunk):
                if k < count:
                    util = dot_nt(chars_ref[start : start + chunk, :], people[k])
                    util_ref[k % 2, start : start + chunk, :] = util
                    peak = jnp.maximum(peak, jnp.max(util.reshape(chunk // 8, 8, sub), axis=0))
                if k > 0:
                    expo = jnp.exp(util_ref[(k - 1) % 2, start : start + chunk, :] - before)
                    total = total + jnp.sum(expo.reshape(chunk // 8, 8, sub), axis=0)
            if k > 0:
                stat_ref[0:1, (k - 1) * sub : k * sub] = before
                stat_ref[1:2, (k - 1) * sub : k * sub] = jnp.sum(total, axis=0, keepdims=True)
            before = jnp.max(peak, axis=0, keepdims=True)

    return pl.pallas_call(
        kernel,
        grid=(consumers // block,),
        in_specs=[
            pl.BlockSpec((rows, depth), lambda i: (0, 0)),
            pl.BlockSpec((block, tastes.shape[1]), lambda i: (i, 0)),
            pl.BlockSpec(memory_space=pl.ANY),
        ],
        out_specs=pl.BlockSpec((2, block), lambda i: (0, i)),
        out_shape=jax.ShapeDtypeStruct((2, consumers), jnp.float32),
        scratch_shapes=[pltpu.VMEM((2, rows, sub), jnp.float32)],
        compiler_params=pltpu.CompilerParams(vmem_limit_bytes=VMEM_BYTES),
        name="stats",
    )(chars, tastes, gate)


def pick_rows(ids_t, chars, tail, stat):
    per_pair, holders = ids_t.shape
    rows, depth = chars.shape
    each = per_pair + 16
    group, pair = 256 // per_pair, 128 // per_pair

    def kernel(ids_ref, chars_ref, tail_ref, stat_ref, out_ref, stat_out_ref):
        stat_out_ref[...] = stat_ref[...]
        lanes = lax.broadcasted_iota(jnp.int32, (per_pair, rows), 1)
        table = chars_ref[...]
        for start in range(0, holders, group):
            span = range(start, start + group)
            marks = [jnp.where(ids_ref[:, q : q + 1] == lanes, 1.0, 0.0).astype(jnp.bfloat16) for q in span]
            picked = jnp.dot(jnp.concatenate(marks, axis=0), table, preferred_element_type=jnp.float32)
            for place, q in enumerate(span):
                if place % pair == 0:
                    beside = picked[place * per_pair : (place + pair) * per_pair, 128:].T[:8, :]
                    block = jnp.concatenate([beside + tail_ref[0:8, :], tail_ref[8:16, :]], axis=0).astype(jnp.bfloat16)
                mine = picked[place * per_pair : (place + 1) * per_pair, :128]
                out_ref[q * each : q * each + per_pair, :] = mine.astype(jnp.bfloat16)
                out_ref[q * each + per_pair : (q + 1) * each, :] = block

    return pl.pallas_call(
        kernel,
        out_shape=[
            jax.ShapeDtypeStruct((each * holders, depth // 2), jnp.bfloat16),
            jax.ShapeDtypeStruct(stat.shape, stat.dtype),
        ],
        compiler_params=pltpu.CompilerParams(vmem_limit_bytes=VMEM_BYTES),
        name="pick_rows",
    )(ids_t, chars, tail, stat)


def place_rows(order, received, beside, holders, gate):
    rows = order.shape[1]
    total, depth = received.shape
    per_pair, each = rows // holders, total // holders
    chunk = 256

    def kernel(order_ref, received_ref, beside_ref, gate_ref, out_ref):
        order_row = order_ref[...]
        table = jnp.concatenate([received_ref[q * each : q * each + per_pair, :] for q in range(holders)], axis=0)
        blank = jnp.zeros((120, 128), jnp.float32)
        columns = [
            jnp.concatenate([beside_ref[:, start : start + 128], blank], axis=0).T.astype(jnp.bfloat16)
            for start in range(0, rows, 128)
        ]
        table = jnp.concatenate([table, jnp.concatenate(columns, axis=0)], axis=1)
        for start in range(0, rows, chunk):
            ids = start + lax.broadcasted_iota(jnp.int32, (chunk, rows), 0)
            hot = jnp.where(ids == order_row, 1.0, 0.0).astype(jnp.bfloat16)
            placed = jnp.dot(hot, table, preferred_element_type=jnp.float32)
            out_ref[start : start + chunk, :] = placed.astype(jnp.bfloat16)

    return pl.pallas_call(
        kernel,
        in_specs=[pl.BlockSpec(memory_space=pltpu.VMEM)] * 3 + [pl.BlockSpec(memory_space=pl.ANY)],
        out_shape=jax.ShapeDtypeStruct((rows, 2 * depth), jnp.bfloat16),
        compiler_params=pltpu.CompilerParams(vmem_limit_bytes=VMEM_BYTES),
        name="place_rows",
    )(order, received, beside, gate)


def lane_groups(values):
    total = values[:, 0:128]
    for start in range(128, values.shape[1], 128):
        total = total + values[:, start : start + 128]
    return total


def first_panel(chars, parts, tastes, row_values, col_chars):
    rows, depth = chars.shape[0] // parts, chars.shape[1]
    consumers = tastes.shape[0]
    cols = col_chars.shape[0]
    block, chunk = 1024, 256

    def kernel(chars_ref, tastes_ref, rows_ref, cols_ref, panel_ref, share_ref, weight_ref, diag_ref):
        step = pl.program_id(0)

        @pl.when(step == 0)
        def _():
            panel_ref[...] = jnp.zeros_like(panel_ref)
            share_ref[...] = jnp.zeros_like(share_ref)
            diag_ref[...] = jnp.zeros_like(diag_ref)

        people = beside_ones(tastes_ref[...])
        peak, ratio = rows_ref[0:1, :], rows_ref[1:2, :]
        weighted = rows_ref[2:3, :] * (jnp.exp(dot_nt(cols_ref[...], people) - peak) * ratio)
        diag_ref[...] += lane_groups(weighted)
        weight = weighted.astype(jnp.bfloat16)
        weight_ref[...] = weight
        for start in range(0, rows, chunk):
            scaled = jnp.exp(dot_nt(chars_ref[start : start + chunk, :], people) - peak) * ratio
            share_ref[start : start + chunk, :] += lane_groups(scaled)
            panel_ref[start : start + chunk, :] += dot_nt(scaled.astype(jnp.bfloat16), weight)

        @pl.when(step == pl.num_programs(0) - 1)
        def _():
            total = jnp.sum(diag_ref[...].T, axis=0, keepdims=True)
            panel_ref[rows:, :] = jnp.broadcast_to(total, (8, cols))

    return pl.pallas_call(
        kernel,
        grid=(consumers // block,),
        in_specs=[
            pl.BlockSpec((rows, depth), lambda i: (0, 0)),
            pl.BlockSpec((block, tastes.shape[1]), lambda i: (i, 0)),
            pl.BlockSpec((3, block), lambda i: (0, i)),
            pl.BlockSpec((cols, depth), lambda i: (0, 0)),
        ],
        out_specs=[
            pl.BlockSpec((rows + 8, cols), lambda i: (0, 0)),
            pl.BlockSpec((rows, 128), lambda i: (0, 0)),
            pl.BlockSpec((cols, block), lambda i: (0, i)),
        ],
        scratch_shapes=[pltpu.VMEM((cols, 128), jnp.float32)],
        out_shape=[
            jax.ShapeDtypeStruct((rows + 8, cols), jnp.float32),
            jax.ShapeDtypeStruct((rows, 128), jnp.float32),
            jax.ShapeDtypeStruct((cols, consumers), jnp.bfloat16),
        ],
        compiler_params=pltpu.CompilerParams(vmem_limit_bytes=VMEM_BYTES),
        cost_estimate=pl.CostEstimate(
            flops=2 * rows * consumers * (depth + cols), bytes_accessed=rows * cols * 8, transcendentals=rows * consumers
        ),
        name="first_panel",
    )(chars, tastes, row_values, col_chars)


def panel(chars, part, parts, tastes, row_values, weighted, gate):
    rows, depth = chars.shape[0] // parts, chars.shape[1]
    consumers = tastes.shape[0]
    cols = weighted.shape[0]
    chunk = 256

    def kernel(chars_ref, tastes_ref, rows_ref, weight_ref, gate_ref, panel_ref, share_ref):
        people, weight = beside_ones(tastes_ref[...]), weight_ref[...]
        peak, ratio = rows_ref[0:1, :], rows_ref[1:2, :]
        for start in range(0, rows, chunk):
            scaled = jnp.exp(dot_nt(chars_ref[start : start + chunk, :], people) - peak) * ratio
            share_ref[start : start + chunk, :] = lane_groups(scaled)
            panel_ref[start : start + chunk, :] = dot_nt(scaled.astype(jnp.bfloat16), weight)

    return pl.pallas_call(
        kernel,
        grid=(1,),
        in_specs=[
            pl.BlockSpec((rows, depth), lambda i: (part, 0)),
            pl.BlockSpec(tastes.shape, lambda i: (0, 0)),
            pl.BlockSpec((3, consumers), lambda i: (0, 0)),
            pl.BlockSpec((cols, consumers), lambda i: (0, 0)),
            pl.BlockSpec(memory_space=pl.ANY),
        ],
        out_specs=[
            pl.BlockSpec((rows, cols), lambda i: (0, 0)),
            pl.BlockSpec((rows, 128), lambda i: (0, 0)),
        ],
        out_shape=[
            jax.ShapeDtypeStruct((rows, cols), jnp.float32),
            jax.ShapeDtypeStruct((rows, 128), jnp.float32),
        ],
        compiler_params=pltpu.CompilerParams(vmem_limit_bytes=VMEM_BYTES),
        cost_estimate=pl.CostEstimate(
            flops=2 * rows * consumers * (depth + cols), bytes_accessed=rows * cols * 8, transcendentals=rows * consumers
        ),
        name="panel",
    )(chars, tastes, row_values, weighted, gate)


def share_sums(chars, tastes, row_values, gate):
    rows, depth = chars.shape
    consumers = tastes.shape[0]
    block, chunk = 1024, 256

    def kernel(chars_ref, tastes_ref, rows_ref, gate_ref, share_ref):
        @pl.when(pl.program_id(0) == 0)
        def _():
            share_ref[...] = jnp.zeros_like(share_ref)

        people = beside_ones(tastes_ref[...])
        peak, ratio = rows_ref[0:1, :], rows_ref[1:2, :]
        for start in range(0, rows, chunk):
            scaled = jnp.exp(dot_nt(chars_ref[start : start + chunk, :], people) - peak) * ratio
            share_ref[start : start + chunk, :] += lane_groups(scaled)

    return pl.pallas_call(
        kernel,
        grid=(consumers // block,),
        in_specs=[
            pl.BlockSpec((rows, depth), lambda i: (0, 0)),
            pl.BlockSpec((block, tastes.shape[1]), lambda i: (i, 0)),
            pl.BlockSpec((3, block), lambda i: (0, i)),
            pl.BlockSpec(memory_space=pl.ANY),
        ],
        out_specs=pl.BlockSpec((rows, 128), lambda i: (0, 0)),
        out_shape=jax.ShapeDtypeStruct((rows, 128), jnp.float32),
        compiler_params=pltpu.CompilerParams(vmem_limit_bytes=VMEM_BYTES),
        name="share_sums",
    )(chars, tastes, row_values, gate)


def swap(value, axis, mask):
    size = lax.axis_size(axis)
    return lax.ppermute(value, axis, [(i, i ^ mask) for i in range(size)])


def butterfly_masks(size):
    masks, step = [], 1
    while step < size:
        masks.append(step)
        if step * 2 < size:
            masks.append(step * 3)
        step *= 4
    return masks


def body(tastes, price_coef, characteristics, mean_utility, panel_cols, firm_map, inverses):
    products, depth = characteristics.shape
    consumers = tastes.shape[0]
    cols = panel_cols.shape[0]
    holders = lax.axis_size("prod")
    per_pair = products // holders
    count_products = products * holders
    count_consumers = consumers * lax.axis_size("cons")
    base = lax.axis_index("prod") * products
    core = lax.axis_index("cons") % 2

    pieces = jnp.stack(split3(mean_utility), axis=1)
    chars = jnp.concatenate([characteristics, jnp.pad(pieces, ((0, 0), (0, depth - 3)))], axis=1)

    wanted, order = lax.sort((firm_map, lax.iota(jnp.int32, products)), num_keys=1)
    wanted = (wanted % products).reshape(holders, per_pair)
    digits = jnp.concatenate([wanted // 256, wanted % 256], axis=1).astype(jnp.bfloat16)[:, None, :]
    product_ids = base + lax.iota(jnp.int32, products)
    hits = (panel_cols[:, None] == product_ids[None, :]).astype(jnp.bfloat16)
    col_part = jnp.dot(hits, chars, preferred_element_type=jnp.float32).astype(jnp.bfloat16)
    share_cols = cols // holders
    col_pieces = col_part[:, depth : depth + 3].reshape(holders, share_cols, 3).transpose(0, 2, 1)
    col_pieces = jnp.pad(col_pieces, ((0, 0), (0, 4), (0, depth - share_cols)))
    message = jnp.concatenate([col_part[:, :depth].reshape(holders, share_cols, depth), digits, col_pieces], axis=1)
    first = lax.all_to_all(message, "prod", split_axis=0, concat_axis=0, tiled=True)

    stat = stats(chars, tastes, message)

    asked = first[:, share_cols, :].astype(jnp.int32)
    ids = asked[:, :per_pair] * 256 + asked[:, per_pair:]
    summed = jnp.sum(first.astype(jnp.float32), axis=0)
    zeros = jnp.zeros((3, depth), jnp.float32)
    tail = jnp.concatenate([zeros, summed[share_cols + 1 : share_cols + 4], zeros[:2], summed[:share_cols]], axis=0)
    each = per_pair + 16
    sent, stat = pick_rows(ids.T, chars, tail, stat)
    second = lax.all_to_all(sent.reshape(holders, each, depth), "prod", split_axis=0, concat_axis=0, tiled=True)
    col_pieces = second[:, per_pair + 3 : per_pair + 6, :share_cols].transpose(0, 2, 1).reshape(cols, 3)
    col_chars = second[:, per_pair + 8 :, :].reshape(cols, depth)
    col_chars = jnp.concatenate([col_chars, jnp.pad(col_pieces, ((0, 0), (0, depth - 3)))], axis=1)
    mean_rows = second[:, per_pair : per_pair + 8, :].astype(jnp.float32)
    odd = lax.axis_index("prod") % 2 == 1
    mean_rows = jnp.where(odd, mean_rows[:, :, per_pair:], mean_rows[:, :, :per_pair])
    mean_rows = jnp.pad(mean_rows[:, :3], ((0, 0), (0, 5), (0, 0))).transpose(1, 0, 2).reshape(8, products)
    half, quarter = products // 2, products // 4
    kept_row = (order // half == core).astype(jnp.int32)
    place = (order // quarter % 2) * half + kept_row * quarter + order % quarter

    def join(stat, masks):
        for mask in masks:
            other = swap(stat, "prod", mask)
            joint = jnp.maximum(stat[0], other[0])
            total = stat[1] * jnp.exp(stat[0] - joint) + other[1] * jnp.exp(other[0] - joint)
            stat = jnp.stack([joint, total])
        return stat

    masks = butterfly_masks(holders)
    stat = lax.cond(panel_cols[0] >= 0, lambda value: join(value, masks), lambda value: value, stat)
    firm_chars = place_rows(
        place.reshape(1, products), second.reshape(holders * each, depth), mean_rows, holders, stat
    )
    peak = jnp.maximum(stat[0], 0.0)
    denom = jnp.exp(-peak) + stat[1] * jnp.exp(stat[0] - peak)
    ratio = count_products / denom

    row_values = jnp.stack([peak, ratio, price_coef])
    given, given_share, weighted = first_panel(firm_chars, 4, tastes, row_values, col_chars)
    own_diagonal = given[quarter]
    got = swap(given, "cons", 1)
    kept, kept_share = panel(firm_chars, 1, 4, tastes, row_values, weighted, given)
    diagonal = own_diagonal + got[quarter]
    room = 32768.0 / (count_products * jnp.maximum(diagonal, 1e-25))

    def fit(values):
        fitted = values * room[None, :]
        return lax.optimization_barrier((fitted.astype(jnp.float16), jnp.max(fitted, axis=0, keepdims=True)))

    def second_quarters(gate):
        given, given_share = panel(firm_chars, 2, 4, tastes, row_values, weighted, gate)
        got = swap(given, "cons", 1)
        kept, kept_share = panel(firm_chars, 3, 4, tastes, row_values, weighted, given)
        return *fit(kept + got), given_share, kept_share

    chip_sum, gate = fit(kept + got[:quarter])
    shapes = jax.eval_shape(second_quarters, gate)
    last_sum, last_gate, given_last, kept_last = lax.cond(
        panel_cols[2] >= 0,
        second_quarters,
        lambda gate: tuple(jnp.zeros(shape.shape, shape.dtype) for shape in shapes),
        gate,
    )
    other_sum = swap(chip_sum, "cons", 2)
    chip_sums = [(chip_sum, other_sum), (last_sum, swap(last_sum, "cons", 2))]
    shares_of = [given_share, kept_share, given_last, kept_last]
    gate = jnp.maximum(last_gate, jnp.max(other_sum.astype(jnp.float32), axis=0, keepdims=True))

    def own_and_exchange(gate, parts, own_diagonal):
        given_0, kept_0, given_1, kept_1 = (jnp.sum(part, axis=1) for part in parts)
        kept_share, given_share = jnp.concatenate([kept_0, kept_1]), jnp.concatenate([given_0, given_1])
        first_half = jnp.where(core == 0, kept_share, given_share)
        second_half = jnp.where(core == 0, given_share, kept_share)
        own_shares = jnp.sum(share_sums(chars, tastes, row_values, gate), axis=1)
        sums = jnp.concatenate([own_shares, first_half, second_half, own_diagonal])
        sums = sums + swap(sums, "cons", 1)
        return sums, swap(sums, "cons", 2)

    sums, other_sums = lax.cond(
        panel_cols[1] >= 0,
        own_and_exchange,
        lambda gate, parts, own_diagonal: (jnp.zeros(2 * products + cols, jnp.float32),) * 2,
        gate,
        shares_of,
        own_diagonal,
    )
    other_diagonal = other_sums[2 * products :]
    sums = (sums + other_sums) / count_consumers
    shares, firm_shares = sums[:products], sums[products : 2 * products]

    firm_count, block_size = inverses.shape[0], inverses.shape[1]
    own_inverses = lax.dynamic_slice_in_dim(inverses, core * (firm_count // 2), firm_count // 2, 0)
    firm_ids = lax.dynamic_slice_in_dim(firm_map, core * half, half, 0)
    other_room = 32768.0 / (count_products * jnp.maximum(other_diagonal, 1e-25))
    unfit, other_unfit = 1.0 / (room * count_consumers), 1.0 / (other_room * count_consumers)
    diagonal = (diagonal + other_diagonal) / count_consumers
    jacobians = []
    for part, (chip_sum, other_sum) in enumerate(chip_sums):
        cross = chip_sum.astype(jnp.float32) * unfit[None, :] + other_sum.astype(jnp.float32) * other_unfit[None, :]
        marks = firm_ids[part * quarter : (part + 1) * quarter, None] == panel_cols[None, :]
        jacobians.append(cross - jnp.where(marks, diagonal[None, :], 0.0))
    mine = jnp.einsum(
        "fab,fbc->fac",
        own_inverses,
        jnp.concatenate(jacobians).reshape(firm_count // 2, block_size, cols),
        precision=lax.Precision.HIGHEST,
    ).reshape(half, cols)
    theirs = swap(mine, "cons", 1)
    response = jnp.where(core == 0, jnp.concatenate([mine, theirs]), jnp.concatenate([theirs, mine]))
    markup = jnp.sum(inverses * firm_shares.reshape(firm_count, 1, block_size), axis=2).reshape(products)
    return (shares, markup, response)


def solution(mesh):
    return jax.shard_map(
        body,
        mesh=mesh,
        in_specs=(
            P("cons", None),
            P("cons"),
            P("prod", None),
            P("prod"),
            P(),
            P("prod"),
            P("prod", None, None),
        ),
        out_specs=(P("prod"), P("prod"), P("prod", None)),
        check_vma=False,
    )
```

```python
import jax
import jax.numpy as jnp
from jax import lax
from jax.experimental import pallas as pl
from jax.experimental.pallas import tpu as pltpu
from jax.sharding import PartitionSpec as P

NT = (((1,), (1,)), ((), ()))
VMEM_BYTES = 24 * 1024 * 1024


def dot_nt(left, right):
    return lax.dot_general(left, right, NT, preferred_element_type=jnp.float32)


def rounded(values):
    return values.astype(jnp.bfloat16).astype(jnp.float32)


def prepare(characteristics, means, firm_row, panel_rows, holders):
    rows, depth = characteristics.shape
    per_pair = rows // holders
    cols = panel_rows.shape[0] * 128
    share_cols = cols // holders
    chunk = 256

    def kernel(chars_ref, means_ref, firm_ref, panel_ref, both_ref, message_ref, order_ref):
        lane = lax.broadcasted_iota(jnp.int32, (128, 128), 1)
        values = means_ref[...]
        high = rounded(values)
        middle = rounded(values - high)
        low = values - high - middle
        pieces = jnp.concatenate([high, middle, low, jnp.zeros((128 - 3 * values.shape[0], 128), jnp.float32)], axis=0).T
        count = values.shape[0]
        both_ref[:, :depth] = chars_ref[...]
        for k in range(count):
            beside = jnp.zeros((128, 128), jnp.float32)
            for piece in range(3):
                place = piece * count + k
                beside = jnp.where(lane == piece + 1, pieces[:, place : place + 1], beside)
            both_ref[k * 128 : (k + 1) * 128, depth:] = beside.astype(jnp.bfloat16)

        firm = firm_ref[...]
        holder, wanted = firm // rows, firm % rows
        holder_id = lax.broadcasted_iota(jnp.int32, (holders, rows), 0)
        named = jnp.where(holder_id == holder, 1.0, 0.0)
        blocks = [named[:, start : start + 128] for start in range(0, rows, 128)]
        before = (lax.broadcasted_iota(jnp.int32, (128, 128), 0) < lane).astype(jnp.float32).astype(jnp.bfloat16)
        counts = jnp.dot(
            jnp.concatenate(blocks, axis=0).astype(jnp.bfloat16), before, preferred_element_type=jnp.float32
        )
        seen = jnp.zeros((holders, 1), jnp.float32)
        ranks = []
        for k, block in enumerate(blocks):
            rank = counts[k * holders : (k + 1) * holders, :] + seen
            ranks.append(jnp.sum(block * rank, axis=0, keepdims=True))
            seen = seen + jnp.sum(block, axis=1, keepdims=True)
        slot = holder * per_pair + jnp.concatenate(ranks, axis=1).astype(jnp.int32)

        row = lax.broadcasted_iota(jnp.int32, (8, rows), 0)
        firm_place = lax.broadcasted_iota(jnp.int32, (8, rows), 1)
        digits = jnp.where(row == 0, wanted // 256, jnp.where(row == 1, wanted % 256, 0))
        digits = jnp.where(row == 2, firm_place // 256, jnp.where(row == 3, firm_place % 256, digits))
        digits = jnp.concatenate([digits, jnp.zeros_like(digits)], axis=0).astype(jnp.float32).astype(jnp.bfloat16)
        asked = []
        for start in range(0, rows, chunk):
            slots = start + lax.broadcasted_iota(jnp.int32, (chunk, rows), 0)
            hot = jnp.where(slots == slot, 1.0, 0.0).astype(jnp.bfloat16)
            found = dot_nt(digits, hot)
            order_ref[:, start : start + chunk] = (found[2:3, :] * 256.0 + found[3:4, :]).astype(jnp.int32)
            asked.append(found)

        products = lax.broadcasted_iota(jnp.int32, (128, rows), 1).astype(jnp.float32)
        both = both_ref[...]
        wide = jnp.concatenate([panel_ref[...], jnp.zeros((128 - panel_ref.shape[0], 128), jnp.float32)], axis=0).T
        part_row = lax.broadcasted_iota(jnp.int32, (8, 128), 0)
        for k in range(cols // 128):
            hot = jnp.where(wide[:, k : k + 1] == products, 1.0, 0.0).astype(jnp.bfloat16)
            part = jnp.dot(hot, both, preferred_element_type=jnp.float32)
            part_pieces = part[:, depth:].T[:8, :]
            for place in range(128 // share_cols):
                q = k * (128 // share_cols) + place
                start = q * per_pair // 128 * 128 % chunk
                found = asked[q * per_pair // chunk][:, start : start + 128]
                extra = jnp.where(part_row == 0, found[0:1, :], jnp.where(part_row == 4, found[1:2, :], part_pieces))
                mine = part[place * share_cols : (place + 1) * share_cols, :depth]
                message_ref[q * 16 : (q + 1) * 16, :] = jnp.concatenate([mine, extra], axis=0).astype(jnp.bfloat16)

    return pl.pallas_call(
        kernel,
        out_shape=[
            jax.ShapeDtypeStruct((rows, 2 * depth), jnp.bfloat16),
            jax.ShapeDtypeStruct((16 * holders, depth), jnp.bfloat16),
            jax.ShapeDtypeStruct((1, rows), jnp.int32),
        ],
        compiler_params=pltpu.CompilerParams(vmem_limit_bytes=VMEM_BYTES),
        name="prepare",
    )(characteristics, means, firm_row, panel_rows)


def beside_ones(tastes):
    lane = lax.broadcasted_iota(jnp.int32, tastes.shape, 1)
    ones = jnp.where((lane >= 1) & (lane <= 3), 1.0, 0.0)
    return jnp.concatenate([tastes, ones.astype(tastes.dtype)], axis=1)


def stats(chars, tastes, gate):
    rows, depth = chars.shape
    consumers = tastes.shape[0]
    block, sub, chunk = 2048, 256, 256
    count = block // sub

    def kernel(chars_ref, tastes_ref, gate_ref, stat_ref, util_ref):
        people = [beside_ones(tastes_ref[k * sub : (k + 1) * sub, :]) for k in range(count)]
        before = None
        for k in range(count + 1):
            peak = jnp.full((8, sub), -jnp.inf, jnp.float32)
            total = jnp.zeros((8, sub), jnp.float32)
            for start in range(0, rows, chunk):
                if k < count:
                    util = dot_nt(chars_ref[start : start + chunk, :], people[k])
                    util_ref[k % 2, start : start + chunk, :] = util
                    peak = jnp.maximum(peak, jnp.max(util.reshape(chunk // 8, 8, sub), axis=0))
                if k > 0:
                    expo = jnp.exp(util_ref[(k - 1) % 2, start : start + chunk, :] - before)
                    total = total + jnp.sum(expo.reshape(chunk // 8, 8, sub), axis=0)
            if k > 0:
                stat_ref[0:1, (k - 1) * sub : k * sub] = before
                stat_ref[1:2, (k - 1) * sub : k * sub] = jnp.sum(total, axis=0, keepdims=True)
            before = jnp.max(peak, axis=0, keepdims=True)

    return pl.pallas_call(
        kernel,
        grid=(consumers // block,),
        in_specs=[
            pl.BlockSpec((rows, depth), lambda i: (0, 0)),
            pl.BlockSpec((block, tastes.shape[1]), lambda i: (i, 0)),
            pl.BlockSpec(memory_space=pl.ANY),
        ],
        out_specs=pl.BlockSpec((2, block), lambda i: (0, i)),
        out_shape=jax.ShapeDtypeStruct((2, consumers), jnp.float32),
        scratch_shapes=[pltpu.VMEM((2, rows, sub), jnp.float32)],
        compiler_params=pltpu.CompilerParams(vmem_limit_bytes=VMEM_BYTES),
        name="stats",
    )(chars, tastes, gate)


def pick_rows(ids_t, chars, tail, stat):
    per_pair, holders = ids_t.shape
    rows, depth = chars.shape
    each = per_pair + 16
    group, pair = 256 // per_pair, 128 // per_pair

    def kernel(ids_ref, chars_ref, tail_ref, stat_ref, out_ref, stat_out_ref):
        stat_out_ref[...] = stat_ref[...]
        lanes = lax.broadcasted_iota(jnp.int32, (per_pair, rows), 1)
        table = chars_ref[...]
        for start in range(0, holders, group):
            span = range(start, start + group)
            marks = [jnp.where(ids_ref[:, q : q + 1] == lanes, 1.0, 0.0).astype(jnp.bfloat16) for q in span]
            picked = jnp.dot(jnp.concatenate(marks, axis=0), table, preferred_element_type=jnp.float32)
            for place, q in enumerate(span):
                if place % pair == 0:
                    beside = picked[place * per_pair : (place + pair) * per_pair, 128:].T[:8, :]
                    block = jnp.concatenate([beside + tail_ref[0:8, :], tail_ref[8:16, :]], axis=0).astype(jnp.bfloat16)
                mine = picked[place * per_pair : (place + 1) * per_pair, :128]
                out_ref[q * each : q * each + per_pair, :] = mine.astype(jnp.bfloat16)
                out_ref[q * each + per_pair : (q + 1) * each, :] = block

    return pl.pallas_call(
        kernel,
        out_shape=[
            jax.ShapeDtypeStruct((each * holders, depth // 2), jnp.bfloat16),
            jax.ShapeDtypeStruct(stat.shape, stat.dtype),
        ],
        compiler_params=pltpu.CompilerParams(vmem_limit_bytes=VMEM_BYTES),
        name="pick_rows",
    )(ids_t, chars, tail, stat)


def place_rows(order, received, beside, holders, gate):
    rows = order.shape[1]
    total, depth = received.shape
    per_pair, each = rows // holders, total // holders
    chunk = 256

    def kernel(order_ref, received_ref, beside_ref, gate_ref, out_ref):
        order_row = order_ref[...]
        table = jnp.concatenate([received_ref[q * each : q * each + per_pair, :] for q in range(holders)], axis=0)
        blank = jnp.zeros((120, 128), jnp.float32)
        columns = [
            jnp.concatenate([beside_ref[:, start : start + 128], blank], axis=0).T.astype(jnp.bfloat16)
            for start in range(0, rows, 128)
        ]
        table = jnp.concatenate([table, jnp.concatenate(columns, axis=0)], axis=1)
        for start in range(0, rows, chunk):
            ids = start + lax.broadcasted_iota(jnp.int32, (chunk, rows), 0)
            hot = jnp.where(ids == order_row, 1.0, 0.0).astype(jnp.bfloat16)
            placed = jnp.dot(hot, table, preferred_element_type=jnp.float32)
            out_ref[start : start + chunk, :] = placed.astype(jnp.bfloat16)

    return pl.pallas_call(
        kernel,
        in_specs=[pl.BlockSpec(memory_space=pltpu.VMEM)] * 3 + [pl.BlockSpec(memory_space=pl.ANY)],
        out_shape=jax.ShapeDtypeStruct((rows, 2 * depth), jnp.bfloat16),
        compiler_params=pltpu.CompilerParams(vmem_limit_bytes=VMEM_BYTES),
        name="place_rows",
    )(order, received, beside, gate)


def lane_groups(values):
    total = values[:, 0:128]
    for start in range(128, values.shape[1], 128):
        total = total + values[:, start : start + 128]
    return total


def first_panel(chars, parts, tastes, row_values, col_chars):
    rows, depth = chars.shape[0] // parts, chars.shape[1]
    consumers = tastes.shape[0]
    cols = col_chars.shape[0]
    block, chunk = 1024, 256

    def kernel(chars_ref, tastes_ref, rows_ref, cols_ref, panel_ref, share_ref, weight_ref, diag_ref):
        step = pl.program_id(0)

        @pl.when(step == 0)
        def _():
            panel_ref[...] = jnp.zeros_like(panel_ref)
            share_ref[...] = jnp.zeros_like(share_ref)
            diag_ref[...] = jnp.zeros_like(diag_ref)

        people = beside_ones(tastes_ref[...])
        peak, ratio = rows_ref[0:1, :], rows_ref[1:2, :]
        weighted = rows_ref[2:3, :] * (jnp.exp(dot_nt(cols_ref[...], people) - peak) * ratio)
        diag_ref[...] += lane_groups(weighted)
        weight = weighted.astype(jnp.bfloat16)
        weight_ref[...] = weight
        for start in range(0, rows, chunk):
            scaled = jnp.exp(dot_nt(chars_ref[start : start + chunk, :], people) - peak) * ratio
            share_ref[start : start + chunk, :] += lane_groups(scaled)
            panel_ref[start : start + chunk, :] += dot_nt(scaled.astype(jnp.bfloat16), weight)

        @pl.when(step == pl.num_programs(0) - 1)
        def _():
            total = jnp.sum(diag_ref[...].T, axis=0, keepdims=True)
            panel_ref[rows:, :] = jnp.broadcast_to(total, (8, cols))

    return pl.pallas_call(
        kernel,
        grid=(consumers // block,),
        in_specs=[
            pl.BlockSpec((rows, depth), lambda i: (0, 0)),
            pl.BlockSpec((block, tastes.shape[1]), lambda i: (i, 0)),
            pl.BlockSpec((3, block), lambda i: (0, i)),
            pl.BlockSpec((cols, depth), lambda i: (0, 0)),
        ],
        out_specs=[
            pl.BlockSpec((rows + 8, cols), lambda i: (0, 0)),
            pl.BlockSpec((rows, 128), lambda i: (0, 0)),
            pl.BlockSpec((cols, block), lambda i: (0, i)),
        ],
        scratch_shapes=[pltpu.VMEM((cols, 128), jnp.float32)],
        out_shape=[
            jax.ShapeDtypeStruct((rows + 8, cols), jnp.float32),
            jax.ShapeDtypeStruct((rows, 128), jnp.float32),
            jax.ShapeDtypeStruct((cols, consumers), jnp.bfloat16),
        ],
        compiler_params=pltpu.CompilerParams(vmem_limit_bytes=VMEM_BYTES),
        cost_estimate=pl.CostEstimate(
            flops=2 * rows * consumers * (depth + cols), bytes_accessed=rows * cols * 8, transcendentals=rows * consumers
        ),
        name="first_panel",
    )(chars, tastes, row_values, col_chars)


def panel(chars, part, parts, tastes, row_values, weighted, gate):
    rows, depth = chars.shape[0] // parts, chars.shape[1]
    consumers = tastes.shape[0]
    cols = weighted.shape[0]
    chunk = 256

    def kernel(chars_ref, tastes_ref, rows_ref, weight_ref, gate_ref, panel_ref, share_ref):
        people, weight = beside_ones(tastes_ref[...]), weight_ref[...]
        peak, ratio = rows_ref[0:1, :], rows_ref[1:2, :]
        for start in range(0, rows, chunk):
            scaled = jnp.exp(dot_nt(chars_ref[start : start + chunk, :], people) - peak) * ratio
            share_ref[start : start + chunk, :] = lane_groups(scaled)
            panel_ref[start : start + chunk, :] = dot_nt(scaled.astype(jnp.bfloat16), weight)

    return pl.pallas_call(
        kernel,
        grid=(1,),
        in_specs=[
            pl.BlockSpec((rows, depth), lambda i: (part, 0)),
            pl.BlockSpec(tastes.shape, lambda i: (0, 0)),
            pl.BlockSpec((3, consumers), lambda i: (0, 0)),
            pl.BlockSpec((cols, consumers), lambda i: (0, 0)),
            pl.BlockSpec(memory_space=pl.ANY),
        ],
        out_specs=[
            pl.BlockSpec((rows, cols), lambda i: (0, 0)),
            pl.BlockSpec((rows, 128), lambda i: (0, 0)),
        ],
        out_shape=[
            jax.ShapeDtypeStruct((rows, cols), jnp.float32),
            jax.ShapeDtypeStruct((rows, 128), jnp.float32),
        ],
        compiler_params=pltpu.CompilerParams(vmem_limit_bytes=VMEM_BYTES),
        cost_estimate=pl.CostEstimate(
            flops=2 * rows * consumers * (depth + cols), bytes_accessed=rows * cols * 8, transcendentals=rows * consumers
        ),
        name="panel",
    )(chars, tastes, row_values, weighted, gate)


def share_sums(chars, tastes, row_values, gate):
    rows, depth = chars.shape
    consumers = tastes.shape[0]
    block, chunk = 1024, 256

    def kernel(chars_ref, tastes_ref, rows_ref, gate_ref, share_ref):
        @pl.when(pl.program_id(0) == 0)
        def _():
            share_ref[...] = jnp.zeros_like(share_ref)

        people = beside_ones(tastes_ref[...])
        peak, ratio = rows_ref[0:1, :], rows_ref[1:2, :]
        for start in range(0, rows, chunk):
            scaled = jnp.exp(dot_nt(chars_ref[start : start + chunk, :], people) - peak) * ratio
            share_ref[start : start + chunk, :] += lane_groups(scaled)

    return pl.pallas_call(
        kernel,
        grid=(consumers // block,),
        in_specs=[
            pl.BlockSpec((rows, depth), lambda i: (0, 0)),
            pl.BlockSpec((block, tastes.shape[1]), lambda i: (i, 0)),
            pl.BlockSpec((3, block), lambda i: (0, i)),
            pl.BlockSpec(memory_space=pl.ANY),
        ],
        out_specs=pl.BlockSpec((rows, 128), lambda i: (0, 0)),
        out_shape=jax.ShapeDtypeStruct((rows, 128), jnp.float32),
        compiler_params=pltpu.CompilerParams(vmem_limit_bytes=VMEM_BYTES),
        name="share_sums",
    )(chars, tastes, row_values, gate)


def swap(value, axis, mask):
    size = lax.axis_size(axis)
    return lax.ppermute(value, axis, [(i, i ^ mask) for i in range(size)])


def butterfly_masks(size):
    masks, step = [], 1
    while step < size:
        masks.append(step)
        if step * 2 < size:
            masks.append(step * 3)
        step *= 4
    return masks


def body(tastes, price_coef, characteristics, mean_utility, panel_cols, firm_map, inverses):
    products, depth = characteristics.shape
    consumers = tastes.shape[0]
    cols = panel_cols.shape[0]
    holders = lax.axis_size("prod")
    per_pair = products // holders
    count_products = products * holders
    count_consumers = consumers * lax.axis_size("cons")
    base = lax.axis_index("prod") * products
    core = lax.axis_index("cons") % 2

    share_cols = cols // holders
    chars, message, order = prepare(
        characteristics,
        mean_utility.reshape(products // 128, 128),
        firm_map.reshape(1, products),
        (panel_cols - base).astype(jnp.float32).reshape(cols // 128, 128),
        holders,
    )
    first = lax.all_to_all(message.reshape(holders, 16, depth), "prod", split_axis=0, concat_axis=0, tiled=True)

    stat = stats(chars, tastes, message)

    odd = lax.axis_index("prod") % 2 == 1

    def own_lanes(values):
        return jnp.where(odd, values[..., per_pair:], values[..., :per_pair])

    high, low = own_lanes(first[:, 8, :]), own_lanes(first[:, 12, :])
    ids = high.astype(jnp.int32) * 256 + low.astype(jnp.int32)
    summed = jnp.sum(first.astype(jnp.float32), axis=0)
    tail = jnp.concatenate([jnp.zeros((5, depth), jnp.float32), summed[9:12], summed[:8]], axis=0)
    each = per_pair + 16
    sent, stat = pick_rows(ids.T, chars, tail, stat)
    second = lax.all_to_all(sent.reshape(holders, each, depth), "prod", split_axis=0, concat_axis=0, tiled=True)
    col_pieces = second[:: 128 // share_cols, per_pair + 5 : per_pair + 8, :].transpose(0, 2, 1).reshape(cols, 3)
    col_chars = second[:, per_pair + 8 :, :].reshape(cols, depth)
    col_chars = jnp.concatenate([col_chars, jnp.pad(col_pieces, ((0, 0), (1, depth - 4)))], axis=1)
    mean_rows = own_lanes(second[:, per_pair : per_pair + 4, :].astype(jnp.float32))
    mean_rows = jnp.pad(mean_rows, ((0, 0), (0, 4), (0, 0))).transpose(1, 0, 2).reshape(8, products)
    half = products // 2
    place = (order // half == core).astype(jnp.int32) * half + order % half

    def join(stat, masks):
        for mask in masks:
            other = swap(stat, "prod", mask)
            joint = jnp.maximum(stat[0], other[0])
            total = stat[1] * jnp.exp(stat[0] - joint) + other[1] * jnp.exp(other[0] - joint)
            stat = jnp.stack([joint, total])
        return stat

    masks = butterfly_masks(holders)
    stat = lax.cond(panel_cols[0] >= 0, lambda value: join(value, masks), lambda value: value, stat)
    firm_chars = place_rows(
        place.reshape(1, products), second.reshape(holders * each, depth), mean_rows, holders, stat
    )
    peak = jnp.maximum(stat[0], 0.0)
    denom = jnp.exp(-peak) + stat[1] * jnp.exp(stat[0] - peak)
    ratio = count_products / denom

    row_values = jnp.stack([peak, ratio, price_coef])
    given, given_share, weighted = first_panel(firm_chars, 2, tastes, row_values, col_chars)
    got = swap(given, "cons", 1)
    kept, kept_share = panel(firm_chars, 1, 2, tastes, row_values, weighted, given)
    diagonal = given[half] + got[half]
    room = 32768.0 / (count_products * jnp.maximum(diagonal, 1e-25))
    fitted = (kept + got[:half]) * room[None, :]
    chip_sum, gate = lax.optimization_barrier((fitted.astype(jnp.float16), jnp.max(fitted, axis=0, keepdims=True)))
    other_sum = swap(chip_sum, "cons", 2)

    given_share, kept_share = jnp.sum(given_share, axis=1), jnp.sum(kept_share, axis=1)
    first_half = jnp.where(core == 0, kept_share, given_share)
    second_half = jnp.where(core == 0, given_share, kept_share)

    def own_and_exchange(gate, others):
        own_shares = jnp.sum(share_sums(chars, tastes, row_values, gate), axis=1)
        sums = jnp.concatenate([own_shares, others])
        sums = sums + swap(sums, "cons", 1)
        return sums, swap(sums, "cons", 2)

    sums, other_sums = lax.cond(
        panel_cols[1] >= 0,
        own_and_exchange,
        lambda gate, others: (jnp.zeros(products + others.shape[0], jnp.float32),) * 2,
        gate,
        jnp.concatenate([first_half, second_half, given[half]]),
    )
    other_diagonal = other_sums[2 * products :]
    sums = (sums + other_sums) / count_consumers
    shares, firm_shares = sums[:products], sums[products : 2 * products]

    firm_count, block_size = inverses.shape[0], inverses.shape[1]
    own_inverses = lax.dynamic_slice_in_dim(inverses, core * (firm_count // 2), firm_count // 2, 0)
    firm_ids = lax.dynamic_slice_in_dim(firm_map, core * half, half, 0)
    other_room = 32768.0 / (count_products * jnp.maximum(other_diagonal, 1e-25))
    unfit, other_unfit = 1.0 / (room * count_consumers), 1.0 / (other_room * count_consumers)
    cross = chip_sum.astype(jnp.float32) * unfit[None, :] + other_sum.astype(jnp.float32) * other_unfit[None, :]
    diagonal = (diagonal + other_diagonal) / count_consumers
    jacobian = cross - jnp.where(firm_ids[:, None] == panel_cols[None, :], diagonal[None, :], 0.0)
    mine = jnp.einsum(
        "fab,fbc->fac",
        own_inverses,
        jacobian.reshape(firm_count // 2, block_size, cols),
        precision=lax.Precision.HIGHEST,
    ).reshape(half, cols)
    theirs = swap(mine, "cons", 1)
    response = jnp.where(core == 0, jnp.concatenate([mine, theirs]), jnp.concatenate([theirs, mine]))
    markup = jnp.sum(inverses * firm_shares.reshape(firm_count, 1, block_size), axis=2).reshape(products)
    return (shares, markup, response)


def solution(mesh):
    return jax.shard_map(
        body,
        mesh=mesh,
        in_specs=(
            P("cons", None),
            P("cons"),
            P("prod", None),
            P("prod"),
            P(),
            P("prod"),
            P("prod", None, None),
        ),
        out_specs=(P("prod"), P("prod"), P("prod", None)),
        check_vma=False,
    )
```

```python
import jax
import jax.numpy as jnp
from jax import lax
from jax.experimental import pallas as pl
from jax.experimental.pallas import tpu as pltpu
from jax.sharding import PartitionSpec as P

NT = (((1,), (1,)), ((), ()))
VMEM_BYTES = 24 * 1024 * 1024


def dot_nt(left, right):
    return lax.dot_general(left, right, NT, preferred_element_type=jnp.float32)


def rounded(values):
    return values.astype(jnp.bfloat16).astype(jnp.float32)


def prepare(characteristics, means, firm_row, panel_rows, holders):
    rows, depth = characteristics.shape
    per_pair = rows // holders
    cols = panel_rows.shape[0] * 128
    share_cols = cols // holders
    chunk = 256

    def kernel(chars_ref, means_ref, firm_ref, panel_ref, both_ref, message_ref, order_ref):
        lane = lax.broadcasted_iota(jnp.int32, (128, 128), 1)
        values = means_ref[...]
        high = rounded(values)
        middle = rounded(values - high)
        low = values - high - middle
        pieces = jnp.concatenate([high, middle, low, jnp.zeros((128 - 3 * values.shape[0], 128), jnp.float32)], axis=0).T
        count = values.shape[0]
        both_ref[:, :depth] = chars_ref[...]
        for k in range(count):
            beside = jnp.zeros((128, 128), jnp.float32)
            for piece in range(3):
                place = piece * count + k
                beside = jnp.where(lane == piece + 1, pieces[:, place : place + 1], beside)
            both_ref[k * 128 : (k + 1) * 128, depth:] = beside.astype(jnp.bfloat16)

        firm = firm_ref[...]
        holder, wanted = firm // rows, firm % rows
        holder_id = lax.broadcasted_iota(jnp.int32, (holders, rows), 0)
        named = jnp.where(holder_id == holder, 1.0, 0.0)
        blocks = [named[:, start : start + 128] for start in range(0, rows, 128)]
        before = (lax.broadcasted_iota(jnp.int32, (128, 128), 0) < lane).astype(jnp.float32).astype(jnp.bfloat16)
        counts = jnp.dot(
            jnp.concatenate(blocks, axis=0).astype(jnp.bfloat16), before, preferred_element_type=jnp.float32
        )
        seen = jnp.zeros((holders, 1), jnp.float32)
        ranks = []
        for k, block in enumerate(blocks):
            rank = counts[k * holders : (k + 1) * holders, :] + seen
            ranks.append(jnp.sum(block * rank, axis=0, keepdims=True))
            seen = seen + jnp.sum(block, axis=1, keepdims=True)
        slot = holder * per_pair + jnp.concatenate(ranks, axis=1).astype(jnp.int32)

        row = lax.broadcasted_iota(jnp.int32, (8, rows), 0)
        firm_place = lax.broadcasted_iota(jnp.int32, (8, rows), 1)
        digits = jnp.where(row == 0, wanted // 256, jnp.where(row == 1, wanted % 256, 0))
        digits = jnp.where(row == 2, firm_place // 256, jnp.where(row == 3, firm_place % 256, digits))
        digits = jnp.concatenate([digits, jnp.zeros_like(digits)], axis=0).astype(jnp.float32).astype(jnp.bfloat16)
        asked = []
        for start in range(0, rows, chunk):
            slots = start + lax.broadcasted_iota(jnp.int32, (chunk, rows), 0)
            hot = jnp.where(slots == slot, 1.0, 0.0).astype(jnp.bfloat16)
            found = dot_nt(digits, hot)
            order_ref[:, start : start + chunk] = (found[2:3, :] * 256.0 + found[3:4, :]).astype(jnp.int32)
            asked.append(found)

        products = lax.broadcasted_iota(jnp.int32, (128, rows), 1).astype(jnp.float32)
        both = both_ref[...]
        wide = jnp.concatenate([panel_ref[...], jnp.zeros((128 - panel_ref.shape[0], 128), jnp.float32)], axis=0).T
        part_row = lax.broadcasted_iota(jnp.int32, (8, 128), 0)
        for k in range(cols // 128):
            hot = jnp.where(wide[:, k : k + 1] == products, 1.0, 0.0).astype(jnp.bfloat16)
            part = jnp.dot(hot, both, preferred_element_type=jnp.float32)
            part_pieces = part[:, depth:].T[:8, :]
            for place in range(128 // share_cols):
                q = k * (128 // share_cols) + place
                start = q * per_pair // 128 * 128 % chunk
                found = asked[q * per_pair // chunk][:, start : start + 128]
                extra = jnp.where(part_row == 0, found[0:1, :], jnp.where(part_row == 4, found[1:2, :], part_pieces))
                mine = part[place * share_cols : (place + 1) * share_cols, :depth]
                message_ref[q * 16 : (q + 1) * 16, :] = jnp.concatenate([mine, extra], axis=0).astype(jnp.bfloat16)

    def whole(shape):
        return pl.BlockSpec(shape, lambda i: (0, 0))

    return pl.pallas_call(
        kernel,
        grid=(1,),
        in_specs=[whole(value.shape) for value in (characteristics, means, firm_row, panel_rows)],
        out_specs=[whole((rows, 2 * depth)), whole((16 * holders, depth)), whole((1, rows))],
        out_shape=[
            jax.ShapeDtypeStruct((rows, 2 * depth), jnp.bfloat16),
            jax.ShapeDtypeStruct((16 * holders, depth), jnp.bfloat16),
            jax.ShapeDtypeStruct((1, rows), jnp.int32),
        ],
        compiler_params=pltpu.CompilerParams(vmem_limit_bytes=60 * 1024 * 1024),
        name="prepare",
    )(characteristics, means, firm_row, panel_rows)


def beside_ones(tastes):
    lane = lax.broadcasted_iota(jnp.int32, tastes.shape, 1)
    ones = jnp.where((lane >= 1) & (lane <= 3), 1.0, 0.0)
    return jnp.concatenate([tastes, ones.astype(tastes.dtype)], axis=1)


def stats(chars, tastes):
    rows, depth = chars.shape
    consumers = tastes.shape[0]
    block, chunk = 2048, 256

    def kernel(chars_ref, tastes_ref, stat_ref):
        people = beside_ones(tastes_ref[...])
        peak = jnp.full((1, block), -jnp.inf, jnp.float32)
        total = jnp.zeros((8, block), jnp.float32)
        for start in range(0, rows, chunk):
            util = dot_nt(chars_ref[start : start + chunk, :], people)
            highest = jnp.max(util.reshape(chunk // 8, 8, block), axis=0)
            joint = jnp.maximum(peak, jnp.max(highest, axis=0, keepdims=True))
            expo = jnp.exp(util - joint)
            total = total * jnp.exp(peak - joint) + jnp.sum(expo.reshape(chunk // 8, 8, block), axis=0)
            peak = joint
        stat_ref[0:1, :] = peak
        stat_ref[1:2, :] = jnp.sum(total, axis=0, keepdims=True)

    return pl.pallas_call(
        kernel,
        grid=(consumers // block,),
        in_specs=[
            pl.BlockSpec((rows, depth), lambda i: (0, 0)),
            pl.BlockSpec((block, tastes.shape[1]), lambda i: (i, 0)),
        ],
        out_specs=pl.BlockSpec((2, block), lambda i: (0, i)),
        out_shape=jax.ShapeDtypeStruct((2, consumers), jnp.float32),
        compiler_params=pltpu.CompilerParams(vmem_limit_bytes=VMEM_BYTES),
        name="stats",
    )(chars, tastes)


def pick_rows(ids_t, chars, tail, stat):
    per_pair, holders = ids_t.shape
    rows, depth = chars.shape
    each = per_pair + 16
    group, pair = 256 // per_pair, 128 // per_pair

    def kernel(ids_ref, chars_ref, tail_ref, stat_ref, out_ref, stat_out_ref):
        stat_out_ref[...] = stat_ref[...]
        lanes = lax.broadcasted_iota(jnp.int32, (per_pair, rows), 1)
        table = chars_ref[...]
        for start in range(0, holders, group):
            span = range(start, start + group)
            marks = [jnp.where(ids_ref[:, q : q + 1] == lanes, 1.0, 0.0).astype(jnp.bfloat16) for q in span]
            picked = jnp.dot(jnp.concatenate(marks, axis=0), table, preferred_element_type=jnp.float32)
            for place, q in enumerate(span):
                if place % pair == 0:
                    beside = picked[place * per_pair : (place + pair) * per_pair, 128:].T[:8, :]
                    block = jnp.concatenate([beside + tail_ref[0:8, :], tail_ref[8:16, :]], axis=0).astype(jnp.bfloat16)
                mine = picked[place * per_pair : (place + 1) * per_pair, :128]
                out_ref[q * each : q * each + per_pair, :] = mine.astype(jnp.bfloat16)
                out_ref[q * each + per_pair : (q + 1) * each, :] = block

    return pl.pallas_call(
        kernel,
        out_shape=[
            jax.ShapeDtypeStruct((each * holders, depth // 2), jnp.bfloat16),
            jax.ShapeDtypeStruct(stat.shape, stat.dtype),
        ],
        compiler_params=pltpu.CompilerParams(vmem_limit_bytes=VMEM_BYTES),
        name="pick_rows",
    )(ids_t, chars, tail, stat)


def place_rows(order, received, beside, holders, gate):
    rows = order.shape[1]
    total, depth = received.shape
    per_pair, each = rows // holders, total // holders
    chunk = 256

    def kernel(order_ref, received_ref, beside_ref, gate_ref, out_ref):
        order_row = order_ref[...]
        table = jnp.concatenate([received_ref[q * each : q * each + per_pair, :] for q in range(holders)], axis=0)
        blank = jnp.zeros((120, 128), jnp.float32)
        columns = [
            jnp.concatenate([beside_ref[:, start : start + 128], blank], axis=0).T.astype(jnp.bfloat16)
            for start in range(0, rows, 128)
        ]
        table = jnp.concatenate([table, jnp.concatenate(columns, axis=0)], axis=1)
        for start in range(0, rows, chunk):
            ids = start + lax.broadcasted_iota(jnp.int32, (chunk, rows), 0)
            hot = jnp.where(ids == order_row, 1.0, 0.0).astype(jnp.bfloat16)
            placed = jnp.dot(hot, table, preferred_element_type=jnp.float32)
            out_ref[start : start + chunk, :] = placed.astype(jnp.bfloat16)

    return pl.pallas_call(
        kernel,
        in_specs=[pl.BlockSpec(memory_space=pltpu.VMEM)] * 3 + [pl.BlockSpec(memory_space=pl.ANY)],
        out_shape=jax.ShapeDtypeStruct((rows, 2 * depth), jnp.bfloat16),
        compiler_params=pltpu.CompilerParams(vmem_limit_bytes=VMEM_BYTES),
        name="place_rows",
    )(order, received, beside, gate)


def lane_groups(values):
    total = values[:, 0:128]
    for start in range(128, values.shape[1], 128):
        total = total + values[:, start : start + 128]
    return total


def first_panel(chars, parts, tastes, row_values, col_chars):
    rows, depth = chars.shape[0] // parts, chars.shape[1]
    consumers = tastes.shape[0]
    cols = col_chars.shape[0]
    block, chunk = 1024, 256

    def kernel(chars_ref, tastes_ref, rows_ref, cols_ref, panel_ref, share_ref, weight_ref, diag_ref):
        step = pl.program_id(0)

        @pl.when(step == 0)
        def _():
            panel_ref[...] = jnp.zeros_like(panel_ref)
            share_ref[...] = jnp.zeros_like(share_ref)
            diag_ref[...] = jnp.zeros_like(diag_ref)

        people = beside_ones(tastes_ref[...])
        peak, ratio = rows_ref[0:1, :], rows_ref[1:2, :]
        weighted = rows_ref[2:3, :] * (jnp.exp(dot_nt(cols_ref[...], people) - peak) * ratio)
        diag_ref[...] += lane_groups(weighted)
        weight = weighted.astype(jnp.bfloat16)
        weight_ref[...] = weight
        for start in range(0, rows, chunk):
            scaled = jnp.exp(dot_nt(chars_ref[start : start + chunk, :], people) - peak) * ratio
            share_ref[start : start + chunk, :] += lane_groups(scaled)
            panel_ref[start : start + chunk, :] += dot_nt(scaled.astype(jnp.bfloat16), weight)

        @pl.when(step == pl.num_programs(0) - 1)
        def _():
            total = jnp.sum(diag_ref[...].T, axis=0, keepdims=True)
            panel_ref[rows:, :] = jnp.broadcast_to(total, (8, cols))

    return pl.pallas_call(
        kernel,
        grid=(consumers // block,),
        in_specs=[
            pl.BlockSpec((rows, depth), lambda i: (0, 0)),
            pl.BlockSpec((block, tastes.shape[1]), lambda i: (i, 0)),
            pl.BlockSpec((3, block), lambda i: (0, i)),
            pl.BlockSpec((cols, depth), lambda i: (0, 0)),
        ],
        out_specs=[
            pl.BlockSpec((rows + 8, cols), lambda i: (0, 0)),
            pl.BlockSpec((rows, 128), lambda i: (0, 0)),
            pl.BlockSpec((cols, block), lambda i: (0, i)),
        ],
        scratch_shapes=[pltpu.VMEM((cols, 128), jnp.float32)],
        out_shape=[
            jax.ShapeDtypeStruct((rows + 8, cols), jnp.float32),
            jax.ShapeDtypeStruct((rows, 128), jnp.float32),
            jax.ShapeDtypeStruct((cols, consumers), jnp.bfloat16),
        ],
        compiler_params=pltpu.CompilerParams(vmem_limit_bytes=VMEM_BYTES),
        cost_estimate=pl.CostEstimate(
            flops=2 * rows * consumers * (depth + cols), bytes_accessed=rows * cols * 8, transcendentals=rows * consumers
        ),
        name="first_panel",
    )(chars, tastes, row_values, col_chars)


def panel(chars, part, parts, tastes, row_values, weighted, gate):
    rows, depth = chars.shape[0] // parts, chars.shape[1]
    consumers = tastes.shape[0]
    cols = weighted.shape[0]
    chunk = 256

    def kernel(chars_ref, tastes_ref, rows_ref, weight_ref, gate_ref, panel_ref, share_ref):
        people, weight = beside_ones(tastes_ref[...]), weight_ref[...]
        peak, ratio = rows_ref[0:1, :], rows_ref[1:2, :]
        for start in range(0, rows, chunk):
            scaled = jnp.exp(dot_nt(chars_ref[start : start + chunk, :], people) - peak) * ratio
            share_ref[start : start + chunk, :] = lane_groups(scaled)
            panel_ref[start : start + chunk, :] = dot_nt(scaled.astype(jnp.bfloat16), weight)

    return pl.pallas_call(
        kernel,
        grid=(1,),
        in_specs=[
            pl.BlockSpec((rows, depth), lambda i: (part, 0)),
            pl.BlockSpec(tastes.shape, lambda i: (0, 0)),
            pl.BlockSpec((3, consumers), lambda i: (0, 0)),
            pl.BlockSpec((cols, consumers), lambda i: (0, 0)),
            pl.BlockSpec(memory_space=pl.ANY),
        ],
        out_specs=[
            pl.BlockSpec((rows, cols), lambda i: (0, 0)),
            pl.BlockSpec((rows, 128), lambda i: (0, 0)),
        ],
        out_shape=[
            jax.ShapeDtypeStruct((rows, cols), jnp.float32),
            jax.ShapeDtypeStruct((rows, 128), jnp.float32),
        ],
        compiler_params=pltpu.CompilerParams(vmem_limit_bytes=VMEM_BYTES),
        cost_estimate=pl.CostEstimate(
            flops=2 * rows * consumers * (depth + cols), bytes_accessed=rows * cols * 8, transcendentals=rows * consumers
        ),
        name="panel",
    )(chars, tastes, row_values, weighted, gate)


def share_sums(chars, tastes, row_values, gate):
    rows, depth = chars.shape
    consumers = tastes.shape[0]
    block, chunk = 1024, 256

    def kernel(chars_ref, tastes_ref, rows_ref, gate_ref, share_ref):
        @pl.when(pl.program_id(0) == 0)
        def _():
            share_ref[...] = jnp.zeros_like(share_ref)

        people = beside_ones(tastes_ref[...])
        peak, ratio = rows_ref[0:1, :], rows_ref[1:2, :]
        for start in range(0, rows, chunk):
            scaled = jnp.exp(dot_nt(chars_ref[start : start + chunk, :], people) - peak) * ratio
            share_ref[start : start + chunk, :] += lane_groups(scaled)

    return pl.pallas_call(
        kernel,
        grid=(consumers // block,),
        in_specs=[
            pl.BlockSpec((rows, depth), lambda i: (0, 0)),
            pl.BlockSpec((block, tastes.shape[1]), lambda i: (i, 0)),
            pl.BlockSpec((3, block), lambda i: (0, i)),
            pl.BlockSpec(memory_space=pl.ANY),
        ],
        out_specs=pl.BlockSpec((rows, 128), lambda i: (0, 0)),
        out_shape=jax.ShapeDtypeStruct((rows, 128), jnp.float32),
        compiler_params=pltpu.CompilerParams(vmem_limit_bytes=VMEM_BYTES),
        name="share_sums",
    )(chars, tastes, row_values, gate)


def swap(value, axis, mask):
    size = lax.axis_size(axis)
    return lax.ppermute(value, axis, [(i, i ^ mask) for i in range(size)])


def butterfly_masks(size):
    masks, step = [], 1
    while step < size:
        masks.append(step)
        if step * 2 < size:
            masks.append(step * 3)
        step *= 4
    return masks


def body(tastes, price_coef, characteristics, mean_utility, panel_cols, firm_map, inverses):
    products, depth = characteristics.shape
    consumers = tastes.shape[0]
    cols = panel_cols.shape[0]
    holders = lax.axis_size("prod")
    per_pair = products // holders
    count_products = products * holders
    count_consumers = consumers * lax.axis_size("cons")
    base = lax.axis_index("prod") * products
    core = lax.axis_index("cons") % 2

    share_cols = cols // holders
    chars, message, order = prepare(
        characteristics,
        mean_utility.reshape(products // 128, 128),
        firm_map.reshape(1, products),
        (panel_cols - base).astype(jnp.float32).reshape(cols // 128, 128),
        holders,
    )
    first = lax.all_to_all(message.reshape(holders, 16, depth), "prod", split_axis=0, concat_axis=0, tiled=True)

    stat = stats(chars, tastes)

    odd = lax.axis_index("prod") % 2 == 1

    def own_lanes(values):
        return jnp.where(odd, values[..., per_pair:], values[..., :per_pair])

    high, low = own_lanes(first[:, 8, :]), own_lanes(first[:, 12, :])
    ids = high.astype(jnp.int32) * 256 + low.astype(jnp.int32)
    summed = jnp.sum(first.astype(jnp.float32), axis=0)
    tail = jnp.concatenate([jnp.zeros((5, depth), jnp.float32), summed[9:12], summed[:8]], axis=0)
    each = per_pair + 16
    sent, stat = pick_rows(ids.T, chars, tail, stat)
    second = lax.all_to_all(sent.reshape(holders, each, depth), "prod", split_axis=0, concat_axis=0, tiled=True)
    col_pieces = second[:: 128 // share_cols, per_pair + 5 : per_pair + 8, :].transpose(0, 2, 1).reshape(cols, 3)
    col_chars = second[:, per_pair + 8 :, :].reshape(cols, depth)
    col_chars = jnp.concatenate([col_chars, jnp.pad(col_pieces, ((0, 0), (1, depth - 4)))], axis=1)
    mean_rows = own_lanes(second[:, per_pair : per_pair + 4, :].astype(jnp.float32))
    mean_rows = jnp.pad(mean_rows, ((0, 0), (0, 4), (0, 0))).transpose(1, 0, 2).reshape(8, products)
    half = products // 2
    place = (order // half == core).astype(jnp.int32) * half + order % half

    def join(stat, masks):
        for mask in masks:
            other = swap(stat, "prod", mask)
            joint = jnp.maximum(stat[0], other[0])
            total = stat[1] * jnp.exp(stat[0] - joint) + other[1] * jnp.exp(other[0] - joint)
            stat = jnp.stack([joint, total])
        return stat

    masks = butterfly_masks(holders)
    taken = panel_cols[0] >= 0
    stat = lax.cond(taken, lambda value: join(value, masks), lambda value: value, stat)
    firm_chars = place_rows(
        place.reshape(1, products), second.reshape(holders * each, depth), mean_rows, holders, stat
    )
    peak = jnp.maximum(stat[0], 0.0)
    denom = jnp.exp(-peak) + stat[1] * jnp.exp(stat[0] - peak)
    ratio = count_products / denom

    row_values = jnp.stack([peak, ratio, price_coef])
    given, given_share, weighted = first_panel(firm_chars, 2, tastes, row_values, col_chars)
    got = swap(given, "cons", 1)
    kept, kept_share = panel(firm_chars, 1, 2, tastes, row_values, weighted, given)
    diagonal = given[half] + got[half]
    room = 32768.0 / (count_products * jnp.maximum(diagonal, 1e-25))
    fitted = (kept + got[:half]) * room[None, :]
    chip_sum, gate = lax.optimization_barrier((fitted.astype(jnp.float16), jnp.max(fitted, axis=0, keepdims=True)))
    other_sum = swap(chip_sum, "cons", 2)

    given_share, kept_share = jnp.sum(given_share, axis=1), jnp.sum(kept_share, axis=1)
    first_half = jnp.where(core == 0, kept_share, given_share)
    second_half = jnp.where(core == 0, given_share, kept_share)

    def own_and_exchange(gate, others):
        own_shares = jnp.sum(share_sums(chars, tastes, row_values, gate), axis=1)
        sums = jnp.concatenate([own_shares, others])
        sums = sums + swap(sums, "cons", 1)
        return sums, swap(sums, "cons", 2)

    sums, other_sums = lax.cond(
        taken,
        own_and_exchange,
        lambda gate, others: (jnp.zeros(products + others.shape[0], jnp.float32),) * 2,
        gate,
        jnp.concatenate([first_half, second_half, given[half]]),
    )
    other_diagonal = other_sums[2 * products :]
    sums = (sums + other_sums) / count_consumers
    shares, firm_shares = sums[:products], sums[products : 2 * products]

    firm_count, block_size = inverses.shape[0], inverses.shape[1]
    own_inverses = lax.dynamic_slice_in_dim(inverses, core * (firm_count // 2), firm_count // 2, 0)
    firm_ids = lax.dynamic_slice_in_dim(firm_map, core * half, half, 0)
    other_room = 32768.0 / (count_products * jnp.maximum(other_diagonal, 1e-25))
    unfit, other_unfit = 1.0 / (room * count_consumers), 1.0 / (other_room * count_consumers)
    cross = chip_sum.astype(jnp.float32) * unfit[None, :] + other_sum.astype(jnp.float32) * other_unfit[None, :]
    diagonal = (diagonal + other_diagonal) / count_consumers
    jacobian = cross - jnp.where(firm_ids[:, None] == panel_cols[None, :], diagonal[None, :], 0.0)
    mine = jnp.einsum(
        "fab,fbc->fac",
        own_inverses,
        jacobian.reshape(firm_count // 2, block_size, cols),
        precision=lax.Precision.HIGHEST,
    ).reshape(half, cols)
    theirs = swap(mine, "cons", 1)
    response = jnp.where(core == 0, jnp.concatenate([mine, theirs]), jnp.concatenate([theirs, mine]))
    markup = jnp.sum(inverses * firm_shares.reshape(firm_count, 1, block_size), axis=2).reshape(products)
    return (shares, markup, response)


def solution(mesh):
    return jax.shard_map(
        body,
        mesh=mesh,
        in_specs=(
            P("cons", None),
            P("cons"),
            P("prod", None),
            P("prod"),
            P(),
            P("prod"),
            P("prod", None, None),
        ),
        out_specs=(P("prod"), P("prod"), P("prod", None)),
        check_vma=False,
    )
```

```python
import jax
import jax.numpy as jnp
from jax import lax
from jax.experimental import pallas as pl
from jax.experimental.pallas import tpu as pltpu
from jax.sharding import PartitionSpec as P

NT = (((1,), (1,)), ((), ()))
VMEM_BYTES = 24 * 1024 * 1024


def dot_nt(left, right):
    return lax.dot_general(left, right, NT, preferred_element_type=jnp.float32)


def rounded(values):
    return values.astype(jnp.bfloat16).astype(jnp.float32)


def prepare(characteristics, means, firm_row, panel_rows, holders):
    rows, depth = characteristics.shape
    per_pair = rows // holders
    cols = panel_rows.shape[0] * 128
    share_cols = cols // holders
    chunk = 256

    def kernel(chars_ref, means_ref, firm_ref, panel_ref, both_ref, message_ref, order_ref):
        lane = lax.broadcasted_iota(jnp.int32, (128, 128), 1)
        values = means_ref[...]
        high = rounded(values)
        middle = rounded(values - high)
        low = values - high - middle
        pieces = jnp.concatenate([high, middle, low, jnp.zeros((128 - 3 * values.shape[0], 128), jnp.float32)], axis=0).T
        count = values.shape[0]
        both_ref[:, :depth] = chars_ref[...]
        for k in range(count):
            beside = jnp.zeros((128, 128), jnp.float32)
            for piece in range(3):
                place = piece * count + k
                beside = jnp.where(lane == piece + 1, pieces[:, place : place + 1], beside)
            both_ref[k * 128 : (k + 1) * 128, depth:] = beside.astype(jnp.bfloat16)

        firm = firm_ref[...]
        holder, wanted = firm // rows, firm % rows
        holder_id = lax.broadcasted_iota(jnp.int32, (holders, rows), 0)
        named = jnp.where(holder_id == holder, 1.0, 0.0)
        blocks = [named[:, start : start + 128] for start in range(0, rows, 128)]
        before = (lax.broadcasted_iota(jnp.int32, (128, 128), 0) < lane).astype(jnp.float32).astype(jnp.bfloat16)
        counts = jnp.dot(
            jnp.concatenate(blocks, axis=0).astype(jnp.bfloat16), before, preferred_element_type=jnp.float32
        )
        seen = jnp.zeros((holders, 1), jnp.float32)
        ranks = []
        for k, block in enumerate(blocks):
            rank = counts[k * holders : (k + 1) * holders, :] + seen
            ranks.append(jnp.sum(block * rank, axis=0, keepdims=True))
            seen = seen + jnp.sum(block, axis=1, keepdims=True)
        slot = holder * per_pair + jnp.concatenate(ranks, axis=1).astype(jnp.int32)

        row = lax.broadcasted_iota(jnp.int32, (8, rows), 0)
        firm_place = lax.broadcasted_iota(jnp.int32, (8, rows), 1)
        digits = jnp.where(row == 0, wanted // 256, jnp.where(row == 1, wanted % 256, 0))
        digits = jnp.where(row == 2, firm_place // 256, jnp.where(row == 3, firm_place % 256, digits))
        digits = jnp.concatenate([digits, jnp.zeros_like(digits)], axis=0).astype(jnp.float32).astype(jnp.bfloat16)
        asked = []
        for start in range(0, rows, chunk):
            slots = start + lax.broadcasted_iota(jnp.int32, (chunk, rows), 0)
            hot = jnp.where(slots == slot, 1.0, 0.0).astype(jnp.bfloat16)
            found = dot_nt(digits, hot)
            order_ref[:, start : start + chunk] = (found[2:3, :] * 256.0 + found[3:4, :]).astype(jnp.int32)
            asked.append(found)

        products = lax.broadcasted_iota(jnp.int32, (128, rows), 1).astype(jnp.float32)
        both = both_ref[...]
        wide = jnp.concatenate([panel_ref[...], jnp.zeros((128 - panel_ref.shape[0], 128), jnp.float32)], axis=0).T
        part_row = lax.broadcasted_iota(jnp.int32, (8, 128), 0)
        for k in range(cols // 128):
            hot = jnp.where(wide[:, k : k + 1] == products, 1.0, 0.0).astype(jnp.bfloat16)
            part = jnp.dot(hot, both, preferred_element_type=jnp.float32)
            part_pieces = part[:, depth:].T[:8, :]
            for place in range(128 // share_cols):
                q = k * (128 // share_cols) + place
                start = q * per_pair // 128 * 128 % chunk
                found = asked[q * per_pair // chunk][:, start : start + 128]
                extra = jnp.where(part_row == 0, found[0:1, :], jnp.where(part_row == 4, found[1:2, :], part_pieces))
                mine = part[place * share_cols : (place + 1) * share_cols, :depth]
                message_ref[q * 16 : (q + 1) * 16, :] = jnp.concatenate([mine, extra], axis=0).astype(jnp.bfloat16)

    def whole(shape):
        return pl.BlockSpec(shape, lambda i: (0, 0))

    return pl.pallas_call(
        kernel,
        grid=(1,),
        in_specs=[whole(value.shape) for value in (characteristics, means, firm_row, panel_rows)],
        out_specs=[whole((rows, 2 * depth)), whole((16 * holders, depth)), whole((1, rows))],
        out_shape=[
            jax.ShapeDtypeStruct((rows, 2 * depth), jnp.bfloat16),
            jax.ShapeDtypeStruct((16 * holders, depth), jnp.bfloat16),
            jax.ShapeDtypeStruct((1, rows), jnp.int32),
        ],
        compiler_params=pltpu.CompilerParams(vmem_limit_bytes=60 * 1024 * 1024),
        name="prepare",
    )(characteristics, means, firm_row, panel_rows)


def beside_ones(tastes):
    lane = lax.broadcasted_iota(jnp.int32, tastes.shape, 1)
    ones = jnp.where((lane >= 1) & (lane <= 3), 1.0, 0.0)
    return jnp.concatenate([tastes, ones.astype(tastes.dtype)], axis=1)


def stats(chars, tastes):
    rows, depth = chars.shape
    consumers = tastes.shape[0]
    block, chunk = 2048, 256

    def kernel(chars_ref, tastes_ref, stat_ref):
        people = beside_ones(tastes_ref[...])
        peak = jnp.full((1, block), -jnp.inf, jnp.float32)
        total = jnp.zeros((8, block), jnp.float32)
        for start in range(0, rows, chunk):
            util = dot_nt(chars_ref[start : start + chunk, :], people)
            highest = jnp.max(util.reshape(chunk // 8, 8, block), axis=0)
            joint = jnp.maximum(peak, jnp.max(highest, axis=0, keepdims=True))
            expo = jnp.exp(util - joint)
            total = total * jnp.exp(peak - joint) + jnp.sum(expo.reshape(chunk // 8, 8, block), axis=0)
            peak = joint
        stat_ref[0:1, :] = peak
        stat_ref[1:2, :] = jnp.sum(total, axis=0, keepdims=True)

    return pl.pallas_call(
        kernel,
        grid=(consumers // block,),
        in_specs=[
            pl.BlockSpec((rows, depth), lambda i: (0, 0)),
            pl.BlockSpec((block, tastes.shape[1]), lambda i: (i, 0)),
        ],
        out_specs=pl.BlockSpec((2, block), lambda i: (0, i)),
        out_shape=jax.ShapeDtypeStruct((2, consumers), jnp.float32),
        compiler_params=pltpu.CompilerParams(vmem_limit_bytes=VMEM_BYTES),
        name="stats",
    )(chars, tastes)


def pick_rows(ids_t, chars, tail, stat):
    per_pair, holders = ids_t.shape
    rows, depth = chars.shape
    each = per_pair + 16
    group, pair = 256 // per_pair, 128 // per_pair

    def kernel(ids_ref, chars_ref, tail_ref, stat_ref, out_ref, stat_out_ref):
        stat_out_ref[...] = stat_ref[...]
        lanes = lax.broadcasted_iota(jnp.int32, (per_pair, rows), 1)
        table = chars_ref[...]
        for start in range(0, holders, group):
            span = range(start, start + group)
            marks = [jnp.where(ids_ref[:, q : q + 1] == lanes, 1.0, 0.0).astype(jnp.bfloat16) for q in span]
            picked = jnp.dot(jnp.concatenate(marks, axis=0), table, preferred_element_type=jnp.float32)
            for place, q in enumerate(span):
                if place % pair == 0:
                    beside = picked[place * per_pair : (place + pair) * per_pair, 128:].T[:8, :]
                    block = jnp.concatenate([beside + tail_ref[0:8, :], tail_ref[8:16, :]], axis=0).astype(jnp.bfloat16)
                mine = picked[place * per_pair : (place + 1) * per_pair, :128]
                out_ref[q * each : q * each + per_pair, :] = mine.astype(jnp.bfloat16)
                out_ref[q * each + per_pair : (q + 1) * each, :] = block

    return pl.pallas_call(
        kernel,
        out_shape=[
            jax.ShapeDtypeStruct((each * holders, depth // 2), jnp.bfloat16),
            jax.ShapeDtypeStruct(stat.shape, stat.dtype),
        ],
        compiler_params=pltpu.CompilerParams(vmem_limit_bytes=VMEM_BYTES),
        name="pick_rows",
    )(ids_t, chars, tail, stat)


def place_rows(order, received, beside, holders, gate):
    rows = order.shape[1]
    total, depth = received.shape
    per_pair, each = rows // holders, total // holders
    chunk = 256

    def kernel(order_ref, received_ref, beside_ref, gate_ref, out_ref):
        order_row = order_ref[...]
        table = jnp.concatenate([received_ref[q * each : q * each + per_pair, :] for q in range(holders)], axis=0)
        blank = jnp.zeros((120, 128), jnp.float32)
        columns = [
            jnp.concatenate([beside_ref[:, start : start + 128], blank], axis=0).T.astype(jnp.bfloat16)
            for start in range(0, rows, 128)
        ]
        table = jnp.concatenate([table, jnp.concatenate(columns, axis=0)], axis=1)
        for start in range(0, rows, chunk):
            ids = start + lax.broadcasted_iota(jnp.int32, (chunk, rows), 0)
            hot = jnp.where(ids == order_row, 1.0, 0.0).astype(jnp.bfloat16)
            placed = jnp.dot(hot, table, preferred_element_type=jnp.float32)
            out_ref[start : start + chunk, :] = placed.astype(jnp.bfloat16)

    return pl.pallas_call(
        kernel,
        in_specs=[pl.BlockSpec(memory_space=pltpu.VMEM)] * 3 + [pl.BlockSpec(memory_space=pl.ANY)],
        out_shape=jax.ShapeDtypeStruct((rows, 2 * depth), jnp.bfloat16),
        compiler_params=pltpu.CompilerParams(vmem_limit_bytes=VMEM_BYTES),
        name="place_rows",
    )(order, received, beside, gate)


def lane_groups(values):
    total = values[:, 0:128]
    for start in range(128, values.shape[1], 128):
        total = total + values[:, start : start + 128]
    return total


def first_panel(chars, parts, tastes, row_values, col_chars):
    rows, depth = chars.shape[0] // parts, chars.shape[1]
    consumers = tastes.shape[0]
    cols = col_chars.shape[0]
    block, chunk = 1024, 256

    def kernel(chars_ref, tastes_ref, rows_ref, cols_ref, panel_ref, share_ref, weight_ref, diag_ref):
        step = pl.program_id(0)

        @pl.when(step == 0)
        def _():
            panel_ref[...] = jnp.zeros_like(panel_ref)
            share_ref[...] = jnp.zeros_like(share_ref)
            diag_ref[...] = jnp.zeros_like(diag_ref)

        people = beside_ones(tastes_ref[...])
        peak, ratio = rows_ref[0:1, :], rows_ref[1:2, :]
        weighted = rows_ref[2:3, :] * (jnp.exp(dot_nt(cols_ref[...], people) - peak) * ratio)
        diag_ref[...] += lane_groups(weighted)
        weight = weighted.astype(jnp.bfloat16)
        weight_ref[...] = weight
        for start in range(0, rows, chunk):
            scaled = jnp.exp(dot_nt(chars_ref[start : start + chunk, :], people) - peak) * ratio
            share_ref[start : start + chunk, :] += lane_groups(scaled)
            panel_ref[start : start + chunk, :] += dot_nt(scaled.astype(jnp.bfloat16), weight)

        @pl.when(step == pl.num_programs(0) - 1)
        def _():
            total = jnp.sum(diag_ref[...].T, axis=0, keepdims=True)
            panel_ref[rows:, :] = jnp.broadcast_to(total, (8, cols))

    return pl.pallas_call(
        kernel,
        grid=(consumers // block,),
        in_specs=[
            pl.BlockSpec((rows, depth), lambda i: (0, 0)),
            pl.BlockSpec((block, tastes.shape[1]), lambda i: (i, 0)),
            pl.BlockSpec((3, block), lambda i: (0, i)),
            pl.BlockSpec((cols, depth), lambda i: (0, 0)),
        ],
        out_specs=[
            pl.BlockSpec((rows + 8, cols), lambda i: (0, 0)),
            pl.BlockSpec((rows, 128), lambda i: (0, 0)),
            pl.BlockSpec((cols, block), lambda i: (0, i)),
        ],
        scratch_shapes=[pltpu.VMEM((cols, 128), jnp.float32)],
        out_shape=[
            jax.ShapeDtypeStruct((rows + 8, cols), jnp.float32),
            jax.ShapeDtypeStruct((rows, 128), jnp.float32),
            jax.ShapeDtypeStruct((cols, consumers), jnp.bfloat16),
        ],
        compiler_params=pltpu.CompilerParams(vmem_limit_bytes=VMEM_BYTES),
        cost_estimate=pl.CostEstimate(
            flops=2 * rows * consumers * (depth + cols), bytes_accessed=rows * cols * 8, transcendentals=rows * consumers
        ),
        name="first_panel",
    )(chars, tastes, row_values, col_chars)


def panel(chars, part, parts, tastes, row_values, weighted, gate):
    rows, depth = chars.shape[0] // parts, chars.shape[1]
    consumers = tastes.shape[0]
    cols = weighted.shape[0]
    chunk = 256

    def kernel(chars_ref, tastes_ref, rows_ref, weight_ref, gate_ref, panel_ref, share_ref):
        people, weight = beside_ones(tastes_ref[...]), weight_ref[...]
        peak, ratio = rows_ref[0:1, :], rows_ref[1:2, :]
        for start in range(0, rows, chunk):
            scaled = jnp.exp(dot_nt(chars_ref[start : start + chunk, :], people) - peak) * ratio
            share_ref[start : start + chunk, :] = lane_groups(scaled)
            panel_ref[start : start + chunk, :] = dot_nt(scaled.astype(jnp.bfloat16), weight)

    return pl.pallas_call(
        kernel,
        grid=(1,),
        in_specs=[
            pl.BlockSpec((rows, depth), lambda i: (part, 0)),
            pl.BlockSpec(tastes.shape, lambda i: (0, 0)),
            pl.BlockSpec((3, consumers), lambda i: (0, 0)),
            pl.BlockSpec((cols, consumers), lambda i: (0, 0)),
            pl.BlockSpec(memory_space=pl.ANY),
        ],
        out_specs=[
            pl.BlockSpec((rows, cols), lambda i: (0, 0)),
            pl.BlockSpec((rows, 128), lambda i: (0, 0)),
        ],
        out_shape=[
            jax.ShapeDtypeStruct((rows, cols), jnp.float32),
            jax.ShapeDtypeStruct((rows, 128), jnp.float32),
        ],
        compiler_params=pltpu.CompilerParams(vmem_limit_bytes=VMEM_BYTES),
        cost_estimate=pl.CostEstimate(
            flops=2 * rows * consumers * (depth + cols), bytes_accessed=rows * cols * 8, transcendentals=rows * consumers
        ),
        name="panel",
    )(chars, tastes, row_values, weighted, gate)


def share_sums(chars, tastes, row_values, gate):
    rows, depth = chars.shape
    consumers = tastes.shape[0]
    block, chunk = 1024, 256

    def kernel(chars_ref, tastes_ref, rows_ref, gate_ref, share_ref):
        @pl.when(pl.program_id(0) == 0)
        def _():
            share_ref[...] = jnp.zeros_like(share_ref)

        people = beside_ones(tastes_ref[...])
        peak, ratio = rows_ref[0:1, :], rows_ref[1:2, :]
        for start in range(0, rows, chunk):
            scaled = jnp.exp(dot_nt(chars_ref[start : start + chunk, :], people) - peak) * ratio
            share_ref[start : start + chunk, :] += lane_groups(scaled)

    return pl.pallas_call(
        kernel,
        grid=(consumers // block,),
        in_specs=[
            pl.BlockSpec((rows, depth), lambda i: (0, 0)),
            pl.BlockSpec((block, tastes.shape[1]), lambda i: (i, 0)),
            pl.BlockSpec((3, block), lambda i: (0, i)),
            pl.BlockSpec(memory_space=pl.ANY),
        ],
        out_specs=pl.BlockSpec((rows, 128), lambda i: (0, 0)),
        out_shape=jax.ShapeDtypeStruct((rows, 128), jnp.float32),
        compiler_params=pltpu.CompilerParams(vmem_limit_bytes=VMEM_BYTES),
        name="share_sums",
    )(chars, tastes, row_values, gate)


def swap(value, axis, mask):
    size = lax.axis_size(axis)
    return lax.ppermute(value, axis, [(i, i ^ mask) for i in range(size)])


def butterfly_masks(size):
    masks, step = [], 1
    while step < size:
        masks.append(step)
        if step * 2 < size:
            masks.append(step * 3)
        step *= 4
    return masks


def body(tastes, price_coef, characteristics, mean_utility, panel_cols, firm_map, inverses):
    products, depth = characteristics.shape
    consumers = tastes.shape[0]
    cols = panel_cols.shape[0]
    holders = lax.axis_size("prod")
    per_pair = products // holders
    count_products = products * holders
    count_consumers = consumers * lax.axis_size("cons")
    base = lax.axis_index("prod") * products
    core = lax.axis_index("cons") % 2

    share_cols = cols // holders
    chars, message, order = prepare(
        characteristics,
        mean_utility.reshape(products // 128, 128),
        firm_map.reshape(1, products),
        (panel_cols - base).astype(jnp.float32).reshape(cols // 128, 128),
        holders,
    )
    first = lax.all_to_all(message.reshape(holders, 16, depth), "prod", split_axis=0, concat_axis=0, tiled=True)

    stat = stats(chars, tastes)

    odd = lax.axis_index("prod") % 2 == 1

    def own_lanes(values):
        return jnp.where(odd, values[..., per_pair:], values[..., :per_pair])

    high, low = own_lanes(first[:, 8, :]), own_lanes(first[:, 12, :])
    ids = high.astype(jnp.int32) * 256 + low.astype(jnp.int32)
    summed = jnp.sum(first.astype(jnp.float32), axis=0)
    tail = jnp.concatenate([jnp.zeros((5, depth), jnp.float32), summed[9:12], summed[:8]], axis=0)
    each = per_pair + 16
    sent, stat = pick_rows(ids.T, chars, tail, stat)
    second = lax.all_to_all(sent.reshape(holders, each, depth), "prod", split_axis=0, concat_axis=0, tiled=True)
    col_pieces = second[:: 128 // share_cols, per_pair + 5 : per_pair + 8, :].transpose(0, 2, 1).reshape(cols, 3)
    col_chars = second[:, per_pair + 8 :, :].reshape(cols, depth)
    col_chars = jnp.concatenate([col_chars, jnp.pad(col_pieces, ((0, 0), (1, depth - 4)))], axis=1)
    mean_rows = own_lanes(second[:, per_pair : per_pair + 4, :].astype(jnp.float32))
    mean_rows = jnp.pad(mean_rows, ((0, 0), (0, 4), (0, 0))).transpose(1, 0, 2).reshape(8, products)
    half = products // 2
    place = (order // half == core).astype(jnp.int32) * half + order % half

    def join(stat, masks):
        peak, total = stat[0], stat[1]
        for mask in masks:
            other = swap(jnp.concatenate([peak, total]), "prod", mask)
            other_peak, other_total = other[:consumers], other[consumers:]
            joint = jnp.maximum(peak, other_peak)
            total = total * jnp.exp(peak - joint) + other_total * jnp.exp(other_peak - joint)
            peak = joint
        return peak, total

    masks = butterfly_masks(holders)
    taken = panel_cols[0] >= 0
    high, total = lax.cond(taken, lambda value: join(value, masks), lambda value: (value[0], value[1]), stat)
    peak = jnp.maximum(high, 0.0)
    denom = jnp.exp(-peak) + total * jnp.exp(high - peak)
    ratio = count_products / denom
    row_values = jnp.stack([peak, ratio, price_coef])
    firm_chars = place_rows(
        place.reshape(1, products), second.reshape(holders * each, depth), mean_rows, holders, row_values
    )
    given, given_share, weighted = first_panel(firm_chars, 2, tastes, row_values, col_chars)
    got = swap(given, "cons", 1)
    kept, kept_share = panel(firm_chars, 1, 2, tastes, row_values, weighted, given)
    diagonal = given[half] + got[half]
    room = 32768.0 / (count_products * jnp.maximum(diagonal, 1e-25))
    fitted = (kept + got[:half]) * room[None, :]
    chip_sum, gate = lax.optimization_barrier((fitted.astype(jnp.float16), jnp.max(fitted, axis=0, keepdims=True)))
    other_sum = swap(chip_sum, "cons", 2)

    given_share, kept_share = jnp.sum(given_share, axis=1), jnp.sum(kept_share, axis=1)
    first_half = jnp.where(core == 0, kept_share, given_share)
    second_half = jnp.where(core == 0, given_share, kept_share)

    def own_and_exchange(gate, others):
        own_shares = jnp.sum(share_sums(chars, tastes, row_values, gate), axis=1)
        sums = jnp.concatenate([own_shares, others])
        sums = sums + swap(sums, "cons", 1)
        return sums, swap(sums, "cons", 2)

    sums, other_sums = lax.cond(
        taken,
        own_and_exchange,
        lambda gate, others: (jnp.zeros(products + others.shape[0], jnp.float32),) * 2,
        gate,
        jnp.concatenate([first_half, second_half, given[half]]),
    )
    other_diagonal = other_sums[2 * products :]
    sums = (sums + other_sums) / count_consumers
    shares, firm_shares = sums[:products], sums[products : 2 * products]

    firm_count, block_size = inverses.shape[0], inverses.shape[1]
    own_inverses = lax.dynamic_slice_in_dim(inverses, core * (firm_count // 2), firm_count // 2, 0)
    firm_ids = lax.dynamic_slice_in_dim(firm_map, core * half, half, 0)
    other_room = 32768.0 / (count_products * jnp.maximum(other_diagonal, 1e-25))
    unfit, other_unfit = 1.0 / (room * count_consumers), 1.0 / (other_room * count_consumers)
    cross = chip_sum.astype(jnp.float32) * unfit[None, :] + other_sum.astype(jnp.float32) * other_unfit[None, :]
    diagonal = (diagonal + other_diagonal) / count_consumers
    jacobian = cross - jnp.where(firm_ids[:, None] == panel_cols[None, :], diagonal[None, :], 0.0)
    mine = jnp.einsum(
        "fab,fbc->fac",
        own_inverses,
        jacobian.reshape(firm_count // 2, block_size, cols),
        precision=lax.Precision.HIGHEST,
    ).reshape(half, cols)
    theirs = swap(mine, "cons", 1)
    response = jnp.where(core == 0, jnp.concatenate([mine, theirs]), jnp.concatenate([theirs, mine]))
    markup = jnp.sum(inverses * firm_shares.reshape(firm_count, 1, block_size), axis=2).reshape(products)
    return (shares, markup, response)


def solution(mesh):
    return jax.shard_map(
        body,
        mesh=mesh,
        in_specs=(
            P("cons", None),
            P("cons"),
            P("prod", None),
            P("prod"),
            P(),
            P("prod"),
            P("prod", None, None),
        ),
        out_specs=(P("prod"), P("prod"), P("prod", None)),
        check_vma=False,
    )
```

```python
import jax
import jax.numpy as jnp
from jax import lax
from jax.experimental import pallas as pl
from jax.experimental.pallas import tpu as pltpu
from jax.sharding import PartitionSpec as P

NT = (((1,), (1,)), ((), ()))
VMEM_BYTES = 24 * 1024 * 1024


def dot_nt(left, right):
    return lax.dot_general(left, right, NT, preferred_element_type=jnp.float32)


def rounded(values):
    return values.astype(jnp.bfloat16).astype(jnp.float32)


def prepare(characteristics, means, firm_row, panel_rows, holders):
    rows, depth = characteristics.shape
    per_pair = rows // holders
    cols = panel_rows.shape[0] * 128
    share_cols = cols // holders
    chunk = 256

    def kernel(chars_ref, means_ref, firm_ref, panel_ref, both_ref, message_ref, order_ref):
        lane = lax.broadcasted_iota(jnp.int32, (128, 128), 1)
        values = means_ref[...]
        high = rounded(values)
        middle = rounded(values - high)
        low = values - high - middle
        pieces = jnp.concatenate([high, middle, low, jnp.zeros((128 - 3 * values.shape[0], 128), jnp.float32)], axis=0).T
        count = values.shape[0]
        both_ref[:, :depth] = chars_ref[...]
        for k in range(count):
            beside = jnp.zeros((128, 128), jnp.float32)
            for piece in range(3):
                place = piece * count + k
                beside = jnp.where(lane == piece + 1, pieces[:, place : place + 1], beside)
            both_ref[k * 128 : (k + 1) * 128, depth:] = beside.astype(jnp.bfloat16)

        firm = firm_ref[...]
        holder, wanted = firm // rows, firm % rows
        holder_id = lax.broadcasted_iota(jnp.int32, (holders, rows), 0)
        named = jnp.where(holder_id == holder, 1.0, 0.0)
        blocks = [named[:, start : start + 128] for start in range(0, rows, 128)]
        before = (lax.broadcasted_iota(jnp.int32, (128, 128), 0) < lane).astype(jnp.float32).astype(jnp.bfloat16)
        counts = jnp.dot(
            jnp.concatenate(blocks, axis=0).astype(jnp.bfloat16), before, preferred_element_type=jnp.float32
        )
        seen = jnp.zeros((holders, 1), jnp.float32)
        ranks = []
        for k, block in enumerate(blocks):
            rank = counts[k * holders : (k + 1) * holders, :] + seen
            ranks.append(jnp.sum(block * rank, axis=0, keepdims=True))
            seen = seen + jnp.sum(block, axis=1, keepdims=True)
        slot = holder * per_pair + jnp.concatenate(ranks, axis=1).astype(jnp.int32)

        row = lax.broadcasted_iota(jnp.int32, (8, rows), 0)
        firm_place = lax.broadcasted_iota(jnp.int32, (8, rows), 1)
        digits = jnp.where(row == 0, wanted // 256, jnp.where(row == 1, wanted % 256, 0))
        digits = jnp.where(row == 2, firm_place // 256, jnp.where(row == 3, firm_place % 256, digits))
        digits = jnp.concatenate([digits, jnp.zeros_like(digits)], axis=0).astype(jnp.float32).astype(jnp.bfloat16)
        asked = []
        for start in range(0, rows, chunk):
            slots = start + lax.broadcasted_iota(jnp.int32, (chunk, rows), 0)
            hot = jnp.where(slots == slot, 1.0, 0.0).astype(jnp.bfloat16)
            found = dot_nt(digits, hot)
            order_ref[:, start : start + chunk] = (found[2:3, :] * 256.0 + found[3:4, :]).astype(jnp.int32)
            asked.append(found)

        products = lax.broadcasted_iota(jnp.int32, (128, rows), 1).astype(jnp.float32)
        both = both_ref[...]
        wide = jnp.concatenate([panel_ref[...], jnp.zeros((128 - panel_ref.shape[0], 128), jnp.float32)], axis=0).T
        part_row = lax.broadcasted_iota(jnp.int32, (8, 128), 0)
        for k in range(cols // 128):
            hot = jnp.where(wide[:, k : k + 1] == products, 1.0, 0.0).astype(jnp.bfloat16)
            part = jnp.dot(hot, both, preferred_element_type=jnp.float32)
            part_pieces = part[:, depth:].T[:8, :]
            for place in range(128 // share_cols):
                q = k * (128 // share_cols) + place
                start = q * per_pair // 128 * 128 % chunk
                found = asked[q * per_pair // chunk][:, start : start + 128]
                extra = jnp.where(part_row == 0, found[0:1, :], jnp.where(part_row == 4, found[1:2, :], part_pieces))
                mine = part[place * share_cols : (place + 1) * share_cols, :depth]
                message_ref[q * 16 : (q + 1) * 16, :] = jnp.concatenate([mine, extra], axis=0).astype(jnp.bfloat16)

    def whole(shape):
        return pl.BlockSpec(shape, lambda i: (0, 0))

    return pl.pallas_call(
        kernel,
        grid=(1,),
        in_specs=[whole(value.shape) for value in (characteristics, means, firm_row, panel_rows)],
        out_specs=[whole((rows, 2 * depth)), whole((16 * holders, depth)), whole((1, rows))],
        out_shape=[
            jax.ShapeDtypeStruct((rows, 2 * depth), jnp.bfloat16),
            jax.ShapeDtypeStruct((16 * holders, depth), jnp.bfloat16),
            jax.ShapeDtypeStruct((1, rows), jnp.int32),
        ],
        compiler_params=pltpu.CompilerParams(vmem_limit_bytes=60 * 1024 * 1024),
        name="prepare",
    )(characteristics, means, firm_row, panel_rows)


def beside_ones(tastes):
    lane = lax.broadcasted_iota(jnp.int32, tastes.shape, 1)
    ones = jnp.where((lane >= 1) & (lane <= 3), 1.0, 0.0)
    return jnp.concatenate([tastes, ones.astype(tastes.dtype)], axis=1)


def stats(chars, tastes):
    rows, depth = chars.shape
    consumers = tastes.shape[0]
    block, chunk = 2048, 256

    def kernel(chars_ref, tastes_ref, stat_ref):
        people = beside_ones(tastes_ref[...])
        peak = jnp.full((1, block), -jnp.inf, jnp.float32)
        total = jnp.zeros((8, block), jnp.float32)
        for start in range(0, rows, chunk):
            util = dot_nt(chars_ref[start : start + chunk, :], people)
            highest = jnp.max(util.reshape(chunk // 8, 8, block), axis=0)
            joint = jnp.maximum(peak, jnp.max(highest, axis=0, keepdims=True))
            expo = jnp.exp(util - joint)
            total = total * jnp.exp(peak - joint) + jnp.sum(expo.reshape(chunk // 8, 8, block), axis=0)
            peak = joint
        stat_ref[...] = peak + jnp.log(jnp.sum(total, axis=0, keepdims=True))

    return pl.pallas_call(
        kernel,
        grid=(consumers // block,),
        in_specs=[
            pl.BlockSpec((rows, depth), lambda i: (0, 0)),
            pl.BlockSpec((block, tastes.shape[1]), lambda i: (i, 0)),
        ],
        out_specs=pl.BlockSpec((1, block), lambda i: (0, i)),
        out_shape=jax.ShapeDtypeStruct((1, consumers), jnp.float32),
        compiler_params=pltpu.CompilerParams(vmem_limit_bytes=VMEM_BYTES),
        name="stats",
    )(chars, tastes)


def pick_rows(ids_t, chars, tail, stat):
    per_pair, holders = ids_t.shape
    rows, depth = chars.shape
    each = per_pair + 16
    group, pair = 256 // per_pair, 128 // per_pair

    def kernel(ids_ref, chars_ref, tail_ref, stat_ref, out_ref, stat_out_ref):
        stat_out_ref[...] = stat_ref[...]
        lanes = lax.broadcasted_iota(jnp.int32, (per_pair, rows), 1)
        table = chars_ref[...]
        for start in range(0, holders, group):
            span = range(start, start + group)
            marks = [jnp.where(ids_ref[:, q : q + 1] == lanes, 1.0, 0.0).astype(jnp.bfloat16) for q in span]
            picked = jnp.dot(jnp.concatenate(marks, axis=0), table, preferred_element_type=jnp.float32)
            for place, q in enumerate(span):
                if place % pair == 0:
                    beside = picked[place * per_pair : (place + pair) * per_pair, 128:].T[:8, :]
                    block = jnp.concatenate([beside + tail_ref[0:8, :], tail_ref[8:16, :]], axis=0).astype(jnp.bfloat16)
                mine = picked[place * per_pair : (place + 1) * per_pair, :128]
                out_ref[q * each : q * each + per_pair, :] = mine.astype(jnp.bfloat16)
                out_ref[q * each + per_pair : (q + 1) * each, :] = block

    return pl.pallas_call(
        kernel,
        out_shape=[
            jax.ShapeDtypeStruct((each * holders, depth // 2), jnp.bfloat16),
            jax.ShapeDtypeStruct(stat.shape, stat.dtype),
        ],
        compiler_params=pltpu.CompilerParams(vmem_limit_bytes=VMEM_BYTES),
        name="pick_rows",
    )(ids_t, chars, tail, stat)


def place_rows(order, received, beside, holders, gate):
    rows = order.shape[1]
    total, depth = received.shape
    per_pair, each = rows // holders, total // holders
    chunk = 256

    def kernel(order_ref, received_ref, beside_ref, gate_ref, out_ref):
        order_row = order_ref[...]
        table = jnp.concatenate([received_ref[q * each : q * each + per_pair, :] for q in range(holders)], axis=0)
        blank = jnp.zeros((120, 128), jnp.float32)
        columns = [
            jnp.concatenate([beside_ref[:, start : start + 128], blank], axis=0).T.astype(jnp.bfloat16)
            for start in range(0, rows, 128)
        ]
        table = jnp.concatenate([table, jnp.concatenate(columns, axis=0)], axis=1)
        for start in range(0, rows, chunk):
            ids = start + lax.broadcasted_iota(jnp.int32, (chunk, rows), 0)
            hot = jnp.where(ids == order_row, 1.0, 0.0).astype(jnp.bfloat16)
            placed = jnp.dot(hot, table, preferred_element_type=jnp.float32)
            out_ref[start : start + chunk, :] = placed.astype(jnp.bfloat16)

    return pl.pallas_call(
        kernel,
        in_specs=[pl.BlockSpec(memory_space=pltpu.VMEM)] * 3 + [pl.BlockSpec(memory_space=pl.ANY)],
        out_shape=jax.ShapeDtypeStruct((rows, 2 * depth), jnp.bfloat16),
        compiler_params=pltpu.CompilerParams(vmem_limit_bytes=VMEM_BYTES),
        name="place_rows",
    )(order, received, beside, gate)


def lane_groups(values):
    total = values[:, 0:128]
    for start in range(128, values.shape[1], 128):
        total = total + values[:, start : start + 128]
    return total


def first_panel(chars, parts, tastes, row_values, col_chars):
    rows, depth = chars.shape[0] // parts, chars.shape[1]
    consumers = tastes.shape[0]
    cols = col_chars.shape[0]
    block, chunk = 1024, 256

    def kernel(chars_ref, tastes_ref, rows_ref, cols_ref, panel_ref, share_ref, weight_ref, diag_ref):
        step = pl.program_id(0)

        @pl.when(step == 0)
        def _():
            panel_ref[...] = jnp.zeros_like(panel_ref)
            share_ref[...] = jnp.zeros_like(share_ref)
            diag_ref[...] = jnp.zeros_like(diag_ref)

        people = beside_ones(tastes_ref[...])
        peak, ratio = rows_ref[0:1, :], rows_ref[1:2, :]
        weighted = rows_ref[2:3, :] * (jnp.exp(dot_nt(cols_ref[...], people) - peak) * ratio)
        diag_ref[...] += lane_groups(weighted)
        weight = weighted.astype(jnp.bfloat16)
        weight_ref[...] = weight
        for start in range(0, rows, chunk):
            scaled = jnp.exp(dot_nt(chars_ref[start : start + chunk, :], people) - peak) * ratio
            share_ref[start : start + chunk, :] += lane_groups(scaled)
            panel_ref[start : start + chunk, :] += dot_nt(scaled.astype(jnp.bfloat16), weight)

        @pl.when(step == pl.num_programs(0) - 1)
        def _():
            total = jnp.sum(diag_ref[...].T, axis=0, keepdims=True)
            panel_ref[rows:, :] = jnp.broadcast_to(total, (8, cols))

    return pl.pallas_call(
        kernel,
        grid=(consumers // block,),
        in_specs=[
            pl.BlockSpec((rows, depth), lambda i: (0, 0)),
            pl.BlockSpec((block, tastes.shape[1]), lambda i: (i, 0)),
            pl.BlockSpec((3, block), lambda i: (0, i)),
            pl.BlockSpec((cols, depth), lambda i: (0, 0)),
        ],
        out_specs=[
            pl.BlockSpec((rows + 8, cols), lambda i: (0, 0)),
            pl.BlockSpec((rows, 128), lambda i: (0, 0)),
            pl.BlockSpec((cols, block), lambda i: (0, i)),
        ],
        scratch_shapes=[pltpu.VMEM((cols, 128), jnp.float32)],
        out_shape=[
            jax.ShapeDtypeStruct((rows + 8, cols), jnp.float32),
            jax.ShapeDtypeStruct((rows, 128), jnp.float32),
            jax.ShapeDtypeStruct((cols, consumers), jnp.bfloat16),
        ],
        compiler_params=pltpu.CompilerParams(vmem_limit_bytes=VMEM_BYTES),
        cost_estimate=pl.CostEstimate(
            flops=2 * rows * consumers * (depth + cols), bytes_accessed=rows * cols * 8, transcendentals=rows * consumers
        ),
        name="first_panel",
    )(chars, tastes, row_values, col_chars)


def panel(chars, part, parts, tastes, row_values, weighted, gate):
    rows, depth = chars.shape[0] // parts, chars.shape[1]
    consumers = tastes.shape[0]
    cols = weighted.shape[0]
    chunk = 256

    def kernel(chars_ref, tastes_ref, rows_ref, weight_ref, gate_ref, panel_ref, share_ref):
        people, weight = beside_ones(tastes_ref[...]), weight_ref[...]
        peak, ratio = rows_ref[0:1, :], rows_ref[1:2, :]
        for start in range(0, rows, chunk):
            scaled = jnp.exp(dot_nt(chars_ref[start : start + chunk, :], people) - peak) * ratio
            share_ref[start : start + chunk, :] = lane_groups(scaled)
            panel_ref[start : start + chunk, :] = dot_nt(scaled.astype(jnp.bfloat16), weight)

    return pl.pallas_call(
        kernel,
        grid=(1,),
        in_specs=[
            pl.BlockSpec((rows, depth), lambda i: (part, 0)),
            pl.BlockSpec(tastes.shape, lambda i: (0, 0)),
            pl.BlockSpec((3, consumers), lambda i: (0, 0)),
            pl.BlockSpec((cols, consumers), lambda i: (0, 0)),
            pl.BlockSpec(memory_space=pl.ANY),
        ],
        out_specs=[
            pl.BlockSpec((rows, cols), lambda i: (0, 0)),
            pl.BlockSpec((rows, 128), lambda i: (0, 0)),
        ],
        out_shape=[
            jax.ShapeDtypeStruct((rows, cols), jnp.float32),
            jax.ShapeDtypeStruct((rows, 128), jnp.float32),
        ],
        compiler_params=pltpu.CompilerParams(vmem_limit_bytes=VMEM_BYTES),
        cost_estimate=pl.CostEstimate(
            flops=2 * rows * consumers * (depth + cols), bytes_accessed=rows * cols * 8, transcendentals=rows * consumers
        ),
        name="panel",
    )(chars, tastes, row_values, weighted, gate)


def share_sums(chars, tastes, row_values, gate):
    rows, depth = chars.shape
    consumers = tastes.shape[0]
    block, chunk = 1024, 256

    def kernel(chars_ref, tastes_ref, rows_ref, gate_ref, share_ref):
        @pl.when(pl.program_id(0) == 0)
        def _():
            share_ref[...] = jnp.zeros_like(share_ref)

        people = beside_ones(tastes_ref[...])
        peak, ratio = rows_ref[0:1, :], rows_ref[1:2, :]
        for start in range(0, rows, chunk):
            scaled = jnp.exp(dot_nt(chars_ref[start : start + chunk, :], people) - peak) * ratio
            share_ref[start : start + chunk, :] += lane_groups(scaled)

    return pl.pallas_call(
        kernel,
        grid=(consumers // block,),
        in_specs=[
            pl.BlockSpec((rows, depth), lambda i: (0, 0)),
            pl.BlockSpec((block, tastes.shape[1]), lambda i: (i, 0)),
            pl.BlockSpec((3, block), lambda i: (0, i)),
            pl.BlockSpec(memory_space=pl.ANY),
        ],
        out_specs=pl.BlockSpec((rows, 128), lambda i: (0, 0)),
        out_shape=jax.ShapeDtypeStruct((rows, 128), jnp.float32),
        compiler_params=pltpu.CompilerParams(vmem_limit_bytes=VMEM_BYTES),
        name="share_sums",
    )(chars, tastes, row_values, gate)


def swap(value, axis, mask):
    size = lax.axis_size(axis)
    return lax.ppermute(value, axis, [(i, i ^ mask) for i in range(size)])


def butterfly_masks(size):
    masks, step = [], 1
    while step < size:
        masks.append(step)
        if step * 2 < size:
            masks.append(step * 3)
        step *= 4
    return masks


def body(tastes, price_coef, characteristics, mean_utility, panel_cols, firm_map, inverses):
    products, depth = characteristics.shape
    consumers = tastes.shape[0]
    cols = panel_cols.shape[0]
    holders = lax.axis_size("prod")
    per_pair = products // holders
    count_products = products * holders
    count_consumers = consumers * lax.axis_size("cons")
    base = lax.axis_index("prod") * products
    core = lax.axis_index("cons") % 2

    share_cols = cols // holders
    chars, message, order = prepare(
        characteristics,
        mean_utility.reshape(products // 128, 128),
        firm_map.reshape(1, products),
        (panel_cols - base).astype(jnp.float32).reshape(cols // 128, 128),
        holders,
    )
    first = lax.all_to_all(message.reshape(holders, 16, depth), "prod", split_axis=0, concat_axis=0, tiled=True)

    stat = stats(chars, tastes)

    odd = lax.axis_index("prod") % 2 == 1

    def own_lanes(values):
        return jnp.where(odd, values[..., per_pair:], values[..., :per_pair])

    high, low = own_lanes(first[:, 8, :]), own_lanes(first[:, 12, :])
    ids = high.astype(jnp.int32) * 256 + low.astype(jnp.int32)
    summed = jnp.sum(first.astype(jnp.float32), axis=0)
    tail = jnp.concatenate([jnp.zeros((5, depth), jnp.float32), summed[9:12], summed[:8]], axis=0)
    each = per_pair + 16
    sent, stat = pick_rows(ids.T, chars, tail, stat)
    second = lax.all_to_all(sent.reshape(holders, each, depth), "prod", split_axis=0, concat_axis=0, tiled=True)
    col_pieces = second[:: 128 // share_cols, per_pair + 5 : per_pair + 8, :].transpose(0, 2, 1).reshape(cols, 3)
    col_chars = second[:, per_pair + 8 :, :].reshape(cols, depth)
    col_chars = jnp.concatenate([col_chars, jnp.pad(col_pieces, ((0, 0), (1, depth - 4)))], axis=1)
    mean_rows = own_lanes(second[:, per_pair : per_pair + 4, :].astype(jnp.float32))
    mean_rows = jnp.pad(mean_rows, ((0, 0), (0, 4), (0, 0))).transpose(1, 0, 2).reshape(8, products)
    half = products // 2
    place = (order // half == core).astype(jnp.int32) * half + order % half

    def join(stat, masks):
        for mask in masks:
            other = swap(stat, "prod", mask)
            joint = jnp.maximum(stat, other)
            stat = joint + jnp.log(jnp.exp(stat - joint) + jnp.exp(other - joint))
        return stat

    masks = butterfly_masks(holders)
    taken = panel_cols[0] >= 0
    total = lax.cond(taken, lambda value: join(value, masks), lambda value: value, stat[0])
    peak = jnp.maximum(total, 0.0)
    denom = jnp.exp(-peak) + jnp.exp(total - peak)
    ratio = count_products / denom
    row_values = jnp.stack([peak, ratio, price_coef])
    firm_chars = place_rows(
        place.reshape(1, products), second.reshape(holders * each, depth), mean_rows, holders, row_values
    )
    given, given_share, weighted = first_panel(firm_chars, 2, tastes, row_values, col_chars)
    got = swap(given, "cons", 1)
    kept, kept_share = panel(firm_chars, 1, 2, tastes, row_values, weighted, given)
    diagonal = given[half] + got[half]
    room = 32768.0 / (count_products * jnp.maximum(diagonal, 1e-25))
    fitted = (kept + got[:half]) * room[None, :]
    chip_sum, gate = lax.optimization_barrier((fitted.astype(jnp.float16), jnp.max(fitted, axis=0, keepdims=True)))
    other_sum = swap(chip_sum, "cons", 2)

    given_share, kept_share = jnp.sum(given_share, axis=1), jnp.sum(kept_share, axis=1)
    first_half = jnp.where(core == 0, kept_share, given_share)
    second_half = jnp.where(core == 0, given_share, kept_share)

    def own_and_exchange(gate, others):
        own_shares = jnp.sum(share_sums(chars, tastes, row_values, gate), axis=1)
        sums = jnp.concatenate([own_shares, others])
        sums = sums + swap(sums, "cons", 1)
        return sums, swap(sums, "cons", 2)

    sums, other_sums = lax.cond(
        taken,
        own_and_exchange,
        lambda gate, others: (jnp.zeros(products + others.shape[0], jnp.float32),) * 2,
        gate,
        jnp.concatenate([first_half, second_half, given[half]]),
    )
    other_diagonal = other_sums[2 * products :]
    sums = (sums + other_sums) / count_consumers
    shares, firm_shares = sums[:products], sums[products : 2 * products]

    firm_count, block_size = inverses.shape[0], inverses.shape[1]
    own_inverses = lax.dynamic_slice_in_dim(inverses, core * (firm_count // 2), firm_count // 2, 0)
    firm_ids = lax.dynamic_slice_in_dim(firm_map, core * half, half, 0)
    other_room = 32768.0 / (count_products * jnp.maximum(other_diagonal, 1e-25))
    unfit, other_unfit = 1.0 / (room * count_consumers), 1.0 / (other_room * count_consumers)
    cross = chip_sum.astype(jnp.float32) * unfit[None, :] + other_sum.astype(jnp.float32) * other_unfit[None, :]
    diagonal = (diagonal + other_diagonal) / count_consumers
    jacobian = cross - jnp.where(firm_ids[:, None] == panel_cols[None, :], diagonal[None, :], 0.0)
    mine = jnp.einsum(
        "fab,fbc->fac",
        own_inverses,
        jacobian.reshape(firm_count // 2, block_size, cols),
        precision=lax.Precision.HIGHEST,
    ).reshape(half, cols)
    theirs = swap(mine, "cons", 1)
    response = jnp.where(core == 0, jnp.concatenate([mine, theirs]), jnp.concatenate([theirs, mine]))
    markup = jnp.sum(inverses * firm_shares.reshape(firm_count, 1, block_size), axis=2).reshape(products)
    return (shares, markup, response)


def solution(mesh):
    return jax.shard_map(
        body,
        mesh=mesh,
        in_specs=(
            P("cons", None),
            P("cons"),
            P("prod", None),
            P("prod"),
            P(),
            P("prod"),
            P("prod", None, None),
        ),
        out_specs=(P("prod"), P("prod"), P("prod", None)),
        check_vma=False,
    )
```

```python
import jax
import jax.numpy as jnp
from jax import lax
from jax.experimental import pallas as pl
from jax.experimental.pallas import tpu as pltpu
from jax.sharding import PartitionSpec as P

NT = (((1,), (1,)), ((), ()))
VMEM_BYTES = 24 * 1024 * 1024


def dot_nt(left, right):
    return lax.dot_general(left, right, NT, preferred_element_type=jnp.float32)


def rounded(values):
    return values.astype(jnp.bfloat16).astype(jnp.float32)


def prepare(characteristics, means, firm_row, panel_rows, holders):
    rows, depth = characteristics.shape
    per_pair = rows // holders
    cols = panel_rows.shape[0] * 128
    share_cols = cols // holders
    chunk = 256

    def kernel(chars_ref, means_ref, firm_ref, panel_ref, both_ref, message_ref, place_ref):
        core, half = lax.axis_index("cons") % 2, rows // 2
        base = lax.axis_index("prod") * rows
        lane = lax.broadcasted_iota(jnp.int32, (128, 128), 1)
        values = means_ref[...]
        high = rounded(values)
        middle = rounded(values - high)
        low = values - high - middle
        pieces = jnp.concatenate([high, middle, low, jnp.zeros((128 - 3 * values.shape[0], 128), jnp.float32)], axis=0).T
        count = values.shape[0]
        both_ref[:, :depth] = chars_ref[...]
        for k in range(count):
            beside = jnp.zeros((128, 128), jnp.float32)
            for piece in range(3):
                place = piece * count + k
                beside = jnp.where(lane == piece + 1, pieces[:, place : place + 1], beside)
            both_ref[k * 128 : (k + 1) * 128, depth:] = beside.astype(jnp.bfloat16)

        firm = firm_ref[...]
        holder, wanted = firm // rows, firm % rows
        holder_id = lax.broadcasted_iota(jnp.int32, (holders, rows), 0)
        named = jnp.where(holder_id == holder, 1.0, 0.0)
        blocks = [named[:, start : start + 128] for start in range(0, rows, 128)]
        before = (lax.broadcasted_iota(jnp.int32, (128, 128), 0) < lane).astype(jnp.float32).astype(jnp.bfloat16)
        counts = jnp.dot(
            jnp.concatenate(blocks, axis=0).astype(jnp.bfloat16), before, preferred_element_type=jnp.float32
        )
        seen = jnp.zeros((holders, 1), jnp.float32)
        ranks = []
        for k, block in enumerate(blocks):
            rank = counts[k * holders : (k + 1) * holders, :] + seen
            ranks.append(jnp.sum(block * rank, axis=0, keepdims=True))
            seen = seen + jnp.sum(block, axis=1, keepdims=True)
        slot = holder * per_pair + jnp.concatenate(ranks, axis=1).astype(jnp.int32)

        row = lax.broadcasted_iota(jnp.int32, (8, rows), 0)
        firm_place = lax.broadcasted_iota(jnp.int32, (8, rows), 1)
        digits = jnp.where(row == 0, wanted // 256, jnp.where(row == 1, wanted % 256, 0))
        digits = jnp.where(row == 2, firm_place // 256, jnp.where(row == 3, firm_place % 256, digits))
        digits = jnp.concatenate([digits, jnp.zeros_like(digits)], axis=0).astype(jnp.float32).astype(jnp.bfloat16)
        asked = []
        for start in range(0, rows, chunk):
            slots = start + lax.broadcasted_iota(jnp.int32, (chunk, rows), 0)
            hot = jnp.where(slots == slot, 1.0, 0.0).astype(jnp.bfloat16)
            found = dot_nt(digits, hot)
            order = (found[2:3, :] * 256.0 + found[3:4, :]).astype(jnp.int32)
            place_ref[:, start : start + chunk] = jnp.where(order // half == core, half, 0) + order % half
            asked.append(found)

        products = lax.broadcasted_iota(jnp.int32, (128, rows), 1).astype(jnp.float32)
        both = both_ref[...]
        local = (panel_ref[...] - base).astype(jnp.float32)
        wide = jnp.concatenate([local, jnp.zeros((128 - panel_ref.shape[0], 128), jnp.float32)], axis=0).T
        part_row = lax.broadcasted_iota(jnp.int32, (8, 128), 0)
        for k in range(cols // 128):
            hot = jnp.where(wide[:, k : k + 1] == products, 1.0, 0.0).astype(jnp.bfloat16)
            part = jnp.dot(hot, both, preferred_element_type=jnp.float32)
            part_pieces = part[:, depth:].T[:8, :]
            for place in range(128 // share_cols):
                q = k * (128 // share_cols) + place
                start = q * per_pair // 128 * 128 % chunk
                found = asked[q * per_pair // chunk][:, start : start + 128]
                extra = jnp.where(part_row == 0, found[0:1, :], jnp.where(part_row == 4, found[1:2, :], part_pieces))
                mine = part[place * share_cols : (place + 1) * share_cols, :depth]
                message_ref[q * 16 : (q + 1) * 16, :] = jnp.concatenate([mine, extra], axis=0).astype(jnp.bfloat16)

    def whole(shape):
        return pl.BlockSpec(shape, lambda i: (0, 0))

    return pl.pallas_call(
        kernel,
        grid=(1,),
        in_specs=[whole(value.shape) for value in (characteristics, means, firm_row, panel_rows)],
        out_specs=[whole((rows, 2 * depth)), whole((16 * holders, depth)), whole((1, rows))],
        out_shape=[
            jax.ShapeDtypeStruct((rows, 2 * depth), jnp.bfloat16),
            jax.ShapeDtypeStruct((16 * holders, depth), jnp.bfloat16),
            jax.ShapeDtypeStruct((1, rows), jnp.int32),
        ],
        compiler_params=pltpu.CompilerParams(vmem_limit_bytes=60 * 1024 * 1024),
        name="prepare",
    )(characteristics, means, firm_row, panel_rows)


def beside_ones(tastes):
    lane = lax.broadcasted_iota(jnp.int32, tastes.shape, 1)
    ones = jnp.where((lane >= 1) & (lane <= 3), 1.0, 0.0)
    return jnp.concatenate([tastes, ones.astype(tastes.dtype)], axis=1)


def stats(chars, tastes):
    rows, depth = chars.shape
    consumers = tastes.shape[0]
    block, chunk = 2048, 256

    def kernel(chars_ref, tastes_ref, stat_ref):
        people = beside_ones(tastes_ref[...])
        peak = jnp.full((1, block), -jnp.inf, jnp.float32)
        total = jnp.zeros((8, block), jnp.float32)
        for start in range(0, rows, chunk):
            util = dot_nt(chars_ref[start : start + chunk, :], people)
            highest = jnp.max(util.reshape(chunk // 8, 8, block), axis=0)
            joint = jnp.maximum(peak, jnp.max(highest, axis=0, keepdims=True))
            expo = jnp.exp(util - joint)
            total = total * jnp.exp(peak - joint) + jnp.sum(expo.reshape(chunk // 8, 8, block), axis=0)
            peak = joint
        stat_ref[...] = peak + jnp.log(jnp.sum(total, axis=0, keepdims=True))

    return pl.pallas_call(
        kernel,
        grid=(consumers // block,),
        in_specs=[
            pl.BlockSpec((rows, depth), lambda i: (0, 0)),
            pl.BlockSpec((block, tastes.shape[1]), lambda i: (i, 0)),
        ],
        out_specs=pl.BlockSpec((1, block), lambda i: (0, i)),
        out_shape=jax.ShapeDtypeStruct((1, consumers), jnp.float32),
        compiler_params=pltpu.CompilerParams(vmem_limit_bytes=VMEM_BYTES),
        name="stats",
    )(chars, tastes)


def pick_rows(ids_t, chars, tail, stat):
    per_pair, holders = ids_t.shape
    rows, depth = chars.shape
    each = per_pair + 16
    group, pair = 256 // per_pair, 128 // per_pair

    def kernel(ids_ref, chars_ref, tail_ref, stat_ref, out_ref, stat_out_ref):
        stat_out_ref[...] = stat_ref[...]
        lanes = lax.broadcasted_iota(jnp.int32, (per_pair, rows), 1)
        table = chars_ref[...]
        for start in range(0, holders, group):
            span = range(start, start + group)
            marks = [jnp.where(ids_ref[:, q : q + 1] == lanes, 1.0, 0.0).astype(jnp.bfloat16) for q in span]
            picked = jnp.dot(jnp.concatenate(marks, axis=0), table, preferred_element_type=jnp.float32)
            for place, q in enumerate(span):
                if place % pair == 0:
                    beside = picked[place * per_pair : (place + pair) * per_pair, 128:].T[:8, :]
                    block = jnp.concatenate([beside + tail_ref[0:8, :], tail_ref[8:16, :]], axis=0).astype(jnp.bfloat16)
                mine = picked[place * per_pair : (place + 1) * per_pair, :128]
                out_ref[q * each : q * each + per_pair, :] = mine.astype(jnp.bfloat16)
                out_ref[q * each + per_pair : (q + 1) * each, :] = block

    return pl.pallas_call(
        kernel,
        out_shape=[
            jax.ShapeDtypeStruct((each * holders, depth // 2), jnp.bfloat16),
            jax.ShapeDtypeStruct(stat.shape, stat.dtype),
        ],
        compiler_params=pltpu.CompilerParams(vmem_limit_bytes=VMEM_BYTES),
        name="pick_rows",
    )(ids_t, chars, tail, stat)


def place_rows(order, received, beside, holders, gate):
    rows = order.shape[1]
    total, depth = received.shape
    per_pair, each = rows // holders, total // holders
    chunk = 256

    def kernel(order_ref, received_ref, beside_ref, gate_ref, out_ref):
        order_row = order_ref[...]
        table = jnp.concatenate([received_ref[q * each : q * each + per_pair, :] for q in range(holders)], axis=0)
        blank = jnp.zeros((120, 128), jnp.float32)
        columns = [
            jnp.concatenate([beside_ref[:, start : start + 128], blank], axis=0).T.astype(jnp.bfloat16)
            for start in range(0, rows, 128)
        ]
        table = jnp.concatenate([table, jnp.concatenate(columns, axis=0)], axis=1)
        for start in range(0, rows, chunk):
            ids = start + lax.broadcasted_iota(jnp.int32, (chunk, rows), 0)
            hot = jnp.where(ids == order_row, 1.0, 0.0).astype(jnp.bfloat16)
            placed = jnp.dot(hot, table, preferred_element_type=jnp.float32)
            out_ref[start : start + chunk, :] = placed.astype(jnp.bfloat16)

    return pl.pallas_call(
        kernel,
        in_specs=[pl.BlockSpec(memory_space=pltpu.VMEM)] * 3 + [pl.BlockSpec(memory_space=pl.ANY)],
        out_shape=jax.ShapeDtypeStruct((rows, 2 * depth), jnp.bfloat16),
        compiler_params=pltpu.CompilerParams(vmem_limit_bytes=VMEM_BYTES),
        name="place_rows",
    )(order, received, beside, gate)


def lane_groups(values):
    total = values[:, 0:128]
    for start in range(128, values.shape[1], 128):
        total = total + values[:, start : start + 128]
    return total


def first_panel(chars, parts, tastes, row_values, col_chars):
    rows, depth = chars.shape[0] // parts, chars.shape[1]
    consumers = tastes.shape[0]
    cols = col_chars.shape[0]
    block, chunk = 1024, 256

    def kernel(chars_ref, tastes_ref, rows_ref, cols_ref, panel_ref, share_ref, weight_ref, diag_ref):
        step = pl.program_id(0)

        @pl.when(step == 0)
        def _():
            panel_ref[...] = jnp.zeros_like(panel_ref)
            share_ref[...] = jnp.zeros_like(share_ref)
            diag_ref[...] = jnp.zeros_like(diag_ref)

        people = beside_ones(tastes_ref[...])
        peak, ratio = rows_ref[0:1, :], rows_ref[1:2, :]
        weighted = rows_ref[2:3, :] * (jnp.exp(dot_nt(cols_ref[...], people) - peak) * ratio)
        diag_ref[...] += lane_groups(weighted)
        weight = weighted.astype(jnp.bfloat16)
        weight_ref[...] = weight
        for start in range(0, rows, chunk):
            scaled = jnp.exp(dot_nt(chars_ref[start : start + chunk, :], people) - peak) * ratio
            share_ref[start : start + chunk, :] += lane_groups(scaled)
            panel_ref[start : start + chunk, :] += dot_nt(scaled.astype(jnp.bfloat16), weight)

        @pl.when(step == pl.num_programs(0) - 1)
        def _():
            total = jnp.sum(diag_ref[...].T, axis=0, keepdims=True)
            panel_ref[rows:, :] = jnp.broadcast_to(total, (8, cols))

    return pl.pallas_call(
        kernel,
        grid=(consumers // block,),
        in_specs=[
            pl.BlockSpec((rows, depth), lambda i: (0, 0)),
            pl.BlockSpec((block, tastes.shape[1]), lambda i: (i, 0)),
            pl.BlockSpec((3, block), lambda i: (0, i)),
            pl.BlockSpec((cols, depth), lambda i: (0, 0)),
        ],
        out_specs=[
            pl.BlockSpec((rows + 8, cols), lambda i: (0, 0)),
            pl.BlockSpec((rows, 128), lambda i: (0, 0)),
            pl.BlockSpec((cols, block), lambda i: (0, i)),
        ],
        scratch_shapes=[pltpu.VMEM((cols, 128), jnp.float32)],
        out_shape=[
            jax.ShapeDtypeStruct((rows + 8, cols), jnp.float32),
            jax.ShapeDtypeStruct((rows, 128), jnp.float32),
            jax.ShapeDtypeStruct((cols, consumers), jnp.bfloat16),
        ],
        compiler_params=pltpu.CompilerParams(vmem_limit_bytes=VMEM_BYTES),
        cost_estimate=pl.CostEstimate(
            flops=2 * rows * consumers * (depth + cols), bytes_accessed=rows * cols * 8, transcendentals=rows * consumers
        ),
        name="first_panel",
    )(chars, tastes, row_values, col_chars)


def panel(chars, part, parts, tastes, row_values, weighted, gate):
    rows, depth = chars.shape[0] // parts, chars.shape[1]
    consumers = tastes.shape[0]
    cols = weighted.shape[0]
    chunk = 256

    def kernel(chars_ref, tastes_ref, rows_ref, weight_ref, gate_ref, panel_ref, share_ref):
        people, weight = beside_ones(tastes_ref[...]), weight_ref[...]
        peak, ratio = rows_ref[0:1, :], rows_ref[1:2, :]
        for start in range(0, rows, chunk):
            scaled = jnp.exp(dot_nt(chars_ref[start : start + chunk, :], people) - peak) * ratio
            share_ref[start : start + chunk, :] = lane_groups(scaled)
            panel_ref[start : start + chunk, :] = dot_nt(scaled.astype(jnp.bfloat16), weight)

    return pl.pallas_call(
        kernel,
        grid=(1,),
        in_specs=[
            pl.BlockSpec((rows, depth), lambda i: (part, 0)),
            pl.BlockSpec(tastes.shape, lambda i: (0, 0)),
            pl.BlockSpec((3, consumers), lambda i: (0, 0)),
            pl.BlockSpec((cols, consumers), lambda i: (0, 0)),
            pl.BlockSpec(memory_space=pl.ANY),
        ],
        out_specs=[
            pl.BlockSpec((rows, cols), lambda i: (0, 0)),
            pl.BlockSpec((rows, 128), lambda i: (0, 0)),
        ],
        out_shape=[
            jax.ShapeDtypeStruct((rows, cols), jnp.float32),
            jax.ShapeDtypeStruct((rows, 128), jnp.float32),
        ],
        compiler_params=pltpu.CompilerParams(vmem_limit_bytes=VMEM_BYTES),
        cost_estimate=pl.CostEstimate(
            flops=2 * rows * consumers * (depth + cols), bytes_accessed=rows * cols * 8, transcendentals=rows * consumers
        ),
        name="panel",
    )(chars, tastes, row_values, weighted, gate)


def share_sums(chars, tastes, row_values, gate):
    rows, depth = chars.shape
    consumers = tastes.shape[0]
    block, chunk = 1024, 256

    def kernel(chars_ref, tastes_ref, rows_ref, gate_ref, share_ref):
        @pl.when(pl.program_id(0) == 0)
        def _():
            share_ref[...] = jnp.zeros_like(share_ref)

        people = beside_ones(tastes_ref[...])
        peak, ratio = rows_ref[0:1, :], rows_ref[1:2, :]
        for start in range(0, rows, chunk):
            scaled = jnp.exp(dot_nt(chars_ref[start : start + chunk, :], people) - peak) * ratio
            share_ref[start : start + chunk, :] += lane_groups(scaled)

    return pl.pallas_call(
        kernel,
        grid=(consumers // block,),
        in_specs=[
            pl.BlockSpec((rows, depth), lambda i: (0, 0)),
            pl.BlockSpec((block, tastes.shape[1]), lambda i: (i, 0)),
            pl.BlockSpec((3, block), lambda i: (0, i)),
            pl.BlockSpec(memory_space=pl.ANY),
        ],
        out_specs=pl.BlockSpec((rows, 128), lambda i: (0, 0)),
        out_shape=jax.ShapeDtypeStruct((rows, 128), jnp.float32),
        compiler_params=pltpu.CompilerParams(vmem_limit_bytes=VMEM_BYTES),
        name="share_sums",
    )(chars, tastes, row_values, gate)


def swap(value, axis, mask):
    size = lax.axis_size(axis)
    return lax.ppermute(value, axis, [(i, i ^ mask) for i in range(size)])


def butterfly_masks(size):
    masks, step = [], 1
    while step < size:
        masks.append(step)
        if step * 2 < size:
            masks.append(step * 3)
        step *= 4
    return masks


def body(tastes, price_coef, characteristics, mean_utility, panel_cols, firm_map, inverses):
    products, depth = characteristics.shape
    consumers = tastes.shape[0]
    cols = panel_cols.shape[0]
    holders = lax.axis_size("prod")
    per_pair = products // holders
    count_products = products * holders
    count_consumers = consumers * lax.axis_size("cons")
    core = lax.axis_index("cons") % 2

    share_cols = cols // holders
    chars, message, place = prepare(
        characteristics,
        mean_utility.reshape(products // 128, 128),
        firm_map.reshape(1, products),
        panel_cols.reshape(cols // 128, 128),
        holders,
    )
    first = lax.all_to_all(message.reshape(holders, 16, depth), "prod", split_axis=0, concat_axis=0, tiled=True)

    stat = stats(chars, tastes)

    odd = lax.axis_index("prod") % 2 == 1

    def own_lanes(values):
        return jnp.where(odd, values[..., per_pair:], values[..., :per_pair])

    high, low = own_lanes(first[:, 8, :]), own_lanes(first[:, 12, :])
    ids = high.astype(jnp.int32) * 256 + low.astype(jnp.int32)
    summed = jnp.sum(first.astype(jnp.float32), axis=0)
    tail = jnp.concatenate([jnp.zeros((5, depth), jnp.float32), summed[9:12], summed[:8]], axis=0)
    each = per_pair + 16
    sent, stat = pick_rows(ids.T, chars, tail, stat)
    second = lax.all_to_all(sent.reshape(holders, each, depth), "prod", split_axis=0, concat_axis=0, tiled=True)
    col_pieces = second[:: 128 // share_cols, per_pair + 5 : per_pair + 8, :].transpose(0, 2, 1).reshape(cols, 3)
    col_chars = second[:, per_pair + 8 :, :].reshape(cols, depth)
    col_chars = jnp.concatenate([col_chars, jnp.pad(col_pieces, ((0, 0), (1, depth - 4)))], axis=1)
    mean_rows = own_lanes(second[:, per_pair : per_pair + 4, :].astype(jnp.float32))
    mean_rows = jnp.pad(mean_rows, ((0, 0), (0, 4), (0, 0))).transpose(1, 0, 2).reshape(8, products)
    half = products // 2

    def join(stat, masks):
        for mask in masks:
            other = swap(stat, "prod", mask)
            joint = jnp.maximum(stat, other)
            stat = joint + jnp.log(jnp.exp(stat - joint) + jnp.exp(other - joint))
        return stat

    masks = butterfly_masks(holders)
    taken = panel_cols[0] >= 0
    total = lax.cond(taken, lambda value: join(value, masks), lambda value: value, stat[0])
    peak = jnp.maximum(total, 0.0)
    denom = jnp.exp(-peak) + jnp.exp(total - peak)
    ratio = count_products / denom
    row_values = jnp.stack([peak, ratio, price_coef])
    firm_chars = place_rows(
        place, second.reshape(holders * each, depth), mean_rows, holders, row_values
    )
    given, given_share, weighted = first_panel(firm_chars, 2, tastes, row_values, col_chars)
    got = swap(given, "cons", 1)
    kept, kept_share = panel(firm_chars, 1, 2, tastes, row_values, weighted, given)
    diagonal = given[half] + got[half]
    room = 32768.0 / (count_products * jnp.maximum(diagonal, 1e-25))
    fitted = (kept + got[:half]) * room[None, :]
    chip_sum, gate = lax.optimization_barrier((fitted.astype(jnp.float16), jnp.max(fitted, axis=0, keepdims=True)))
    other_sum = swap(chip_sum, "cons", 2)

    given_share, kept_share = jnp.sum(given_share, axis=1), jnp.sum(kept_share, axis=1)
    first_half = jnp.where(core == 0, kept_share, given_share)
    second_half = jnp.where(core == 0, given_share, kept_share)

    def own_and_exchange(gate, others):
        own_shares = jnp.sum(share_sums(chars, tastes, row_values, gate), axis=1)
        sums = jnp.concatenate([own_shares, others])
        sums = sums + swap(sums, "cons", 1)
        other_sums = swap(sums, "cons", 2)
        return (sums + other_sums) / count_consumers, other_sums[2 * products :]

    sums, other_diagonal = lax.cond(
        taken,
        own_and_exchange,
        lambda gate, others: (jnp.zeros(2 * products + cols, jnp.float32), jnp.zeros(cols, jnp.float32)),
        gate,
        jnp.concatenate([first_half, second_half, given[half]]),
    )
    shares, firm_shares = sums[:products], sums[products : 2 * products]

    firm_count, block_size = inverses.shape[0], inverses.shape[1]
    own_inverses = lax.dynamic_slice_in_dim(inverses, core * (firm_count // 2), firm_count // 2, 0)
    firm_ids = lax.dynamic_slice_in_dim(firm_map, core * half, half, 0)
    other_room = 32768.0 / (count_products * jnp.maximum(other_diagonal, 1e-25))
    unfit, other_unfit = 1.0 / (room * count_consumers), 1.0 / (other_room * count_consumers)
    cross = chip_sum.astype(jnp.float32) * unfit[None, :] + other_sum.astype(jnp.float32) * other_unfit[None, :]
    diagonal = (diagonal + other_diagonal) / count_consumers
    jacobian = cross - jnp.where(firm_ids[:, None] == panel_cols[None, :], diagonal[None, :], 0.0)
    mine = jnp.einsum(
        "fab,fbc->fac",
        own_inverses,
        jacobian.reshape(firm_count // 2, block_size, cols),
        precision=lax.Precision.HIGHEST,
    ).reshape(half, cols)
    theirs = swap(mine, "cons", 1)
    response = jnp.where(core == 0, jnp.concatenate([mine, theirs]), jnp.concatenate([theirs, mine]))
    markup = jnp.sum(inverses * firm_shares.reshape(firm_count, 1, block_size), axis=2).reshape(products)
    return (shares, markup, response)


def solution(mesh):
    return jax.shard_map(
        body,
        mesh=mesh,
        in_specs=(
            P("cons", None),
            P("cons"),
            P("prod", None),
            P("prod"),
            P(),
            P("prod"),
            P("prod", None, None),
        ),
        out_specs=(P("prod"), P("prod"), P("prod", None)),
        check_vma=False,
    )
```

```python
import jax
import jax.numpy as jnp
from jax import lax
from jax.experimental import pallas as pl
from jax.experimental.pallas import tpu as pltpu
from jax.sharding import PartitionSpec as P

NT = (((1,), (1,)), ((), ()))
VMEM_BYTES = 24 * 1024 * 1024


def dot_nt(left, right):
    return lax.dot_general(left, right, NT, preferred_element_type=jnp.float32)


def rounded(values):
    return values.astype(jnp.bfloat16).astype(jnp.float32)


def prepare(characteristics, means, firm_row, panel_rows, holders):
    rows, depth = characteristics.shape
    per_pair = rows // holders
    cols = panel_rows.shape[0] * 128
    share_cols = cols // holders
    chunk = 256

    def kernel(chars_ref, means_ref, firm_ref, panel_ref, both_ref, message_ref, place_ref):
        core, half = lax.axis_index("cons") % 2, rows // 2
        base = lax.axis_index("prod") * rows
        lane = lax.broadcasted_iota(jnp.int32, (128, 128), 1)
        values = means_ref[...]
        high = rounded(values)
        middle = rounded(values - high)
        low = values - high - middle
        pieces = jnp.concatenate([high, middle, low, jnp.zeros((128 - 3 * values.shape[0], 128), jnp.float32)], axis=0).T
        count = values.shape[0]
        both_ref[:, :depth] = chars_ref[...]
        for k in range(count):
            beside = jnp.zeros((128, 128), jnp.float32)
            for piece in range(3):
                place = piece * count + k
                beside = jnp.where(lane == piece + 1, pieces[:, place : place + 1], beside)
            both_ref[k * 128 : (k + 1) * 128, depth:] = beside.astype(jnp.bfloat16)

        firm = firm_ref[...]
        holder, wanted = firm // rows, firm % rows
        holder_id = lax.broadcasted_iota(jnp.int32, (holders, rows), 0)
        named = jnp.where(holder_id == holder, 1.0, 0.0)
        blocks = [named[:, start : start + 128] for start in range(0, rows, 128)]
        before = (lax.broadcasted_iota(jnp.int32, (128, 128), 0) < lane).astype(jnp.float32).astype(jnp.bfloat16)
        counts = jnp.dot(
            jnp.concatenate(blocks, axis=0).astype(jnp.bfloat16), before, preferred_element_type=jnp.float32
        )
        seen = jnp.zeros((holders, 1), jnp.float32)
        ranks = []
        for k, block in enumerate(blocks):
            rank = counts[k * holders : (k + 1) * holders, :] + seen
            ranks.append(jnp.sum(block * rank, axis=0, keepdims=True))
            seen = seen + jnp.sum(block, axis=1, keepdims=True)
        slot = holder * per_pair + jnp.concatenate(ranks, axis=1).astype(jnp.int32)

        row = lax.broadcasted_iota(jnp.int32, (8, rows), 0)
        firm_place = lax.broadcasted_iota(jnp.int32, (8, rows), 1)
        digits = jnp.where(row == 0, wanted // 256, jnp.where(row == 1, wanted % 256, 0))
        digits = jnp.where(row == 2, firm_place // 256, jnp.where(row == 3, firm_place % 256, digits))
        digits = jnp.concatenate([digits, jnp.zeros_like(digits)], axis=0).astype(jnp.float32).astype(jnp.bfloat16)
        asked = []
        for start in range(0, rows, chunk):
            slots = start + lax.broadcasted_iota(jnp.int32, (chunk, rows), 0)
            hot = jnp.where(slots == slot, 1.0, 0.0).astype(jnp.bfloat16)
            found = dot_nt(digits, hot)
            order = (found[2:3, :] * 256.0 + found[3:4, :]).astype(jnp.int32)
            place_ref[:, start : start + chunk] = jnp.where(order // half == core, half, 0) + order % half
            asked.append(found)

        products = lax.broadcasted_iota(jnp.int32, (128, rows), 1).astype(jnp.float32)
        both = both_ref[...]
        local = (panel_ref[...] - base).astype(jnp.float32)
        wide = jnp.concatenate([local, jnp.zeros((128 - panel_ref.shape[0], 128), jnp.float32)], axis=0).T
        part_row = lax.broadcasted_iota(jnp.int32, (8, 128), 0)
        for k in range(cols // 128):
            hot = jnp.where(wide[:, k : k + 1] == products, 1.0, 0.0).astype(jnp.bfloat16)
            part = jnp.dot(hot, both, preferred_element_type=jnp.float32)
            part_pieces = part[:, depth:].T[:8, :]
            part_pieces = jnp.concatenate([part_pieces[4:8, :], part_pieces[0:4, :]], axis=0)
            for place in range(128 // share_cols):
                q = k * (128 // share_cols) + place
                start = q * per_pair // 128 * 128 % chunk
                found = asked[q * per_pair // chunk][:, start : start + 128]
                extra = jnp.where(part_row == 0, found[0:1, :], jnp.where(part_row == 4, found[1:2, :], part_pieces))
                mine = part[place * share_cols : (place + 1) * share_cols, :depth]
                message_ref[q * 16 : (q + 1) * 16, :] = jnp.concatenate([mine, extra], axis=0).astype(jnp.bfloat16)

    def whole(shape):
        return pl.BlockSpec(shape, lambda i: (0, 0))

    return pl.pallas_call(
        kernel,
        grid=(1,),
        in_specs=[whole(value.shape) for value in (characteristics, means, firm_row, panel_rows)],
        out_specs=[whole((rows, 2 * depth)), whole((16 * holders, depth)), whole((1, rows))],
        out_shape=[
            jax.ShapeDtypeStruct((rows, 2 * depth), jnp.bfloat16),
            jax.ShapeDtypeStruct((16 * holders, depth), jnp.bfloat16),
            jax.ShapeDtypeStruct((1, rows), jnp.int32),
        ],
        compiler_params=pltpu.CompilerParams(vmem_limit_bytes=60 * 1024 * 1024),
        name="prepare",
    )(characteristics, means, firm_row, panel_rows)


def beside_ones(tastes):
    lane = lax.broadcasted_iota(jnp.int32, tastes.shape, 1)
    ones = jnp.where((lane >= 1) & (lane <= 3), 1.0, 0.0)
    return jnp.concatenate([tastes, ones.astype(tastes.dtype)], axis=1)


def stats(chars, tastes):
    rows, depth = chars.shape
    consumers = tastes.shape[0]
    block, chunk = 2048, 256

    def kernel(chars_ref, tastes_ref, stat_ref):
        people = beside_ones(tastes_ref[...])
        peak = jnp.full((1, block), -jnp.inf, jnp.float32)
        total = jnp.zeros((8, block), jnp.float32)
        for start in range(0, rows, chunk):
            util = dot_nt(chars_ref[start : start + chunk, :], people)
            highest = jnp.max(util.reshape(chunk // 8, 8, block), axis=0)
            joint = jnp.maximum(peak, jnp.max(highest, axis=0, keepdims=True))
            expo = jnp.exp(util - joint)
            total = total * jnp.exp(peak - joint) + jnp.sum(expo.reshape(chunk // 8, 8, block), axis=0)
            peak = joint
        stat_ref[...] = peak + jnp.log(jnp.sum(total, axis=0, keepdims=True))

    return pl.pallas_call(
        kernel,
        grid=(consumers // block,),
        in_specs=[
            pl.BlockSpec((rows, depth), lambda i: (0, 0)),
            pl.BlockSpec((block, tastes.shape[1]), lambda i: (i, 0)),
        ],
        out_specs=pl.BlockSpec((1, block), lambda i: (0, i)),
        out_shape=jax.ShapeDtypeStruct((1, consumers), jnp.float32),
        compiler_params=pltpu.CompilerParams(vmem_limit_bytes=VMEM_BYTES),
        name="stats",
    )(chars, tastes)


def pick_rows(ids_t, chars, tail, stat):
    per_pair, holders = ids_t.shape
    rows, depth = chars.shape
    each = per_pair + 16
    group, pair = 256 // per_pair, 128 // per_pair

    def kernel(ids_ref, chars_ref, tail_ref, stat_ref, out_ref, stat_out_ref):
        stat_out_ref[...] = stat_ref[...]
        lanes = lax.broadcasted_iota(jnp.int32, (per_pair, rows), 1)
        table = chars_ref[...]
        pieces = jnp.where(lax.broadcasted_iota(jnp.int32, (8, 128), 0) >= 5, tail_ref[8:16, :], 0.0)
        for start in range(0, holders, group):
            span = range(start, start + group)
            marks = [jnp.where(ids_ref[:, q : q + 1] == lanes, 1.0, 0.0).astype(jnp.bfloat16) for q in span]
            picked = jnp.dot(jnp.concatenate(marks, axis=0), table, preferred_element_type=jnp.float32)
            for place, q in enumerate(span):
                if place % pair == 0:
                    beside = picked[place * per_pair : (place + pair) * per_pair, 128:].T[:8, :]
                    block = jnp.concatenate([beside + pieces, tail_ref[0:8, :]], axis=0).astype(jnp.bfloat16)
                mine = picked[place * per_pair : (place + 1) * per_pair, :128]
                out_ref[q * each : q * each + per_pair, :] = mine.astype(jnp.bfloat16)
                out_ref[q * each + per_pair : (q + 1) * each, :] = block

    return pl.pallas_call(
        kernel,
        out_shape=[
            jax.ShapeDtypeStruct((each * holders, depth // 2), jnp.bfloat16),
            jax.ShapeDtypeStruct(stat.shape, stat.dtype),
        ],
        compiler_params=pltpu.CompilerParams(vmem_limit_bytes=VMEM_BYTES),
        name="pick_rows",
    )(ids_t, chars, tail, stat)


def place_rows(order, received, beside, holders, gate):
    rows = order.shape[1]
    total, depth = received.shape
    per_pair, each = rows // holders, total // holders
    chunk = 256

    def kernel(order_ref, received_ref, beside_ref, gate_ref, out_ref):
        order_row = order_ref[...]
        table = jnp.concatenate([received_ref[q * each : q * each + per_pair, :] for q in range(holders)], axis=0)
        blank = jnp.zeros((120, 128), jnp.float32)
        columns = [
            jnp.concatenate([beside_ref[:, start : start + 128], blank], axis=0).T.astype(jnp.bfloat16)
            for start in range(0, rows, 128)
        ]
        table = jnp.concatenate([table, jnp.concatenate(columns, axis=0)], axis=1)
        for start in range(0, rows, chunk):
            ids = start + lax.broadcasted_iota(jnp.int32, (chunk, rows), 0)
            hot = jnp.where(ids == order_row, 1.0, 0.0).astype(jnp.bfloat16)
            placed = jnp.dot(hot, table, preferred_element_type=jnp.float32)
            out_ref[start : start + chunk, :] = placed.astype(jnp.bfloat16)

    return pl.pallas_call(
        kernel,
        in_specs=[pl.BlockSpec(memory_space=pltpu.VMEM)] * 3 + [pl.BlockSpec(memory_space=pl.ANY)],
        out_shape=jax.ShapeDtypeStruct((rows, 2 * depth), jnp.bfloat16),
        compiler_params=pltpu.CompilerParams(vmem_limit_bytes=VMEM_BYTES),
        name="place_rows",
    )(order, received, beside, gate)


def lane_groups(values):
    total = values[:, 0:128]
    for start in range(128, values.shape[1], 128):
        total = total + values[:, start : start + 128]
    return total


def first_panel(chars, parts, tastes, row_values, col_chars):
    rows, depth = chars.shape[0] // parts, chars.shape[1]
    consumers = tastes.shape[0]
    cols = col_chars.shape[0]
    block, chunk = 1024, 256

    def kernel(chars_ref, tastes_ref, rows_ref, cols_ref, panel_ref, share_ref, weight_ref, diag_ref):
        step = pl.program_id(0)

        @pl.when(step == 0)
        def _():
            panel_ref[...] = jnp.zeros_like(panel_ref)
            share_ref[...] = jnp.zeros_like(share_ref)
            diag_ref[...] = jnp.zeros_like(diag_ref)

        people = beside_ones(tastes_ref[...])
        peak, ratio = rows_ref[0:1, :], rows_ref[1:2, :]
        weighted = rows_ref[2:3, :] * (jnp.exp(dot_nt(cols_ref[...], people) - peak) * ratio)
        diag_ref[...] += lane_groups(weighted)
        weight = weighted.astype(jnp.bfloat16)
        weight_ref[...] = weight
        for start in range(0, rows, chunk):
            scaled = jnp.exp(dot_nt(chars_ref[start : start + chunk, :], people) - peak) * ratio
            share_ref[start : start + chunk, :] += lane_groups(scaled)
            panel_ref[start : start + chunk, :] += dot_nt(scaled.astype(jnp.bfloat16), weight)

        @pl.when(step == pl.num_programs(0) - 1)
        def _():
            total = jnp.sum(diag_ref[...].T, axis=0, keepdims=True)
            panel_ref[rows:, :] = jnp.broadcast_to(total, (8, cols))

    return pl.pallas_call(
        kernel,
        grid=(consumers // block,),
        in_specs=[
            pl.BlockSpec((rows, depth), lambda i: (0, 0)),
            pl.BlockSpec((block, tastes.shape[1]), lambda i: (i, 0)),
            pl.BlockSpec((3, block), lambda i: (0, i)),
            pl.BlockSpec((cols, depth), lambda i: (0, 0)),
        ],
        out_specs=[
            pl.BlockSpec((rows + 8, cols), lambda i: (0, 0)),
            pl.BlockSpec((rows, 128), lambda i: (0, 0)),
            pl.BlockSpec((cols, block), lambda i: (0, i)),
        ],
        scratch_shapes=[pltpu.VMEM((cols, 128), jnp.float32)],
        out_shape=[
            jax.ShapeDtypeStruct((rows + 8, cols), jnp.float32),
            jax.ShapeDtypeStruct((rows, 128), jnp.float32),
            jax.ShapeDtypeStruct((cols, consumers), jnp.bfloat16),
        ],
        compiler_params=pltpu.CompilerParams(vmem_limit_bytes=VMEM_BYTES),
        cost_estimate=pl.CostEstimate(
            flops=2 * rows * consumers * (depth + cols), bytes_accessed=rows * cols * 8, transcendentals=rows * consumers
        ),
        name="first_panel",
    )(chars, tastes, row_values, col_chars)


def panel(chars, part, parts, tastes, row_values, weighted, gate):
    rows, depth = chars.shape[0] // parts, chars.shape[1]
    consumers = tastes.shape[0]
    cols = weighted.shape[0]
    chunk = 256

    def kernel(chars_ref, tastes_ref, rows_ref, weight_ref, gate_ref, panel_ref, share_ref):
        people, weight = beside_ones(tastes_ref[...]), weight_ref[...]
        peak, ratio = rows_ref[0:1, :], rows_ref[1:2, :]
        for start in range(0, rows, chunk):
            scaled = jnp.exp(dot_nt(chars_ref[start : start + chunk, :], people) - peak) * ratio
            share_ref[start : start + chunk, :] = lane_groups(scaled)
            panel_ref[start : start + chunk, :] = dot_nt(scaled.astype(jnp.bfloat16), weight)

    return pl.pallas_call(
        kernel,
        grid=(1,),
        in_specs=[
            pl.BlockSpec((rows, depth), lambda i: (part, 0)),
            pl.BlockSpec(tastes.shape, lambda i: (0, 0)),
            pl.BlockSpec((3, consumers), lambda i: (0, 0)),
            pl.BlockSpec((cols, consumers), lambda i: (0, 0)),
            pl.BlockSpec(memory_space=pl.ANY),
        ],
        out_specs=[
            pl.BlockSpec((rows, cols), lambda i: (0, 0)),
            pl.BlockSpec((rows, 128), lambda i: (0, 0)),
        ],
        out_shape=[
            jax.ShapeDtypeStruct((rows, cols), jnp.float32),
            jax.ShapeDtypeStruct((rows, 128), jnp.float32),
        ],
        compiler_params=pltpu.CompilerParams(vmem_limit_bytes=VMEM_BYTES),
        cost_estimate=pl.CostEstimate(
            flops=2 * rows * consumers * (depth + cols), bytes_accessed=rows * cols * 8, transcendentals=rows * consumers
        ),
        name="panel",
    )(chars, tastes, row_values, weighted, gate)


def share_sums(chars, tastes, row_values, gate):
    rows, depth = chars.shape
    consumers = tastes.shape[0]
    block, chunk = 1024, 256

    def kernel(chars_ref, tastes_ref, rows_ref, gate_ref, share_ref):
        @pl.when(pl.program_id(0) == 0)
        def _():
            share_ref[...] = jnp.zeros_like(share_ref)

        people = beside_ones(tastes_ref[...])
        peak, ratio = rows_ref[0:1, :], rows_ref[1:2, :]
        for start in range(0, rows, chunk):
            scaled = jnp.exp(dot_nt(chars_ref[start : start + chunk, :], people) - peak) * ratio
            share_ref[start : start + chunk, :] += lane_groups(scaled)

    return pl.pallas_call(
        kernel,
        grid=(consumers // block,),
        in_specs=[
            pl.BlockSpec((rows, depth), lambda i: (0, 0)),
            pl.BlockSpec((block, tastes.shape[1]), lambda i: (i, 0)),
            pl.BlockSpec((3, block), lambda i: (0, i)),
            pl.BlockSpec(memory_space=pl.ANY),
        ],
        out_specs=pl.BlockSpec((rows, 128), lambda i: (0, 0)),
        out_shape=jax.ShapeDtypeStruct((rows, 128), jnp.float32),
        compiler_params=pltpu.CompilerParams(vmem_limit_bytes=VMEM_BYTES),
        name="share_sums",
    )(chars, tastes, row_values, gate)


def swap(value, axis, mask):
    size = lax.axis_size(axis)
    return lax.ppermute(value, axis, [(i, i ^ mask) for i in range(size)])


def butterfly_masks(size):
    masks, step = [], 1
    while step < size:
        masks.append(step)
        if step * 2 < size:
            masks.append(step * 3)
        step *= 4
    return masks


def body(tastes, price_coef, characteristics, mean_utility, panel_cols, firm_map, inverses):
    products, depth = characteristics.shape
    consumers = tastes.shape[0]
    cols = panel_cols.shape[0]
    holders = lax.axis_size("prod")
    per_pair = products // holders
    count_products = products * holders
    count_consumers = consumers * lax.axis_size("cons")
    core = lax.axis_index("cons") % 2

    share_cols = cols // holders
    chars, message, place = prepare(
        characteristics,
        mean_utility.reshape(products // 128, 128),
        firm_map.reshape(1, products),
        panel_cols.reshape(cols // 128, 128),
        holders,
    )
    first = lax.all_to_all(message.reshape(holders, 16, depth), "prod", split_axis=0, concat_axis=0, tiled=True)

    stat = stats(chars, tastes)

    odd = lax.axis_index("prod") % 2 == 1

    def own_lanes(values):
        return jnp.where(odd, values[..., per_pair:], values[..., :per_pair])

    high, low = own_lanes(first[:, 8, :]), own_lanes(first[:, 12, :])
    ids = high.astype(jnp.int32) * 256 + low.astype(jnp.int32)
    summed = jnp.sum(first.astype(jnp.float32), axis=0)
    each = per_pair + 16
    sent, stat = pick_rows(ids.T, chars, summed, stat)
    second = lax.all_to_all(sent.reshape(holders, each, depth), "prod", split_axis=0, concat_axis=0, tiled=True)
    col_pieces = second[:: 128 // share_cols, per_pair + 5 : per_pair + 8, :].transpose(0, 2, 1).reshape(cols, 3)
    col_chars = second[:, per_pair + 8 :, :].reshape(cols, depth)
    col_chars = jnp.concatenate([col_chars, jnp.pad(col_pieces, ((0, 0), (1, depth - 4)))], axis=1)
    mean_rows = own_lanes(second[:, per_pair : per_pair + 4, :].astype(jnp.float32))
    mean_rows = jnp.pad(mean_rows, ((0, 0), (0, 4), (0, 0))).transpose(1, 0, 2).reshape(8, products)
    half = products // 2

    def join(stat, masks):
        for mask in masks:
            other = swap(stat, "prod", mask)
            joint = jnp.maximum(stat, other)
            stat = joint + jnp.log(jnp.exp(stat - joint) + jnp.exp(other - joint))
        return stat

    masks = butterfly_masks(holders)
    taken = ids[0, 0] >= 0
    total = lax.cond(taken, lambda value: join(value, masks), lambda value: value, stat[0])
    peak = jnp.maximum(total, 0.0)
    denom = jnp.exp(-peak) + jnp.exp(total - peak)
    ratio = count_products / denom
    row_values = jnp.stack([peak, ratio, price_coef])
    firm_chars = place_rows(
        place, second.reshape(holders * each, depth), mean_rows, holders, row_values
    )
    given, given_share, weighted = first_panel(firm_chars, 2, tastes, row_values, col_chars)
    got = swap(given, "cons", 1)
    kept, kept_share = panel(firm_chars, 1, 2, tastes, row_values, weighted, given)
    diagonal = given[half] + got[half]
    room = 32768.0 / (count_products * jnp.maximum(diagonal, 1e-25))
    fitted = (kept + got[:half]) * room[None, :]
    chip_sum, gate = lax.optimization_barrier((fitted.astype(jnp.float16), jnp.max(fitted, axis=0, keepdims=True)))
    other_sum = swap(chip_sum, "cons", 2)

    given_share, kept_share = jnp.sum(given_share, axis=1), jnp.sum(kept_share, axis=1)
    first_half = jnp.where(core == 0, kept_share, given_share)
    second_half = jnp.where(core == 0, given_share, kept_share)

    def own_and_exchange(gate, others):
        own_shares = jnp.sum(share_sums(chars, tastes, row_values, gate), axis=1)
        sums = jnp.concatenate([own_shares, others])
        sums = sums + swap(sums, "cons", 1)
        other_sums = swap(sums, "cons", 2)
        return (sums + other_sums) / count_consumers, other_sums[2 * products :]

    sums, other_diagonal = lax.cond(
        taken,
        own_and_exchange,
        lambda gate, others: (jnp.zeros(2 * products + cols, jnp.float32), jnp.zeros(cols, jnp.float32)),
        gate,
        jnp.concatenate([first_half, second_half, given[half]]),
    )
    shares, firm_shares = sums[:products], sums[products : 2 * products]

    firm_count, block_size = inverses.shape[0], inverses.shape[1]
    own_inverses = lax.dynamic_slice_in_dim(inverses, core * (firm_count // 2), firm_count // 2, 0)
    firm_ids = lax.dynamic_slice_in_dim(firm_map, core * half, half, 0)
    other_room = 32768.0 / (count_products * jnp.maximum(other_diagonal, 1e-25))
    unfit, other_unfit = 1.0 / (room * count_consumers), 1.0 / (other_room * count_consumers)
    cross = chip_sum.astype(jnp.float32) * unfit[None, :] + other_sum.astype(jnp.float32) * other_unfit[None, :]
    diagonal = (diagonal + other_diagonal) / count_consumers
    jacobian = cross - jnp.where(firm_ids[:, None] == panel_cols[None, :], diagonal[None, :], 0.0)
    mine = jnp.einsum(
        "fab,fbc->fac",
        own_inverses,
        jacobian.reshape(firm_count // 2, block_size, cols),
        precision=lax.Precision.HIGHEST,
    ).reshape(half, cols)
    theirs = swap(mine, "cons", 1)
    response = jnp.where(core == 0, jnp.concatenate([mine, theirs]), jnp.concatenate([theirs, mine]))
    markup = jnp.sum(inverses * firm_shares.reshape(firm_count, 1, block_size), axis=2).reshape(products)
    return (shares, markup, response)


def solution(mesh):
    return jax.shard_map(
        body,
        mesh=mesh,
        in_specs=(
            P("cons", None),
            P("cons"),
            P("prod", None),
            P("prod"),
            P(),
            P("prod"),
            P("prod", None, None),
        ),
        out_specs=(P("prod"), P("prod"), P("prod", None)),
        check_vma=False,
    )
```

```python
import jax
import jax.numpy as jnp
from jax import lax
from jax.experimental import pallas as pl
from jax.experimental.pallas import tpu as pltpu
from jax.sharding import PartitionSpec as P

NT = (((1,), (1,)), ((), ()))
VMEM_BYTES = 24 * 1024 * 1024


def dot_nt(left, right):
    return lax.dot_general(left, right, NT, preferred_element_type=jnp.float32)


def rounded(values):
    return values.astype(jnp.bfloat16).astype(jnp.float32)


def prepare(characteristics, means, firm_row, panel_rows, holders):
    rows, depth = characteristics.shape
    per_pair = rows // holders
    cols = panel_rows.shape[0] * 128
    share_cols = cols // holders
    chunk = 256

    def kernel(chars_ref, means_ref, firm_ref, panel_ref, both_ref, message_ref, place_ref):
        core, half = lax.axis_index("cons") % 2, rows // 2
        base = lax.axis_index("prod") * rows
        lane = lax.broadcasted_iota(jnp.int32, (128, 128), 1)
        values = means_ref[...]
        high = rounded(values)
        middle = rounded(values - high)
        low = values - high - middle
        pieces = jnp.concatenate([high, middle, low, jnp.zeros((128 - 3 * values.shape[0], 128), jnp.float32)], axis=0).T
        count = values.shape[0]
        both_ref[:, :depth] = chars_ref[...]
        for k in range(count):
            beside = jnp.zeros((128, 128), jnp.float32)
            for piece in range(3):
                place = piece * count + k
                beside = jnp.where(lane == piece + 1, pieces[:, place : place + 1], beside)
            both_ref[k * 128 : (k + 1) * 128, depth:] = beside.astype(jnp.bfloat16)

        firm = firm_ref[...]
        holder, wanted = firm // rows, firm % rows
        holder_id = lax.broadcasted_iota(jnp.int32, (holders, rows), 0)
        named = jnp.where(holder_id == holder, 1.0, 0.0)
        blocks = [named[:, start : start + 128] for start in range(0, rows, 128)]
        before = (lax.broadcasted_iota(jnp.int32, (128, 128), 0) < lane).astype(jnp.float32).astype(jnp.bfloat16)
        counts = jnp.dot(
            jnp.concatenate(blocks, axis=0).astype(jnp.bfloat16), before, preferred_element_type=jnp.float32
        )
        seen = jnp.zeros((holders, 1), jnp.float32)
        ranks = []
        for k, block in enumerate(blocks):
            rank = counts[k * holders : (k + 1) * holders, :] + seen
            ranks.append(jnp.sum(block * rank, axis=0, keepdims=True))
            seen = seen + jnp.sum(block, axis=1, keepdims=True)
        slot = holder * per_pair + jnp.concatenate(ranks, axis=1).astype(jnp.int32)

        row = lax.broadcasted_iota(jnp.int32, (8, rows), 0)
        firm_place = lax.broadcasted_iota(jnp.int32, (8, rows), 1)
        digits = jnp.where(row == 0, wanted // 256, jnp.where(row == 1, wanted % 256, 0))
        digits = jnp.where(row == 2, firm_place // 256, jnp.where(row == 3, firm_place % 256, digits))
        digits = jnp.concatenate([digits, jnp.zeros_like(digits)], axis=0).astype(jnp.float32).astype(jnp.bfloat16)
        asked = []
        for start in range(0, rows, chunk):
            slots = start + lax.broadcasted_iota(jnp.int32, (chunk, rows), 0)
            hot = jnp.where(slots == slot, 1.0, 0.0).astype(jnp.bfloat16)
            found = dot_nt(digits, hot)
            order = (found[2:3, :] * 256.0 + found[3:4, :]).astype(jnp.int32)
            place_ref[:, start : start + chunk] = jnp.where(order // half == core, half, 0) + order % half
            asked.append(found)

        products = lax.broadcasted_iota(jnp.int32, (128, rows), 1).astype(jnp.float32)
        both = both_ref[...]
        local = (panel_ref[...] - base).astype(jnp.float32)
        wide = jnp.concatenate([local, jnp.zeros((128 - panel_ref.shape[0], 128), jnp.float32)], axis=0).T
        part_row = lax.broadcasted_iota(jnp.int32, (8, 128), 0)
        for k in range(cols // 128):
            hot = jnp.where(wide[:, k : k + 1] == products, 1.0, 0.0).astype(jnp.bfloat16)
            part = jnp.dot(hot, both, preferred_element_type=jnp.float32)
            part_pieces = part[:, depth:].T[:8, :]
            part_pieces = jnp.concatenate([part_pieces[4:8, :], part_pieces[0:4, :]], axis=0)
            for place in range(128 // share_cols):
                q = k * (128 // share_cols) + place
                start = q * per_pair // 128 * 128 % chunk
                found = asked[q * per_pair // chunk][:, start : start + 128]
                extra = jnp.where(part_row == 0, found[0:1, :], jnp.where(part_row == 4, found[1:2, :], part_pieces))
                mine = part[place * share_cols : (place + 1) * share_cols, :depth]
                message_ref[q * 16 : (q + 1) * 16, :] = jnp.concatenate([mine, extra], axis=0).astype(jnp.bfloat16)

    def whole(shape):
        return pl.BlockSpec(shape, lambda i: (0, 0))

    return pl.pallas_call(
        kernel,
        grid=(1,),
        in_specs=[whole(value.shape) for value in (characteristics, means, firm_row, panel_rows)],
        out_specs=[whole((rows, 2 * depth)), whole((16 * holders, depth)), whole((1, rows))],
        out_shape=[
            jax.ShapeDtypeStruct((rows, 2 * depth), jnp.bfloat16),
            jax.ShapeDtypeStruct((16 * holders, depth), jnp.bfloat16),
            jax.ShapeDtypeStruct((1, rows), jnp.int32),
        ],
        compiler_params=pltpu.CompilerParams(vmem_limit_bytes=60 * 1024 * 1024),
        name="prepare",
    )(characteristics, means, firm_row, panel_rows)


def beside_ones(tastes):
    lane = lax.broadcasted_iota(jnp.int32, tastes.shape, 1)
    ones = jnp.where((lane >= 1) & (lane <= 3), 1.0, 0.0)
    return jnp.concatenate([tastes, ones.astype(tastes.dtype)], axis=1)


def stats(chars, tastes):
    rows, depth = chars.shape
    consumers = tastes.shape[0]
    block, chunk = 2048, 256

    def kernel(chars_ref, tastes_ref, stat_ref):
        people = beside_ones(tastes_ref[...])
        peak = jnp.full((1, block), -jnp.inf, jnp.float32)
        total = jnp.zeros((8, block), jnp.float32)
        for start in range(0, rows, chunk):
            util = dot_nt(chars_ref[start : start + chunk, :], people)
            highest = jnp.max(util.reshape(chunk // 8, 8, block), axis=0)
            joint = jnp.maximum(peak, jnp.max(highest, axis=0, keepdims=True))
            expo = jnp.exp(util - joint)
            total = total * jnp.exp(peak - joint) + jnp.sum(expo.reshape(chunk // 8, 8, block), axis=0)
            peak = joint
        stat_ref[...] = peak + jnp.log(jnp.sum(total, axis=0, keepdims=True))

    return pl.pallas_call(
        kernel,
        grid=(consumers // block,),
        in_specs=[
            pl.BlockSpec((rows, depth), lambda i: (0, 0)),
            pl.BlockSpec((block, tastes.shape[1]), lambda i: (i, 0)),
        ],
        out_specs=pl.BlockSpec((1, block), lambda i: (0, i)),
        out_shape=jax.ShapeDtypeStruct((1, consumers), jnp.float32),
        compiler_params=pltpu.CompilerParams(vmem_limit_bytes=VMEM_BYTES),
        name="stats",
    )(chars, tastes)


def pick_rows(ids_t, chars, tail, stat):
    per_pair, holders = ids_t.shape
    rows, depth = chars.shape
    each = per_pair + 16
    group, pair = 256 // per_pair, 128 // per_pair

    def kernel(ids_ref, chars_ref, tail_ref, stat_ref, out_ref, stat_out_ref):
        stat_out_ref[...] = stat_ref[...]
        lanes = lax.broadcasted_iota(jnp.int32, (per_pair, rows), 1)
        table = chars_ref[...]
        pieces = jnp.where(lax.broadcasted_iota(jnp.int32, (8, 128), 0) >= 5, tail_ref[8:16, :], 0.0)
        for start in range(0, holders, group):
            span = range(start, start + group)
            marks = [jnp.where(ids_ref[:, q : q + 1] == lanes, 1.0, 0.0).astype(jnp.bfloat16) for q in span]
            picked = jnp.dot(jnp.concatenate(marks, axis=0), table, preferred_element_type=jnp.float32)
            for place, q in enumerate(span):
                if place % pair == 0:
                    beside = picked[place * per_pair : (place + pair) * per_pair, 128:].T[:8, :]
                    block = jnp.concatenate([beside + pieces, tail_ref[0:8, :]], axis=0).astype(jnp.bfloat16)
                mine = picked[place * per_pair : (place + 1) * per_pair, :128]
                out_ref[q * each : q * each + per_pair, :] = mine.astype(jnp.bfloat16)
                out_ref[q * each + per_pair : (q + 1) * each, :] = block

    return pl.pallas_call(
        kernel,
        out_shape=[
            jax.ShapeDtypeStruct((each * holders, depth // 2), jnp.bfloat16),
            jax.ShapeDtypeStruct(stat.shape, stat.dtype),
        ],
        compiler_params=pltpu.CompilerParams(vmem_limit_bytes=VMEM_BYTES),
        name="pick_rows",
    )(ids_t, chars, tail, stat)


def place_rows(order, received, beside, holders, gate):
    rows = order.shape[1]
    total, depth = received.shape
    per_pair, each = rows // holders, total // holders
    chunk = 256

    def kernel(order_ref, received_ref, beside_ref, gate_ref, out_ref):
        order_row = order_ref[...]
        table = jnp.concatenate([received_ref[q * each : q * each + per_pair, :] for q in range(holders)], axis=0)
        blank = jnp.zeros((120, 128), jnp.float32)
        columns = [
            jnp.concatenate([beside_ref[:, start : start + 128], blank], axis=0).T.astype(jnp.bfloat16)
            for start in range(0, rows, 128)
        ]
        table = jnp.concatenate([table, jnp.concatenate(columns, axis=0)], axis=1)
        for start in range(0, rows, chunk):
            ids = start + lax.broadcasted_iota(jnp.int32, (chunk, rows), 0)
            hot = jnp.where(ids == order_row, 1.0, 0.0).astype(jnp.bfloat16)
            placed = jnp.dot(hot, table, preferred_element_type=jnp.float32)
            out_ref[start : start + chunk, :] = placed.astype(jnp.bfloat16)

    return pl.pallas_call(
        kernel,
        in_specs=[pl.BlockSpec(memory_space=pltpu.VMEM)] * 3 + [pl.BlockSpec(memory_space=pl.ANY)],
        out_shape=jax.ShapeDtypeStruct((rows, 2 * depth), jnp.bfloat16),
        compiler_params=pltpu.CompilerParams(vmem_limit_bytes=VMEM_BYTES),
        name="place_rows",
    )(order, received, beside, gate)


def lane_groups(values):
    total = values[:, 0:128]
    for start in range(128, values.shape[1], 128):
        total = total + values[:, start : start + 128]
    return total


def first_panel(chars, parts, tastes, row_values, col_chars):
    rows, depth = chars.shape[0] // parts, chars.shape[1]
    consumers = tastes.shape[0]
    cols = col_chars.shape[0]
    block, chunk = 2048, 256

    def kernel(chars_ref, tastes_ref, rows_ref, cols_ref, panel_ref, share_ref, weight_ref, diag_ref):
        step = pl.program_id(0)

        @pl.when(step == 0)
        def _():
            panel_ref[...] = jnp.zeros_like(panel_ref)
            share_ref[...] = jnp.zeros_like(share_ref)
            diag_ref[...] = jnp.zeros_like(diag_ref)

        people = beside_ones(tastes_ref[...])
        peak, ratio = rows_ref[0:1, :], rows_ref[1:2, :]
        weighted = rows_ref[2:3, :] * (jnp.exp(dot_nt(cols_ref[...], people) - peak) * ratio)
        diag_ref[...] += lane_groups(weighted)
        weight = weighted.astype(jnp.bfloat16)
        weight_ref[...] = weight
        for start in range(0, rows, chunk):
            scaled = jnp.exp(dot_nt(chars_ref[start : start + chunk, :], people) - peak) * ratio
            share_ref[start : start + chunk, :] += lane_groups(scaled)
            panel_ref[start : start + chunk, :] += dot_nt(scaled.astype(jnp.bfloat16), weight)

        @pl.when(step == pl.num_programs(0) - 1)
        def _():
            total = jnp.sum(diag_ref[...].T, axis=0, keepdims=True)
            panel_ref[rows:, :] = jnp.broadcast_to(total, (8, cols))

    return pl.pallas_call(
        kernel,
        grid=(consumers // block,),
        in_specs=[
            pl.BlockSpec((rows, depth), lambda i: (0, 0)),
            pl.BlockSpec((block, tastes.shape[1]), lambda i: (i, 0)),
            pl.BlockSpec((3, block), lambda i: (0, i)),
            pl.BlockSpec((cols, depth), lambda i: (0, 0)),
        ],
        out_specs=[
            pl.BlockSpec((rows + 8, cols), lambda i: (0, 0)),
            pl.BlockSpec((rows, 128), lambda i: (0, 0)),
            pl.BlockSpec((cols, block), lambda i: (0, i)),
        ],
        scratch_shapes=[pltpu.VMEM((cols, 128), jnp.float32)],
        out_shape=[
            jax.ShapeDtypeStruct((rows + 8, cols), jnp.float32),
            jax.ShapeDtypeStruct((rows, 128), jnp.float32),
            jax.ShapeDtypeStruct((cols, consumers), jnp.bfloat16),
        ],
        compiler_params=pltpu.CompilerParams(vmem_limit_bytes=VMEM_BYTES),
        cost_estimate=pl.CostEstimate(
            flops=2 * rows * consumers * (depth + cols), bytes_accessed=rows * cols * 8, transcendentals=rows * consumers
        ),
        name="first_panel",
    )(chars, tastes, row_values, col_chars)


def panel(chars, part, parts, tastes, row_values, weighted, gate):
    rows, depth = chars.shape[0] // parts, chars.shape[1]
    consumers = tastes.shape[0]
    cols = weighted.shape[0]
    chunk = 256

    def kernel(chars_ref, tastes_ref, rows_ref, weight_ref, gate_ref, panel_ref, share_ref):
        people, weight = beside_ones(tastes_ref[...]), weight_ref[...]
        peak, ratio = rows_ref[0:1, :], rows_ref[1:2, :]
        for start in range(0, rows, chunk):
            scaled = jnp.exp(dot_nt(chars_ref[start : start + chunk, :], people) - peak) * ratio
            share_ref[start : start + chunk, :] = lane_groups(scaled)
            panel_ref[start : start + chunk, :] = dot_nt(scaled.astype(jnp.bfloat16), weight)

    return pl.pallas_call(
        kernel,
        grid=(1,),
        in_specs=[
            pl.BlockSpec((rows, depth), lambda i: (part, 0)),
            pl.BlockSpec(tastes.shape, lambda i: (0, 0)),
            pl.BlockSpec((3, consumers), lambda i: (0, 0)),
            pl.BlockSpec((cols, consumers), lambda i: (0, 0)),
            pl.BlockSpec(memory_space=pl.ANY),
        ],
        out_specs=[
            pl.BlockSpec((rows, cols), lambda i: (0, 0)),
            pl.BlockSpec((rows, 128), lambda i: (0, 0)),
        ],
        out_shape=[
            jax.ShapeDtypeStruct((rows, cols), jnp.float32),
            jax.ShapeDtypeStruct((rows, 128), jnp.float32),
        ],
        compiler_params=pltpu.CompilerParams(vmem_limit_bytes=VMEM_BYTES),
        cost_estimate=pl.CostEstimate(
            flops=2 * rows * consumers * (depth + cols), bytes_accessed=rows * cols * 8, transcendentals=rows * consumers
        ),
        name="panel",
    )(chars, tastes, row_values, weighted, gate)


def share_sums(chars, tastes, row_values, gate):
    rows, depth = chars.shape
    consumers = tastes.shape[0]
    block, chunk = 1024, 256

    def kernel(chars_ref, tastes_ref, rows_ref, gate_ref, share_ref):
        @pl.when(pl.program_id(0) == 0)
        def _():
            share_ref[...] = jnp.zeros_like(share_ref)

        people = beside_ones(tastes_ref[...])
        peak, ratio = rows_ref[0:1, :], rows_ref[1:2, :]
        for start in range(0, rows, chunk):
            scaled = jnp.exp(dot_nt(chars_ref[start : start + chunk, :], people) - peak) * ratio
            share_ref[start : start + chunk, :] += lane_groups(scaled)

    return pl.pallas_call(
        kernel,
        grid=(consumers // block,),
        in_specs=[
            pl.BlockSpec((rows, depth), lambda i: (0, 0)),
            pl.BlockSpec((block, tastes.shape[1]), lambda i: (i, 0)),
            pl.BlockSpec((3, block), lambda i: (0, i)),
            pl.BlockSpec(memory_space=pl.ANY),
        ],
        out_specs=pl.BlockSpec((rows, 128), lambda i: (0, 0)),
        out_shape=jax.ShapeDtypeStruct((rows, 128), jnp.float32),
        compiler_params=pltpu.CompilerParams(vmem_limit_bytes=VMEM_BYTES),
        name="share_sums",
    )(chars, tastes, row_values, gate)


def swap(value, axis, mask):
    size = lax.axis_size(axis)
    return lax.ppermute(value, axis, [(i, i ^ mask) for i in range(size)])


def butterfly_masks(size):
    masks, step = [], 1
    while step < size:
        masks.append(step)
        if step * 2 < size:
            masks.append(step * 3)
        step *= 4
    return masks


def body(tastes, price_coef, characteristics, mean_utility, panel_cols, firm_map, inverses):
    products, depth = characteristics.shape
    consumers = tastes.shape[0]
    cols = panel_cols.shape[0]
    holders = lax.axis_size("prod")
    per_pair = products // holders
    count_products = products * holders
    count_consumers = consumers * lax.axis_size("cons")
    core = lax.axis_index("cons") % 2

    share_cols = cols // holders
    chars, message, place = prepare(
        characteristics,
        mean_utility.reshape(products // 128, 128),
        firm_map.reshape(1, products),
        panel_cols.reshape(cols // 128, 128),
        holders,
    )
    first = lax.all_to_all(message.reshape(holders, 16, depth), "prod", split_axis=0, concat_axis=0, tiled=True)

    stat = stats(chars, tastes)

    odd = lax.axis_index("prod") % 2 == 1

    def own_lanes(values):
        return jnp.where(odd, values[..., per_pair:], values[..., :per_pair])

    high, low = own_lanes(first[:, 8, :]), own_lanes(first[:, 12, :])
    ids = high.astype(jnp.int32) * 256 + low.astype(jnp.int32)
    summed = jnp.sum(first.astype(jnp.float32), axis=0)
    each = per_pair + 16
    sent, stat = pick_rows(ids.T, chars, summed, stat)
    second = lax.all_to_all(sent.reshape(holders, each, depth), "prod", split_axis=0, concat_axis=0, tiled=True)
    col_pieces = second[:: 128 // share_cols, per_pair + 5 : per_pair + 8, :].transpose(0, 2, 1).reshape(cols, 3)
    col_chars = second[:, per_pair + 8 :, :].reshape(cols, depth)
    col_chars = jnp.concatenate([col_chars, jnp.pad(col_pieces, ((0, 0), (1, depth - 4)))], axis=1)
    mean_rows = own_lanes(second[:, per_pair : per_pair + 4, :].astype(jnp.float32))
    mean_rows = jnp.pad(mean_rows, ((0, 0), (0, 4), (0, 0))).transpose(1, 0, 2).reshape(8, products)
    half = products // 2

    def join(stat, masks):
        for mask in masks:
            other = swap(stat, "prod", mask)
            joint = jnp.maximum(stat, other)
            stat = joint + jnp.log(jnp.exp(stat - joint) + jnp.exp(other - joint))
        return stat

    masks = butterfly_masks(holders)
    taken = ids[0, 0] >= 0
    total = lax.cond(taken, lambda value: join(value, masks), lambda value: value, stat[0])
    peak = jnp.maximum(total, 0.0)
    denom = jnp.exp(-peak) + jnp.exp(total - peak)
    ratio = count_products / denom
    row_values = jnp.stack([peak, ratio, price_coef])
    firm_chars = place_rows(
        place, second.reshape(holders * each, depth), mean_rows, holders, row_values
    )
    given, given_share, weighted = first_panel(firm_chars, 2, tastes, row_values, col_chars)
    got = swap(given, "cons", 1)
    kept, kept_share = panel(firm_chars, 1, 2, tastes, row_values, weighted, given)
    diagonal = given[half] + got[half]
    room = 32768.0 / (count_products * jnp.maximum(diagonal, 1e-25))
    fitted = (kept + got[:half]) * room[None, :]
    chip_sum, gate = lax.optimization_barrier((fitted.astype(jnp.float16), jnp.max(fitted, axis=0, keepdims=True)))
    other_sum = swap(chip_sum, "cons", 2)

    given_share, kept_share = jnp.sum(given_share, axis=1), jnp.sum(kept_share, axis=1)
    first_half = jnp.where(core == 0, kept_share, given_share)
    second_half = jnp.where(core == 0, given_share, kept_share)

    def own_and_exchange(gate, others):
        own_shares = jnp.sum(share_sums(chars, tastes, row_values, gate), axis=1)
        sums = jnp.concatenate([own_shares, others])
        sums = sums + swap(sums, "cons", 1)
        other_sums = swap(sums, "cons", 2)
        return (sums + other_sums) / count_consumers, other_sums[2 * products :]

    sums, other_diagonal = lax.cond(
        taken,
        own_and_exchange,
        lambda gate, others: (jnp.zeros(2 * products + cols, jnp.float32), jnp.zeros(cols, jnp.float32)),
        gate,
        jnp.concatenate([first_half, second_half, given[half]]),
    )
    shares, firm_shares = sums[:products], sums[products : 2 * products]

    firm_count, block_size = inverses.shape[0], inverses.shape[1]
    own_inverses = lax.dynamic_slice_in_dim(inverses, core * (firm_count // 2), firm_count // 2, 0)
    firm_ids = lax.dynamic_slice_in_dim(firm_map, core * half, half, 0)
    other_room = 32768.0 / (count_products * jnp.maximum(other_diagonal, 1e-25))
    unfit, other_unfit = 1.0 / (room * count_consumers), 1.0 / (other_room * count_consumers)
    cross = chip_sum.astype(jnp.float32) * unfit[None, :] + other_sum.astype(jnp.float32) * other_unfit[None, :]
    diagonal = (diagonal + other_diagonal) / count_consumers
    jacobian = cross - jnp.where(firm_ids[:, None] == panel_cols[None, :], diagonal[None, :], 0.0)
    mine = jnp.einsum(
        "fab,fbc->fac",
        own_inverses,
        jacobian.reshape(firm_count // 2, block_size, cols),
        precision=lax.Precision.HIGHEST,
    ).reshape(half, cols)
    theirs = swap(mine, "cons", 1)
    response = jnp.where(core == 0, jnp.concatenate([mine, theirs]), jnp.concatenate([theirs, mine]))
    markup = jnp.sum(inverses * firm_shares.reshape(firm_count, 1, block_size), axis=2).reshape(products)
    return (shares, markup, response)


def solution(mesh):
    return jax.shard_map(
        body,
        mesh=mesh,
        in_specs=(
            P("cons", None),
            P("cons"),
            P("prod", None),
            P("prod"),
            P(),
            P("prod"),
            P("prod", None, None),
        ),
        out_specs=(P("prod"), P("prod"), P("prod", None)),
        check_vma=False,
    )
```
